512 devices in a mesh: row: 32 (over z_hi, y), col: 16 (over z_lo, x, core).
Axes of the slice: x: 4, y: 8, z: 8 (z_hi: 4, z_lo: 2; z = z_hi * 2 + z_lo), core: 2. Of those that a mesh axis runs over, the one named last changes fastest.
Arguments:
- fock: bfloat16 [4096, 4096], P('row', 'col'), may hold values from -0.09375 to 0.09375
- density: bfloat16 [4096, 4096], P('row', 'col'), may hold values from -0.09375 to 0.09375
- intersection: bfloat16 [4096, 4096], P('row', 'col'), may hold values from -6 to 6
- fock_mask: int32 [32, 32], P('row', 'col'), may hold values 0 or 1
- density_mask: int32 [32, 32], P('row', 'col'), may hold values 0 or 1
- intersection_mask: int32 [32, 32], P('row', 'col'), may hold values 0 or 1
- product_filter: int32 [32, 32], P('row', 'col'), may hold values 0 or 1
Outputs:
- residual: float32 [4096, 4096], P('row', 'col')
The draws below stay inside these ranges and needn't reach their ends.
All inputs are finite; a program needn't handle non-finite values. No bound on the sum of `fock_mask` or of `density_mask` or of `intersection_mask` or of `product_filter` on one device may be relied on, other than what follows from the above.
Results may differ from the reference program's by a relative error of at most 0.0041.
Values may be sent and summed in bfloat16 or wider, within the bound.
A program may use at most 64 MiB of HBM per device.

```python
import jax
import jax.numpy as jnp

NB = 32
ORDER = 4096


def plant(entries, stream_key, low, high):
    longest = entries.shape.index(max(entries.shape))
    spots = []
    for shift in (0, 1):
        where = [jax.random.randint(jax.random.fold_in(stream_key, axis), (), 0, length) for axis, length in enumerate(entries.shape)]
        where[longest] = (where[longest] + shift) % entries.shape[longest]
        spots.append(tuple(where))
    return entries.at[spots[0]].set(low).at[spots[1]].set(high)


def level_of(stream_key, shape, pieces, low, largest):
    level = 1.0
    for axis_at, parts in pieces:
        steps = jax.random.uniform(jax.random.fold_in(jax.random.fold_in(stream_key, 6), axis_at), (parts,), jnp.float32, low / len(pieces), largest / len(pieces))
        level = level * jnp.repeat(jnp.exp(steps), shape[axis_at] // parts).reshape((-1,) + (1,) * (len(shape) - 1 - axis_at))
    return level


def scatter_about(rng, shape, deviation, bound, pieces=(), kind=jnp.bfloat16):
    result = deviation * jax.random.normal(rng, shape, jnp.float32)
    if pieces:
        result = result * level_of(rng, shape, pieces, -0.22, 0.18)
    return jnp.clip(result, -bound, bound).astype(kind)


def setup_inputs(seed: int = 0) -> dict:
    splits = jax.random.split(jax.random.key(seed), 8)
    fock = scatter_about(splits[0], (ORDER, ORDER), ORDER ** -0.5, 0.09375, ((0, 32), (1, 16)))
    density = scatter_about(splits[1], (ORDER, ORDER), ORDER ** -0.5, 0.09375, ((0, 32), (1, 16)))
    intersection = scatter_about(splits[2], (ORDER, ORDER), 1.0, 6.0, ((0, 32), (1, 16)))
    fock_mask = plant((jax.random.randint(splits[3], (NB, NB), 0, 4) < 3).astype(jnp.int32), jax.random.fold_in(splits[3], 1), 0, 1)
    density_mask = plant((jax.random.randint(splits[4], (NB, NB), 0, 4) < 3).astype(jnp.int32), jax.random.fold_in(splits[4], 1), 0, 1)
    intersection_mask = plant((jax.random.randint(splits[5], (NB, NB), 0, 4) < 3).astype(jnp.int32), jax.random.fold_in(splits[5], 1), 0, 1)
    product_filter = plant((jax.random.randint(splits[6], (NB, NB), 0, 4) < 3).astype(jnp.int32), jax.random.fold_in(splits[6], 1), 0, 1)
    return {"fock": fock, "density": density, "intersection": intersection, "fock_mask": fock_mask, "density_mask": density_mask, "intersection_mask": intersection_mask, "product_filter": product_filter}


def apply_mask(matrix, mask):
    rows_b, cols_b = mask.shape
    size_r = matrix.shape[0] // rows_b
    size_c = matrix.shape[1] // cols_b
    shaped = matrix.reshape(rows_b, size_r, cols_b, size_c)
    return (shaped * mask[:, None, :, None].astype(matrix.dtype)).reshape(matrix.shape)


def reference(fock, density, intersection, fock_mask, density_mask, intersection_mask, product_filter):
    first = jnp.dot(apply_mask(fock, fock_mask), apply_mask(density, density_mask), preferred_element_type=jnp.float32)
    kept = apply_mask(first, product_filter).astype(jnp.bfloat16)
    product = jnp.dot(kept, apply_mask(intersection, intersection_mask), preferred_element_type=jnp.float32).astype(jnp.bfloat16)
    wide = product.astype(jnp.float32)
    return wide - wide.T
```

```python
import jax
import jax.numpy as jnp
from jax import lax
from jax.experimental import pallas as pl
from jax.experimental.pallas import tpu as pltpu
from jax.sharding import PartitionSpec as P

MESH = pl.DeviceIdType.MESH
Z, Y, J = 4, 8, 4
COLS = Z * J
CHIPS = COLS // 2
BF16, F32 = jnp.bfloat16, jnp.float32


def masked(block, mask_ref):
    lane = lax.broadcasted_iota(jnp.int32, block.shape, 1)
    keep = jnp.where(lane < block.shape[1] // 2, mask_ref[0, 0], mask_ref[0, 1])
    return (block.astype(F32) * keep.astype(F32)).astype(BF16)


def kernel(
    f_ref, p_ref, s_ref, fm_ref, pm_ref, sm_ref, filt_ref, out_ref,
    f_send, f_all, k_all, p_all, s_all, filt_send, filt_here,
    part, parts_in, part_send, part2_in, tile_send, tile_in,
    t_sem, p_send_sem, p_recv_sem, s_send_sem, s_recv_sem,
    f_send_sem, f_recv_sem, k_send_sem, k_recv_sem,
    a_send_sem, a_recv_sem, b_send_sem, b_recv_sem, x_send_sem, x_recv_sem,
):
    r, c = lax.axis_index("row"), lax.axis_index("col")
    zh, y = lax.div(r, Y), lax.rem(r, Y)
    q, j = lax.div(c, J), lax.rem(c, J)
    chip, core = lax.div(c, 2), lax.rem(c, 2)
    partner = (r, 2 * chip + 1 - core)
    moved = q != zh
    swap_to = (q * Y + y, zh * J + j)

    def ring(d):
        return zh * Y + lax.rem(y + d, Y)

    def line(d):
        return 2 * lax.rem(chip + d, CHIPS) + core

    def other(d):
        return lax.rem(zh + d, Z)

    def tile_to(b):
        return (2 * c + b, lax.div(r, 2))

    def off_diagonal(b):
        return r != 2 * c + b

    def copy(src, dst, send, recv, to):
        return pltpu.make_async_remote_copy(
            src_ref=src, dst_ref=dst, send_sem=send, recv_sem=recv, device_id=to, device_id_type=MESH
        )

    barrier = pltpu.get_barrier_semaphore()

    def greet(to):
        pl.semaphore_signal(barrier, inc=1, device_id=to, device_id_type=MESH)

    for d in range(1, Y):
        greet((ring(d), c))
    for d in range(1, CHIPS):
        greet((r, line(d)))
    greet(partner)
    for d in range(1, Z):
        greet((other(d) * Y + y, zh * J + j))
        greet((other(d) * Y + y, c))
    for b in range(2):

        @pl.when(off_diagonal(b))
        def _():
            greet(tile_to(b))

    p_all[y] = masked(p_ref[...], pm_ref)
    f_masked = masked(f_ref[...], fm_ref)
    f_send[...] = f_masked
    lane = lax.broadcasted_iota(jnp.int32, filt_send.shape, 1)
    filt_send[...] = jnp.where(lane < 128, filt_ref[0, 0], filt_ref[0, 1]).astype(F32)
    s_all[y] = masked(s_ref[...], sm_ref)

    signals = (Y - 1) + (CHIPS - 1) + 1 + (Z - 1) + jnp.where(moved, Z, 0)
    for b in range(2):
        signals = signals + jnp.where(off_diagonal(b), 1, 0)
    pl.semaphore_wait(barrier, signals)

    f_swap = copy(f_send, f_all.at[j, zh], t_sem.at[0], t_sem.at[1], swap_to)
    filt_swap = copy(filt_send, filt_here, t_sem.at[2], t_sem.at[3], swap_to)

    @pl.when(moved)
    def _():
        f_swap.start()
        filt_swap.start()

    p_copies = []
    for d in (4, 3, 5, 2, 6, 1, 7):
        p_copies.append(
            copy(p_all.at[y], p_all.at[y], p_send_sem.at[d], p_recv_sem.at[y], (ring(d), c))
        )
        p_copies[-1].start()

    @pl.when(moved)
    def _():
        copy(f_send, f_all.at[j, q], t_sem.at[0], t_sem.at[1], swap_to).wait_recv()
        filt_swap.wait_recv()

    @pl.when(jnp.logical_not(moved))
    def _():
        f_all[j, q] = f_send[...]
        filt_here[...] = filt_send[...]

    def gather_line(buf, send_sem, recv_sem):
        mine = buf.at[j, q]
        copies = []

        def send(src, to, slot, sem):
            copies.append(copy(src, src, send_sem.at[sem], recv_sem.at[slot], to))
            copies[-1].start()

        for d in (4, 3, 5, 2, 6, 1, 7):
            send(mine, (r, line(d)), c, d)
        send(mine, partner, c, 0)
        for d in (1, 7, 2, 6, 3, 5, 4):
            src = line(d)
            slot = buf.at[lax.rem(src, J), lax.div(src, J)]
            copy(slot, slot, send_sem.at[d], recv_sem.at[src], partner).wait_recv()
            send(slot, partner, src, CHIPS + d)
        for d in range(CHIPS):
            src = 2 * lax.rem(chip + d, CHIPS) + 1 - core
            slot = buf.at[lax.rem(src, J), lax.div(src, J)]
            copy(slot, slot, send_sem.at[d], recv_sem.at[src], partner).wait_recv()
        return copies

    def wait_ring(buf, send_sem, recv_sem):
        for d in range(1, Y):
            src = lax.rem(y + d, Y)
            copy(buf.at[src], buf.at[src], send_sem.at[d], recv_sem.at[src], (ring(d), c)).wait_recv()

    f_copies = gather_line(f_all, f_send_sem, f_recv_sem)
    wait_ring(p_all, p_send_sem, p_recv_sem)

    s_copies = []
    for d in (4, 3, 5, 2, 6, 1, 7):
        s_copies.append(
            copy(s_all.at[y], s_all.at[y], s_send_sem.at[d], s_recv_sem.at[y], (ring(d), c))
        )
        s_copies[-1].start()

    def product(left, right):
        total = None
        for k in range(J):
            a = left[k].reshape(Z * 128, 256)
            b = right[2 * k : 2 * k + 2].reshape(256, 256)
            term = jnp.dot(a, b, preferred_element_type=F32)
            total = term if total is None else total + term
        return total.reshape(Z, 128, 256)

    part[...] = product(f_all, p_all)
    a_copies = []
    for d in range(Z):
        z = other(d)
        a_copies.append(
            copy(part.at[z], parts_in.at[zh], a_send_sem.at[d], a_recv_sem.at[zh], (q * Y + y, z * J + j))
        )
    for d in range(1, Z):
        a_copies[d].start()

    @pl.when(moved)
    def _():
        a_copies[0].start()

    @pl.when(jnp.logical_not(moved))
    def _():
        parts_in[zh] = part[zh]

    def a_wait(d):
        z = other(d)
        copy(part.at[z], parts_in.at[z], a_send_sem.at[d], a_recv_sem.at[z], (z * Y + y, zh * J + j)).wait_recv()

    for d in range(1, Z):
        a_wait(d)

    @pl.when(moved)
    def _():
        a_wait(0)

    first = (parts_in[0] + parts_in[1]) + (parts_in[2] + parts_in[3])
    k_all[j, q] = (first * filt_here[0:1, :]).astype(BF16)
    k_copies = gather_line(k_all, k_send_sem, k_recv_sem)
    for d in range(1, Z):
        a_copies[d].wait_send()

    @pl.when(moved)
    def _():
        a_copies[0].wait_send()

    wait_ring(s_all, s_send_sem, s_recv_sem)

    part[...] = product(k_all, s_all)
    b_copies = []
    for d in (2, 1, 3):
        z = other(d)
        part_send[d] = part[z].astype(BF16)
        b_copies.append(
            copy(part_send.at[d], part2_in.at[zh], b_send_sem.at[d], b_recv_sem.at[zh], (z * Y + y, c))
        )
        b_copies[-1].start()
    total = part[zh]
    for d in (1, 3, 2):
        z = other(d)
        copy(part_send.at[d], part2_in.at[z], b_send_sem.at[d], b_recv_sem.at[z], (z * Y + y, c)).wait_recv()
        total = total + part2_in[z].astype(F32)
    wide = total.astype(BF16).astype(F32)

    x_copies = []
    for b in range(2):
        tile = wide[:, 128 * b : 128 * (b + 1)]
        tile_send[b] = tile.astype(BF16)
        x_copies.append(
            copy(tile_send.at[b], tile_in.at[lax.rem(r, 2)], x_send_sem.at[b], x_recv_sem.at[lax.rem(r, 2)], tile_to(b))
        )

        @pl.when(off_diagonal(b))
        def _():
            x_copies[b].start()

        @pl.when(jnp.logical_not(off_diagonal(b)))
        def _():
            tile_in[b] = tile_send[b]

    for b in range(2):

        @pl.when(off_diagonal(b))
        def _():
            copy(tile_send.at[b], tile_in.at[b], x_send_sem.at[b], x_recv_sem.at[b], tile_to(b)).wait_recv()

        mirrored = tile_in[b].astype(F32).T
        out_ref[:, 128 * b : 128 * (b + 1)] = wide[:, 128 * b : 128 * (b + 1)] - mirrored

    for one in p_copies + s_copies + f_copies + k_copies + b_copies:
        one.wait_send()

    @pl.when(moved)
    def _():
        f_swap.wait_send()
        filt_swap.wait_send()

    for b in range(2):

        @pl.when(off_diagonal(b))
        def _():
            x_copies[b].wait_send()


def per_device(fock, density, intersection, fock_mask, density_mask, intersection_mask, product_filter):
    vmem = pl.BlockSpec(memory_space=pltpu.VMEM)
    smem = pl.BlockSpec(memory_space=pltpu.SMEM)
    dma = pltpu.SemaphoreType.DMA
    block = (128, 256)
    return pl.pallas_call(
        kernel,
        out_shape=jax.ShapeDtypeStruct(block, F32),
        in_specs=[vmem] * 3 + [smem] * 4,
        out_specs=vmem,
        scratch_shapes=[
            pltpu.VMEM(block, BF16),
            pltpu.VMEM((J, Z) + block, BF16),
            pltpu.VMEM((J, Z) + block, BF16),
            pltpu.VMEM((Y,) + block, BF16),
            pltpu.VMEM((Y,) + block, BF16),
            pltpu.VMEM((8, 256), F32),
            pltpu.VMEM((8, 256), F32),
            pltpu.VMEM((Z,) + block, F32),
            pltpu.VMEM((Z,) + block, F32),
            pltpu.VMEM((Z,) + block, BF16),
            pltpu.VMEM((Z,) + block, BF16),
            pltpu.VMEM((2, 128, 128), BF16),
            pltpu.VMEM((2, 128, 128), BF16),
            dma((4,)),
            dma((Y,)), dma((Y,)), dma((Y,)), dma((Y,)),
            dma((COLS,)), dma((COLS,)), dma((COLS,)), dma((COLS,)),
            dma((Z,)), dma((Z,)), dma((Z,)), dma((Z,)),
            dma((2,)), dma((2,)),
        ],
        compiler_params=pltpu.CompilerParams(
            collective_id=0, has_side_effects=True, vmem_limit_bytes=32 * 1024 * 1024
        ),
        cost_estimate=pl.CostEstimate(flops=2 * 2 * 512 * 1024 * 256, bytes_accessed=6 * 1024 * 1024, transcendentals=0),
    )(fock, density, intersection, fock_mask, density_mask, intersection_mask, product_filter)


def solution(mesh):
    spec = P("row", "col")
    return jax.shard_map(
        per_device, mesh=mesh, in_specs=(spec,) * 7, out_specs=spec, check_vma=False
    )
```

```python
import jax
import jax.numpy as jnp
from jax import lax
from jax.experimental import pallas as pl
from jax.experimental.pallas import tpu as pltpu
from jax.sharding import PartitionSpec as P

MESH = pl.DeviceIdType.MESH
Z, Y, J = 4, 8, 4
COLS = Z * J
CHIPS = COLS // 2
BF16, F32 = jnp.bfloat16, jnp.float32


def masked(block, mask_ref):
    lane = lax.broadcasted_iota(jnp.int32, block.shape, 1)
    keep = jnp.where(lane < block.shape[1] // 2, mask_ref[0, 0], mask_ref[0, 1])
    return (block.astype(F32) * keep.astype(F32)).astype(BF16)


def kernel(
    f_hbm, p_hbm, s_hbm, fm_hbm, pm_hbm, sm_hbm, filt_hbm, out_ref,
    f_ref, p_ref, s_ref, fm_ref, pm_ref, sm_ref, filt_ref, in_sem,
    f_send, f_all, k_all, p_all, s_all, filt_send, filt_here,
    part, parts_in, part_send, part2_in, tile_send, tile_in,
    t_sem, p_send_sem, p_recv_sem, s_send_sem, s_recv_sem,
    f_send_sem, f_recv_sem, k_send_sem, k_recv_sem,
    a_send_sem, a_recv_sem, b_send_sem, b_recv_sem, x_send_sem, x_recv_sem,
):
    r, c = lax.axis_index("row"), lax.axis_index("col")
    zh, y = lax.div(r, Y), lax.rem(r, Y)
    q, j = lax.div(c, J), lax.rem(c, J)
    chip, core = lax.div(c, 2), lax.rem(c, 2)
    partner = (r, 2 * chip + 1 - core)
    moved = q != zh
    swap_to = (q * Y + y, zh * J + j)

    def ring(d):
        return zh * Y + lax.rem(y + d, Y)

    def line(d):
        return 2 * lax.rem(chip + d, CHIPS) + core

    def other(d):
        return lax.rem(zh + d, Z)

    def tile_to(b):
        return (2 * c + b, lax.div(r, 2))

    def off_diagonal(b):
        return r != 2 * c + b

    def copy(src, dst, send, recv, to):
        return pltpu.make_async_remote_copy(
            src_ref=src, dst_ref=dst, send_sem=send, recv_sem=recv, device_id=to, device_id_type=MESH
        )

    fetches = []
    for n, (src, dst) in enumerate((
        (p_hbm, p_ref), (pm_hbm, pm_ref), (f_hbm, f_ref), (fm_hbm, fm_ref),
        (filt_hbm, filt_ref), (s_hbm, s_ref), (sm_hbm, sm_ref),
    )):
        fetches.append(pltpu.make_async_copy(src, dst, in_sem.at[n]))
        fetches[-1].start()

    barrier = pltpu.get_barrier_semaphore()

    def greet(to):
        pl.semaphore_signal(barrier, inc=1, device_id=to, device_id_type=MESH)

    for d in (1, 2, 6, 7):
        greet((ring(d), c))
    for d in range(1, CHIPS):
        greet((r, line(d)))
    greet(partner)
    for d in range(1, Z):
        greet((other(d) * Y + y, zh * J + j))
        greet((other(d) * Y + y, c))
    for b in range(2):

        @pl.when(off_diagonal(b))
        def _():
            greet(tile_to(b))

    for one in fetches:
        one.wait()
    p_all[y] = masked(p_ref[...], pm_ref)
    f_masked = masked(f_ref[...], fm_ref)
    f_send[...] = f_masked
    lane = lax.broadcasted_iota(jnp.int32, filt_send.shape, 1)
    filt_send[...] = jnp.where(lane < 128, filt_ref[0, 0], filt_ref[0, 1]).astype(F32)
    s_all[y] = masked(s_ref[...], sm_ref)

    signals = 4 + (CHIPS - 1) + 1 + (Z - 1) + jnp.where(moved, Z, 0)
    for b in range(2):
        signals = signals + jnp.where(off_diagonal(b), 1, 0)
    pl.semaphore_wait(barrier, signals)

    f_swap = copy(f_send, f_all.at[j, zh], t_sem.at[0], t_sem.at[1], swap_to)
    filt_swap = copy(filt_send, filt_here, t_sem.at[2], t_sem.at[3], swap_to)

    @pl.when(moved)
    def _():
        f_swap.start()
        filt_swap.start()

    def ring_send(buf, sems, src, d, n, half=None):
        send_sem, recv_sem = sems
        slot = lax.rem(y + src, Y)
        ref = buf.at[slot] if half is None else buf.at[slot, pl.ds(64 * half, 64)]
        recv = recv_sem.at[slot] if half is None else recv_sem.at[Y + half]
        one = copy(ref, ref, send_sem.at[n], recv, (ring(d), c))
        one.start()
        return one

    def ring_wait(buf, sems, src, half=None):
        send_sem, recv_sem = sems
        slot = lax.rem(y + src, Y)
        ref = buf.at[slot] if half is None else buf.at[slot, pl.ds(64 * half, 64)]
        recv = recv_sem.at[slot] if half is None else recv_sem.at[Y + half]
        copy(ref, ref, send_sem.at[0], recv, (ring(1), c)).wait_recv()

    def ring_start(buf, sems):
        return [ring_send(buf, sems, 0, d, n) for n, d in enumerate((2, 6, 1, 7))]

    def ring_relay(buf, sems):
        ring_wait(buf, sems, 6)
        copies = [ring_send(buf, sems, 6, 1, 4), ring_send(buf, sems, 6, 2, 5, 0)]
        ring_wait(buf, sems, 2)
        return copies + [ring_send(buf, sems, 2, 7, 6), ring_send(buf, sems, 2, 6, 7, 1)]

    def ring_finish(buf, sems):
        for src in (1, 7, 5, 3):
            ring_wait(buf, sems, src)
        for half in range(2):
            ring_wait(buf, sems, 4, half)

    p_sems, s_sems = (p_send_sem, p_recv_sem), (s_send_sem, s_recv_sem)
    p_copies = ring_start(p_all, p_sems)

    @pl.when(moved)
    def _():
        copy(f_send, f_all.at[j, q], t_sem.at[0], t_sem.at[1], swap_to).wait_recv()
        filt_swap.wait_recv()

    @pl.when(jnp.logical_not(moved))
    def _():
        f_all[j, q] = f_send[...]
        filt_here[...] = filt_send[...]

    def line_send(buf, sems, src, to, n):
        slot = buf.at[lax.rem(src, J), lax.div(src, J)]
        one = copy(slot, slot, sems[0].at[n], sems[1].at[src], to)
        one.start()
        return one

    def line_wait(buf, sems, src):
        slot = buf.at[lax.rem(src, J), lax.div(src, J)]
        copy(slot, slot, sems[0].at[0], sems[1].at[src], partner).wait_recv()

    def line_start(buf, sems):
        copies = [line_send(buf, sems, c, (r, line(d)), d) for d in (4, 3, 5, 2, 6, 1, 7)]
        return copies + [line_send(buf, sems, c, partner, 0)]

    def line_finish(buf, sems):
        copies = []
        for d in (1, 7, 2, 6, 3, 5, 4):
            line_wait(buf, sems, line(d))
            copies.append(line_send(buf, sems, line(d), partner, CHIPS + d))
        for d in range(CHIPS):
            line_wait(buf, sems, 2 * lax.rem(chip + d, CHIPS) + 1 - core)
        return copies

    f_sems, k_sems = (f_send_sem, f_recv_sem), (k_send_sem, k_recv_sem)
    f_copies = line_start(f_all, f_sems)
    p_copies += ring_relay(p_all, p_sems)
    f_copies += line_finish(f_all, f_sems)
    ring_finish(p_all, p_sems)
    s_copies = ring_start(s_all, s_sems)

    def product(left, right):
        total = None
        for k in range(J):
            a = left[k].reshape(Z * 128, 256)
            b = right[2 * k : 2 * k + 2].reshape(256, 256)
            term = jnp.dot(a, b, preferred_element_type=F32)
            total = term if total is None else total + term
        return total.reshape(Z, 128, 256)

    part[...] = product(f_all, p_all)
    a_copies = []
    for d in range(Z):
        z = other(d)
        a_copies.append(
            copy(part.at[z], parts_in.at[zh], a_send_sem.at[d], a_recv_sem.at[zh], (q * Y + y, z * J + j))
        )
    for d in range(1, Z):
        a_copies[d].start()

    @pl.when(moved)
    def _():
        a_copies[0].start()

    @pl.when(jnp.logical_not(moved))
    def _():
        parts_in[zh] = part[zh]

    s_copies += ring_relay(s_all, s_sems)

    def a_wait(d):
        z = other(d)
        copy(part.at[z], parts_in.at[z], a_send_sem.at[d], a_recv_sem.at[z], (z * Y + y, zh * J + j)).wait_recv()

    for d in range(1, Z):
        a_wait(d)

    @pl.when(moved)
    def _():
        a_wait(0)

    first = (parts_in[0] + parts_in[1]) + (parts_in[2] + parts_in[3])
    k_all[j, q] = (first * filt_here[0:1, :]).astype(BF16)
    k_copies = line_start(k_all, k_sems)
    k_copies += line_finish(k_all, k_sems)
    for d in range(1, Z):
        a_copies[d].wait_send()

    @pl.when(moved)
    def _():
        a_copies[0].wait_send()

    ring_finish(s_all, s_sems)

    part[...] = product(k_all, s_all)
    b_copies = []
    for d in (2, 1, 3):
        z = other(d)
        part_send[d] = part[z].astype(BF16)
        b_copies.append(
            copy(part_send.at[d], part2_in.at[zh], b_send_sem.at[d], b_recv_sem.at[zh], (z * Y + y, c))
        )
        b_copies[-1].start()
    total = part[zh]
    for d in (1, 3, 2):
        z = other(d)
        copy(part_send.at[d], part2_in.at[z], b_send_sem.at[d], b_recv_sem.at[z], (z * Y + y, c)).wait_recv()
        total = total + part2_in[z].astype(F32)
    wide = total.astype(BF16).astype(F32)

    x_copies = []
    for b in range(2):
        tile = wide[:, 128 * b : 128 * (b + 1)]
        tile_send[b] = tile.astype(BF16)
        x_copies.append(
            copy(tile_send.at[b], tile_in.at[lax.rem(r, 2)], x_send_sem.at[b], x_recv_sem.at[lax.rem(r, 2)], tile_to(b))
        )

        @pl.when(off_diagonal(b))
        def _():
            x_copies[b].start()

        @pl.when(jnp.logical_not(off_diagonal(b)))
        def _():
            tile_in[b] = tile_send[b]

    for b in range(2):

        @pl.when(off_diagonal(b))
        def _():
            copy(tile_send.at[b], tile_in.at[b], x_send_sem.at[b], x_recv_sem.at[b], tile_to(b)).wait_recv()

        mirrored = tile_in[b].astype(F32).T
        out_ref[:, 128 * b : 128 * (b + 1)] = wide[:, 128 * b : 128 * (b + 1)] - mirrored

    for one in p_copies + s_copies + f_copies + k_copies + b_copies:
        one.wait_send()

    @pl.when(moved)
    def _():
        f_swap.wait_send()
        filt_swap.wait_send()

    for b in range(2):

        @pl.when(off_diagonal(b))
        def _():
            x_copies[b].wait_send()


def per_device(fock, density, intersection, fock_mask, density_mask, intersection_mask, product_filter):
    hbm = pl.BlockSpec(memory_space=pltpu.HBM)
    vmem = pl.BlockSpec(memory_space=pltpu.VMEM)
    dma = pltpu.SemaphoreType.DMA
    block = (128, 256)
    return pl.pallas_call(
        kernel,
        out_shape=jax.ShapeDtypeStruct(block, F32),
        in_specs=[hbm] * 7,
        out_specs=vmem,
        scratch_shapes=[pltpu.VMEM(block, BF16)] * 3
        + [pltpu.SMEM((1, 2), jnp.int32)] * 4
        + [
            dma((7,)),
            pltpu.VMEM(block, BF16),
            pltpu.VMEM((J, Z) + block, BF16),
            pltpu.VMEM((J, Z) + block, BF16),
            pltpu.VMEM((Y,) + block, BF16),
            pltpu.VMEM((Y,) + block, BF16),
            pltpu.VMEM((8, 256), F32),
            pltpu.VMEM((8, 256), F32),
            pltpu.VMEM((Z,) + block, F32),
            pltpu.VMEM((Z,) + block, F32),
            pltpu.VMEM((Z,) + block, BF16),
            pltpu.VMEM((Z,) + block, BF16),
            pltpu.VMEM((2, 128, 128), BF16),
            pltpu.VMEM((2, 128, 128), BF16),
            dma((4,)),
            dma((Y,)), dma((Y + 2,)), dma((Y,)), dma((Y + 2,)),
            dma((COLS,)), dma((COLS,)), dma((COLS,)), dma((COLS,)),
            dma((Z,)), dma((Z,)), dma((Z,)), dma((Z,)),
            dma((2,)), dma((2,)),
        ],
        compiler_params=pltpu.CompilerParams(
            collective_id=0, has_side_effects=True, vmem_limit_bytes=60 * 1024 * 1024
        ),
        cost_estimate=pl.CostEstimate(flops=2 * 2 * 512 * 1024 * 256, bytes_accessed=6 * 1024 * 1024, transcendentals=0),
    )(fock, density, intersection, fock_mask, density_mask, intersection_mask, product_filter)


def solution(mesh):
    spec = P("row", "col")
    return jax.shard_map(
        per_device, mesh=mesh, in_specs=(spec,) * 7, out_specs=spec, check_vma=False
    )
```

```python
import jax
import jax.numpy as jnp
from jax import lax
from jax.experimental import pallas as pl
from jax.experimental.pallas import tpu as pltpu
from jax.sharding import PartitionSpec as P

MESH = pl.DeviceIdType.MESH
Z, Y, J = 4, 8, 4
X = 4
COLS = Z * J
H, HALF = 2, 64
BF16, F32 = jnp.bfloat16, jnp.float32


def masked(block, mask_ref):
    lane = lax.broadcasted_iota(jnp.int32, block.shape, 1)
    keep = jnp.where(lane < block.shape[1] // 2, mask_ref[0, 0], mask_ref[0, 1])
    return (block.astype(F32) * keep.astype(F32)).astype(BF16)


def kernel(
    f_hbm, p_hbm, s_hbm, fm_hbm, pm_hbm, sm_hbm, filt_hbm, out_ref,
    f_ref, p_ref, s_ref, fm_ref, pm_ref, sm_ref, filt_ref, in_sem,
    f_send, f_all, k_all, p_all, s_all, filt_send, filt_here,
    part, parts_in, part2, part_send, part2_in, tile_send, tile_in,
    t_send_sem, t_recv_sem, p_send_sem, p_recv_sem, s_send_sem, s_recv_sem,
    f_send_sem, f_recv_sem, f_core_sem, k_send_sem, k_recv_sem, k_core_sem,
    a_send_sem, a_recv_sem, b_send_sem, b_recv_sem, x_send_sem, x_recv_sem,
):
    r, c = lax.axis_index("row"), lax.axis_index("col")
    zh, y = lax.div(r, Y), lax.rem(r, Y)
    q, j = lax.div(c, J), lax.rem(c, J)
    zl, x, core = lax.div(c, 2 * X), lax.rem(lax.div(c, 2), X), lax.rem(c, 2)
    ahead = jnp.where(core == 0, 1, X - 1)
    moved = q != zh
    stays = jnp.logical_not(moved)
    swap_to = (q * Y + y, zh * J + j)

    def ring(d):
        return zh * Y + lax.rem(y + d, Y)

    def on_line(dz, dx, dc=0):
        return lax.rem(zl + dz, 2) * (2 * X) + lax.rem(x + dx, X) * 2 + lax.rem(core + dc, 2)

    def other(d):
        return lax.rem(zh + d, Z)

    def tile_to(b):
        return (2 * c + b, lax.div(r, 2))

    def off_diagonal(b):
        return r != 2 * c + b

    def copy(src, dst, send, recv, to):
        return pltpu.make_async_remote_copy(
            src_ref=src, dst_ref=dst, send_sem=send, recv_sem=recv, device_id=to, device_id_type=MESH
        )

    def await_sent(ref, sem):
        copy(ref, ref, sem, sem, swap_to).wait_send()

    def await_recv(ref, sem):
        copy(ref, ref, sem, sem, swap_to).wait_recv()

    fetches = []
    for n, (src, dst) in enumerate((
        (f_hbm, f_ref), (fm_hbm, fm_ref), (p_hbm, p_ref), (pm_hbm, pm_ref),
        (filt_hbm, filt_ref), (s_hbm, s_ref), (sm_hbm, sm_ref),
    )):
        fetches.append(pltpu.make_async_copy(src, dst, in_sem.at[n]))
        fetches[-1].start()

    barrier = pltpu.get_barrier_semaphore()

    def greet(to):
        pl.semaphore_signal(barrier, inc=1, device_id=to, device_id_type=MESH)

    for d in (1, 2, 6, 7):
        greet((ring(d), c))
    for to in (on_line(1, 0), on_line(0, 1), on_line(0, X - 1), on_line(0, 0, 1)):
        greet((r, to))
    for d in range(1, Z):
        greet((other(d) * Y + y, zh * J + j))

    @pl.when(moved)
    def _():
        greet((r, zh * J + j))

    for one in fetches[:5]:
        one.wait()
    f_send[...] = masked(f_ref[...], fm_ref).reshape(H, HALF, 256)
    p_all[y] = masked(p_ref[...], pm_ref)
    lane = lax.broadcasted_iota(jnp.int32, filt_send.shape, 1)
    filt_send[...] = jnp.where(lane < 128, filt_ref[0, 0], filt_ref[0, 1]).astype(F32)

    pl.semaphore_wait(barrier, 4 + 4 + (Z - 1) + jnp.where(moved, 1, 0))

    f_swaps = [
        copy(f_send.at[h], f_all.at[h, J * j + zh], t_send_sem.at[h], t_recv_sem.at[h], swap_to)
        for h in range(H)
    ]
    filt_swap = copy(filt_send, filt_here, t_send_sem.at[H], t_recv_sem.at[H], swap_to)

    @pl.when(moved)
    def _():
        for h in range(H):
            f_swaps[h].start()
        filt_swap.start()

    def ring_ref(buf, sems, src, half):
        slot = lax.rem(y + src, Y)
        if half is None:
            return buf.at[slot], sems[1].at[slot]
        return buf.at[slot, pl.ds(64 * half, 64)], sems[1].at[Y + half]

    def ring_send(buf, sems, src, d, half=None):
        ref, recv = ring_ref(buf, sems, src, half)
        copy(ref, ref, sems[0], recv, (ring(d), c)).start()

    def ring_wait(buf, sems, src, half=None):
        await_recv(*ring_ref(buf, sems, src, half))

    def ring_start(buf, sems):
        for d in (2, 6, 1, 7):
            ring_send(buf, sems, 0, d)

    def ring_relay(buf, sems):
        ring_wait(buf, sems, 6)
        ring_send(buf, sems, 6, 1)
        ring_send(buf, sems, 6, 2, 0)
        ring_wait(buf, sems, 2)
        ring_send(buf, sems, 2, 7)
        ring_send(buf, sems, 2, 6, 1)

    def ring_finish(buf, sems):
        for src in (1, 7, 5, 3):
            ring_wait(buf, sems, src)
        for half in range(2):
            ring_wait(buf, sems, 4, half)

    p_sems, s_sems = (p_send_sem, p_recv_sem), (s_send_sem, s_recv_sem)
    ring_start(p_all, p_sems)

    def slot_of(src):
        return J * lax.rem(src, J) + lax.div(src, J)

    def line_send(buf, sems, h, src, to):
        ref = buf.at[h, slot_of(src)]
        copy(ref, ref, sems[0].at[h], sems[1].at[h, src], (r, to)).start()

    def line_to_core(buf, sems, h, src):
        ref = buf.at[h, slot_of(src)]
        copy(ref, ref, sems[0].at[h], sems[2].at[h], (r, on_line(0, 0, 1))).start()

    def line_wait(buf, sems, h, src):
        await_recv(buf.at[h, slot_of(src)], sems[1].at[h, src])

    def line_start(buf, sems, h):
        for to in (on_line(1, 0), on_line(0, 1), on_line(0, X - 1)):
            line_send(buf, sems, h, c, to)
        line_to_core(buf, sems, h, c)

    def line_relay_z(buf, sems, h):
        src = on_line(1, 0)
        line_wait(buf, sems, h, src)
        line_send(buf, sems, h, src, on_line(0, 1))
        line_send(buf, sems, h, src, on_line(0, X - 1))
        line_to_core(buf, sems, h, src)

    def line_relay_x(buf, sems, h, dz):
        behind = on_line(dz, X - ahead)
        line_wait(buf, sems, h, behind)
        line_send(buf, sems, h, behind, on_line(0, ahead))
        line_to_core(buf, sems, h, behind)
        line_wait(buf, sems, h, on_line(dz, ahead))
        line_to_core(buf, sems, h, on_line(dz, ahead))

    def line_far(buf, sems, h, dz):
        line_wait(buf, sems, h, on_line(dz, 2))
        line_to_core(buf, sems, h, on_line(dz, 2))

    def line_steps(buf, sems, halves):
        for h in halves:
            line_relay_z(buf, sems, h)
        for dz in range(2):
            for h in halves:
                line_relay_x(buf, sems, h, dz)
        for dz in range(2):
            for h in halves:
                line_far(buf, sems, h, dz)

    def line_finish(buf, sems, h):
        await_recv(buf.at[h, pl.ds(0, COLS // 2)], sems[2].at[h])

    f_sems, k_sems = (f_send_sem, f_recv_sem, f_core_sem), (k_send_sem, k_recv_sem, k_core_sem)
    for h in range(H):

        @pl.when(moved)
        def _():
            await_recv(f_all.at[h, J * j + q], t_recv_sem.at[h])

        @pl.when(stays)
        def _():
            f_all[h, J * j + q] = f_send[h]

        line_start(f_all, f_sems, h)

    ring_relay(p_all, p_sems)
    line_steps(f_all, f_sems, range(H))

    for one in fetches[5:]:
        one.wait()
    s_all[y] = masked(s_ref[...], sm_ref)

    @pl.when(moved)
    def _():
        filt_swap.wait_recv()

    @pl.when(stays)
    def _():
        filt_here[...] = filt_send[...]

    ring_finish(p_all, p_sems)
    ring_start(s_all, s_sems)

    def product(left, h, right):
        total = None
        for k in range(J):
            a = left[h, J * k : J * (k + 1)].reshape(Z * HALF, 256)
            b = right[2 * k : 2 * k + 2].reshape(256, 256)
            term = jnp.dot(a, b, preferred_element_type=F32)
            total = term if total is None else total + term
        return total.reshape(Z, HALF, 256)

    def a_copy(h, d):
        z = other(d)
        return copy(part.at[h, z], parts_in.at[h, zh], a_send_sem.at[h], a_recv_sem.at[h], (q * Y + y, z * J + j))

    for h in range(H):
        line_finish(f_all, f_sems, h)
        part[h] = product(f_all, h, p_all)
        for d in (2, 1, 3):
            a_copy(h, d).start()

        @pl.when(moved)
        def _():
            a_copy(h, 0).start()

        @pl.when(stays)
        def _():
            parts_in[h, zh] = part[h, zh]

    ring_relay(s_all, s_sems)

    def keep(h):
        @pl.when(moved)
        def _():
            await_recv(parts_in.at[h], a_recv_sem.at[h])

        @pl.when(stays)
        def _():
            await_recv(parts_in.at[h, pl.ds(0, Z - 1)], a_recv_sem.at[h])

        first = (parts_in[h, 0] + parts_in[h, 1]) + (parts_in[h, 2] + parts_in[h, 3])
        k_all[h, J * j + q] = (first * filt_here[0:1, :]).astype(BF16)
        line_start(k_all, k_sems, h)

    def second(h):
        line_finish(k_all, k_sems, h)
        part2[h] = product(k_all, h, s_all)
        for d in (2, 1, 3):
            z = other(d)
            part_send[h, z] = part2[h, z].astype(BF16)
            copy(part_send.at[h, z], part2_in.at[h, zh], b_send_sem.at[h], b_recv_sem.at[h], (z * Y + y, c)).start()

    keep(0)
    line_steps(k_all, k_sems, (0,))
    keep(1)
    ring_finish(s_all, s_sems)
    second(0)
    line_steps(k_all, k_sems, (1,))
    second(1)

    def drain(ref, sem):
        await_sent(ref, sem)

    for h in range(H):
        drain(f_all.at[h, pl.ds(0, COLS - 1)], f_send_sem.at[h])
        drain(k_all.at[h, pl.ds(0, COLS - 1)], k_send_sem.at[h])

        @pl.when(moved)
        def _():
            f_swaps[h].wait_send()
            drain(part.at[h], a_send_sem.at[h])

        @pl.when(stays)
        def _():
            drain(part.at[h, pl.ds(0, Z - 1)], a_send_sem.at[h])

    drain(p_all.at[pl.ds(0, Y - 1)], p_send_sem)
    drain(s_all.at[pl.ds(0, Y - 1)], s_send_sem)

    @pl.when(moved)
    def _():
        filt_swap.wait_send()

    def x_copy(h, b):
        at = lax.rem(r, 2)
        return copy(
            tile_send.at[h, b], tile_in.at[at, pl.ds(HALF * h, HALF)], x_send_sem.at[h, b], x_recv_sem.at[h, at], tile_to(b)
        )

    for h in range(H):
        await_recv(part2_in.at[h, pl.ds(0, Z - 1)], b_recv_sem.at[h])
        total = part2[h, zh]
        for d in (1, 2, 3):
            total = total + part2_in[h, other(d)].astype(F32)
        rounded = total.astype(BF16)
        for b in range(2):
            tile_send[h, b] = rounded[:, 128 * b : 128 * (b + 1)]

            @pl.when(off_diagonal(b))
            def _():
                x_copy(h, b).start()

            @pl.when(jnp.logical_not(off_diagonal(b)))
            def _():
                tile_in[b, pl.ds(HALF * h, HALF)] = tile_send[h, b]

        out_ref[HALF * h : HALF * (h + 1), :] = rounded.astype(F32)

    for h in range(H):
        await_sent(part_send.at[h, pl.ds(0, Z - 1)], b_send_sem.at[h])

    for b in range(2):
        here = slice(128 * b, 128 * (b + 1))

        @pl.when(off_diagonal(b))
        def _():
            for h in range(H):
                await_recv(tile_in.at[b, pl.ds(HALF * h, HALF)], x_recv_sem.at[h, b])

        out_ref[:, here] = out_ref[:, here] - tile_in[b].astype(F32).T

    for b in range(2):

        @pl.when(off_diagonal(b))
        def _():
            for h in range(H):
                x_copy(h, b).wait_send()


def per_device(fock, density, intersection, fock_mask, density_mask, intersection_mask, product_filter):
    hbm = pl.BlockSpec(memory_space=pltpu.HBM)
    vmem = pl.BlockSpec(memory_space=pltpu.VMEM)
    dma = pltpu.SemaphoreType.DMA
    block, half = (128, 256), (HALF, 256)
    return pl.pallas_call(
        kernel,
        out_shape=jax.ShapeDtypeStruct(block, F32),
        in_specs=[hbm] * 7,
        out_specs=vmem,
        scratch_shapes=[pltpu.VMEM(block, BF16)] * 3
        + [pltpu.SMEM((1, 2), jnp.int32)] * 4
        + [
            dma((7,)),
            pltpu.VMEM((H,) + half, BF16),
            pltpu.VMEM((H, COLS) + half, BF16),
            pltpu.VMEM((H, COLS) + half, BF16),
            pltpu.VMEM((Y,) + block, BF16),
            pltpu.VMEM((Y,) + block, BF16),
            pltpu.VMEM((8, 256), F32),
            pltpu.VMEM((8, 256), F32),
            pltpu.VMEM((H, Z) + half, F32),
            pltpu.VMEM((H, Z) + half, F32),
            pltpu.VMEM((H, Z) + half, F32),
            pltpu.VMEM((H, Z) + half, BF16),
            pltpu.VMEM((H, Z) + half, BF16),
            pltpu.VMEM((H, 2, HALF, 128), BF16),
            pltpu.VMEM((2, 128, 128), BF16),
            dma((H + 1,)), dma((H + 1,)),
            dma, dma((Y + 2,)), dma, dma((Y + 2,)),
            dma((H,)), dma((H, COLS)), dma((H,)),
            dma((H,)), dma((H, COLS)), dma((H,)),
            dma((H,)), dma((H,)), dma((H,)), dma((H,)),
            dma((H, 2)), dma((H, 2)),
        ],
        compiler_params=pltpu.CompilerParams(
            collective_id=0, has_side_effects=True, vmem_limit_bytes=60 * 1024 * 1024
        ),
        cost_estimate=pl.CostEstimate(flops=2 * 2 * 512 * 1024 * 256, bytes_accessed=6 * 1024 * 1024, transcendentals=0),
    )(fock, density, intersection, fock_mask, density_mask, intersection_mask, product_filter)


def solution(mesh):
    spec = P("row", "col")
    return jax.shard_map(
        per_device, mesh=mesh, in_specs=(spec,) * 7, out_specs=spec, check_vma=False
    )
```

```python
import jax
import jax.numpy as jnp
from jax import lax
from jax.experimental import pallas as pl
from jax.experimental.pallas import tpu as pltpu
from jax.sharding import PartitionSpec as P

MESH = pl.DeviceIdType.MESH
Z, Y, J = 4, 8, 4
X = 4
COLS = Z * J
BF16, F32 = jnp.bfloat16, jnp.float32


def masked(block, mask_ref):
    lane = lax.broadcasted_iota(jnp.int32, block.shape, 1)
    keep = jnp.where(lane < block.shape[1] // 2, mask_ref[0, 0], mask_ref[0, 1])
    return (block.astype(F32) * keep.astype(F32)).astype(BF16)


def kernel(
    f_hbm, p_hbm, s_hbm, fm_hbm, pm_hbm, sm_hbm, filt_hbm, out_ref,
    f_ref, p_ref, s_ref, fm_ref, pm_ref, sm_ref, filt_ref, in_sem,
    f_send, f_all, k_all, p_all, s_all, filt_send, filt_here,
    part, parts_in, part2, part_send, part2_in, own_in, tile_send, tile_in,
    t_send_sem, t_recv_sem,
    p_send_sem, p_recv_sem, p_over_sem, p_core_sem, s_send_sem, s_recv_sem, s_over_sem, s_core_sem,
    f_send_sem, f_recv_sem, k_send_sem, k_recv_sem,
    a_send_sem, a_recv_sem, b_send_sem, b_recv_sem, o_send_sem, o_recv_sem, x_send_sem, x_recv_sem,
):
    r, c = lax.axis_index("row"), lax.axis_index("col")
    zh, y = lax.div(r, Y), lax.rem(r, Y)
    zl, x, core = lax.div(c, 2 * X), lax.rem(lax.div(c, 2), X), lax.rem(c, 2)
    q, jh = lax.div(c, J), lax.rem(x, 2)
    ahead = jnp.where(core == 0, 1, X - 1)
    over = (r, c + 1 - 2 * core)

    def holder(quarter, e, k, h, l):
        at = lax.rem(2 * lax.rem(quarter, 2) + h + e * (2 * h - 1) + X, X)
        return l * (2 * X) + at * 2 + k

    def slot_of(z_low, at):
        return X * z_low + lax.rem(at - 2 * lax.rem(zh, 2) + 1 + X, X)

    def static_slot(e, j):
        return X * (j % 2) + ((1 - e) if j < 2 else (2 + e))

    place = lax.rem(x - 2 * lax.rem(zh, 2) + 1 + X, X)
    held_h = lax.div(place, 2)
    held_e = jnp.where(lax.rem(place, 3) == 0, 1, 0)
    held_z = 2 * held_e + core
    held_from = (held_z * Y + y, J * zh + 2 * held_h + zl)
    term_col = J * zh + 2 * held_h + core
    move_col = holder(q, lax.div(zh, 2), lax.rem(zh, 2), jh, core)
    move_to = (q * Y + y, move_col)
    home = q == zh
    away = q != zh
    moved = jnp.logical_or(away, move_col != c)
    stays = jnp.logical_not(moved)
    mine = lax.rem(zh, 2) == core
    not_mine = lax.rem(zh, 2) != core

    def ring(d):
        return zh * Y + lax.rem(y + d, Y)

    def on_line(dz, dx):
        return lax.rem(zl + dz, 2) * (2 * X) + lax.rem(x + dx, X) * 2 + core

    def other(d):
        return lax.rem(zh + d, Z)

    def tile_to(b):
        return (2 * c + b, lax.div(r, 2))

    def off_diagonal(b):
        return r != 2 * c + b

    def copy(src, dst, send, recv, to):
        return pltpu.make_async_remote_copy(
            src_ref=src, dst_ref=dst, send_sem=send, recv_sem=recv, device_id=to, device_id_type=MESH
        )

    def await_sent(ref, sem):
        copy(ref, ref, sem, sem, over).wait_send()

    def await_recv(ref, sem):
        copy(ref, ref, sem, sem, over).wait_recv()

    fetches = []
    for n, (src, dst) in enumerate((
        (f_hbm, f_ref), (fm_hbm, fm_ref), (p_hbm, p_ref), (pm_hbm, pm_ref),
        (filt_hbm, filt_ref), (s_hbm, s_ref), (sm_hbm, sm_ref),
    )):
        fetches.append(pltpu.make_async_copy(src, dst, in_sem.at[n]))
        fetches[-1].start()

    barrier = pltpu.get_barrier_semaphore()

    def greet(to):
        pl.semaphore_signal(barrier, inc=1, device_id=to, device_id_type=MESH)

    for d in range(1, Z):
        greet((other(d) * Y + y, term_col))

    @pl.when(away)
    def _():
        greet((r, term_col))

    @pl.when(moved)
    def _():
        greet(held_from)

    for d in (1, 2, 6, 7):
        greet((ring(d), c))
    for dz, dx in ((1, 0), (0, 1), (0, X - 1), (1, X - ahead)):
        greet((r, on_line(dz, dx)))
    greet(over)

    for one in fetches[:5]:
        one.wait()
    f_send[...] = masked(f_ref[...], fm_ref)
    p_all[core, y] = masked(p_ref[...], pm_ref)
    lane = lax.broadcasted_iota(jnp.int32, filt_send.shape, 1)
    filt_send[...] = jnp.where(lane < 128, filt_ref[0, 0], filt_ref[0, 1]).astype(F32)

    pl.semaphore_wait(barrier, (Z - 1) + jnp.where(away, 1, 0) + jnp.where(moved, 1, 0) + 4 + 4 + 1)

    my_slot = slot_of(zl, x)
    to_slot = X * core + jnp.where(jh == 0, 1 - lax.div(zh, 2), 2 + lax.div(zh, 2))
    f_move = copy(f_send, f_all.at[to_slot], t_send_sem.at[0], t_recv_sem.at[0], move_to)
    filt_move = copy(filt_send, filt_here, t_send_sem.at[1], t_recv_sem.at[1], move_to)

    @pl.when(moved)
    def _():
        f_move.start()
        filt_move.start()

    def ring_ref(buf, sems, src, half):
        slot = lax.rem(y + src, Y)
        if half is None:
            return buf.at[core, slot], sems[1].at[slot]
        return buf.at[core, slot, pl.ds(64 * half, 64)], sems[1].at[Y + half]

    def ring_send(buf, sems, src, d, half=None):
        ref, recv = ring_ref(buf, sems, src, half)
        copy(ref, ref, sems[0], recv, (ring(d), c)).start()

    def ring_wait(buf, sems, src, half=None):
        await_recv(*ring_ref(buf, sems, src, half))

    def ring_start(buf, sems):
        for d in (2, 6, 1, 7):
            ring_send(buf, sems, 0, d)

    def cross(buf, sems, src):
        ref, _ = ring_ref(buf, sems, src, None)
        copy(ref, ref, sems[2], sems[3], over).start()

    def ring_relay(buf, sems, crossing):
        for src, on, far, half in ((6, 1, 2, 0), (2, 7, 6, 1)):
            ring_wait(buf, sems, src)
            ring_send(buf, sems, src, on)
            ring_send(buf, sems, src, far, half)
            if crossing:
                cross(buf, sems, src)

    def ring_finish(buf, sems, crossing):
        for src in (1, 7, 5, 3):
            ring_wait(buf, sems, src)
            if crossing:
                cross(buf, sems, src)
        for half in range(2):
            ring_wait(buf, sems, 4, half)
        if crossing:
            cross(buf, sems, 4)

    p_sems = (p_send_sem, p_recv_sem, p_over_sem, p_core_sem)
    s_sems = (s_send_sem, s_recv_sem, s_over_sem, s_core_sem)
    ring_start(p_all, p_sems)
    cross(p_all, p_sems, 0)

    def line_send(buf, sems, dz, dx, to):
        slot = slot_of(lax.rem(zl + dz, 2), lax.rem(x + dx, X))
        ref = buf.at[slot]
        copy(ref, ref, sems[0], sems[1].at[slot], (r, to)).start()

    def line_wait(buf, sems, dz, dx):
        slot = slot_of(lax.rem(zl + dz, 2), lax.rem(x + dx, X))
        await_recv(buf.at[slot], sems[1].at[slot])

    def line_start(buf, sems):
        for to in (on_line(1, 0), on_line(0, ahead), on_line(0, X - ahead)):
            line_send(buf, sems, 0, 0, to)

    def line_relay(buf, sems):
        line_wait(buf, sems, 1, 0)
        line_send(buf, sems, 1, 0, on_line(0, 1))
        line_send(buf, sems, 1, 0, on_line(0, X - 1))
        line_wait(buf, sems, 0, X - ahead)
        line_send(buf, sems, 0, X - ahead, on_line(0, ahead))
        line_send(buf, sems, 0, X - ahead, on_line(1, ahead))

    def line_finish(buf, sems):
        for dz, dx in ((0, ahead), (1, 1), (1, X - 1), (0, 2), (1, 2)):
            line_wait(buf, sems, dz, dx)

    f_sems, k_sems = (f_send_sem, f_recv_sem), (k_send_sem, k_recv_sem)

    @pl.when(moved)
    def _():
        await_recv(f_all.at[my_slot], t_recv_sem.at[0])

    @pl.when(stays)
    def _():
        f_all[my_slot] = f_send[...]

    line_start(f_all, f_sems)
    ring_relay(p_all, p_sems, True)
    line_relay(f_all, f_sems)

    for one in fetches[5:]:
        one.wait()
    s_all[core, y] = masked(s_ref[...], sm_ref)

    ring_finish(p_all, p_sems, True)
    ring_start(s_all, s_sems)

    @pl.when(moved)
    def _():
        filt_move.wait_recv()

    @pl.when(stays)
    def _():
        filt_here[...] = filt_send[...]

    line_finish(f_all, f_sems)
    await_recv(p_all.at[0], p_core_sem)

    def product(left, right, b):
        total = None
        for j in range(J):
            rows = jnp.concatenate([left[static_slot(e, j)] for e in range(2)], axis=0)
            depth = right[b, 2 * j : 2 * j + 2].reshape(256, 256)
            term = jnp.dot(rows, depth, preferred_element_type=F32)
            total = term if total is None else total + term
        return total.reshape(2, 128, 256)

    for b in range(2):
        part[b] = product(f_all, p_all, b)
        for e in (1, 0):
            send = copy(
                part.at[b, e], parts_in.at[zh], a_send_sem, a_recv_sem, (q * Y + y, holder(q, e, core, jh, b))
            )
            if e == 1:
                send.start()
            else:
                here = jnp.logical_and(home, zl == b)

                @pl.when(here)
                def _():
                    parts_in[zh] = part[b, e]

                @pl.when(jnp.logical_not(here))
                def _():
                    send.start()

    ring_relay(s_all, s_sems, False)
    ring_finish(s_all, s_sems, False)
    copy(s_all.at[core], s_all.at[core], s_over_sem, s_core_sem, over).start()

    @pl.when(away)
    def _():
        await_recv(parts_in, a_recv_sem)

    @pl.when(home)
    def _():
        await_recv(parts_in.at[pl.ds(0, Z - 1)], a_recv_sem)

    first = (parts_in[0] + parts_in[1]) + (parts_in[2] + parts_in[3])
    k_all[my_slot] = (first * filt_here[0:1, :]).astype(BF16)
    line_start(k_all, k_sems)
    line_relay(k_all, k_sems)
    await_recv(s_all.at[0], s_core_sem)
    line_finish(k_all, k_sems)

    for b in range(2):
        part2[b] = product(k_all, s_all, b)
        for e in range(2):
            z = 2 * e + core

            @pl.when(z != zh)
            def _():
                part_send[b, e] = part2[b, e].astype(BF16)
                copy(
                    part_send.at[b, e], part2_in.at[zh], b_send_sem, b_recv_sem.at[zh], (z * Y + y, c - core + b)
                ).start()

    own_e = lax.div(zh, 2)
    own_copy = copy(part2.at[1 - core, own_e], own_in, o_send_sem, o_recv_sem, over)

    @pl.when(mine)
    def _():
        own_copy.start()
        own_in[...] = part2[core, own_e]

    @pl.when(moved)
    def _():
        f_move.wait_send()
        filt_move.wait_send()

    await_sent(p_all.at[0, pl.ds(0, Y - 1)], p_send_sem)
    await_sent(s_all.at[0, pl.ds(0, Y - 1)], s_send_sem)
    await_sent(p_all.at[0], p_over_sem)
    await_sent(s_all.at[0], s_over_sem)
    await_sent(f_all.at[pl.ds(0, 2 * X - 1)], f_send_sem)
    await_sent(k_all.at[pl.ds(0, 2 * X - 1)], k_send_sem)

    @pl.when(away)
    def _():
        await_sent(parts_in, a_send_sem)

    @pl.when(home)
    def _():
        await_sent(parts_in.at[pl.ds(0, Z - 1)], a_send_sem)

    def x_copy(b):
        at = lax.rem(r, 2)
        return copy(tile_send.at[b], tile_in.at[at], x_send_sem.at[b], x_recv_sem.at[at], tile_to(b))

    @pl.when(not_mine)
    def _():
        await_recv(own_in, o_recv_sem)

    total = own_in[...]
    for d in (1, 3, 2):
        z = other(d)
        await_recv(part2_in.at[z], b_recv_sem.at[z])
        total = total + part2_in[z].astype(F32)
    rounded = total.astype(BF16)
    for b in range(2):
        tile_send[b] = rounded[:, 128 * b : 128 * (b + 1)]

        @pl.when(off_diagonal(b))
        def _():
            x_copy(b).start()

        @pl.when(jnp.logical_not(off_diagonal(b)))
        def _():
            tile_in[b] = tile_send[b]

    wide = rounded.astype(F32)

    @pl.when(mine)
    def _():
        own_copy.wait_send()
        await_sent(part_send.at[0], b_send_sem)

    @pl.when(not_mine)
    def _():
        await_sent(part_send, b_send_sem)

    for b in range(2):
        here = slice(128 * b, 128 * (b + 1))

        @pl.when(off_diagonal(b))
        def _():
            await_recv(tile_in.at[b], x_recv_sem.at[b])

        out_ref[:, here] = wide[:, here] - tile_in[b].astype(F32).T

    for b in range(2):

        @pl.when(off_diagonal(b))
        def _():
            x_copy(b).wait_send()


def per_device(fock, density, intersection, fock_mask, density_mask, intersection_mask, product_filter):
    hbm = pl.BlockSpec(memory_space=pltpu.HBM)
    vmem = pl.BlockSpec(memory_space=pltpu.VMEM)
    dma = pltpu.SemaphoreType.DMA
    block = (128, 256)
    return pl.pallas_call(
        kernel,
        out_shape=jax.ShapeDtypeStruct(block, F32),
        in_specs=[hbm] * 7,
        out_specs=vmem,
        scratch_shapes=[pltpu.VMEM(block, BF16)] * 3
        + [pltpu.SMEM((1, 2), jnp.int32)] * 4
        + [
            dma((7,)),
            pltpu.VMEM(block, BF16),
            pltpu.VMEM((2 * X,) + block, BF16),
            pltpu.VMEM((2 * X,) + block, BF16),
            pltpu.VMEM((2, Y) + block, BF16),
            pltpu.VMEM((2, Y) + block, BF16),
            pltpu.VMEM((8, 256), F32),
            pltpu.VMEM((8, 256), F32),
            pltpu.VMEM((2, 2) + block, F32),
            pltpu.VMEM((Z,) + block, F32),
            pltpu.VMEM((2, 2) + block, F32),
            pltpu.VMEM((2, 2) + block, BF16),
            pltpu.VMEM((Z,) + block, BF16),
            pltpu.VMEM(block, F32),
            pltpu.VMEM((2, 128, 128), BF16),
            pltpu.VMEM((2, 128, 128), BF16),
            dma((2,)), dma((2,)),
            dma, dma((Y + 2,)), dma, dma,
            dma, dma((Y + 2,)), dma, dma,
            dma, dma((2 * X,)), dma, dma((2 * X,)),
            dma, dma, dma, dma((Z,)), dma, dma,
            dma((2,)), dma((2,)),
        ],
        compiler_params=pltpu.CompilerParams(
            collective_id=0, has_side_effects=True, vmem_limit_bytes=60 * 1024 * 1024
        ),
        cost_estimate=pl.CostEstimate(flops=2 * 2 * 512 * 1024 * 256, bytes_accessed=6 * 1024 * 1024, transcendentals=0),
    )(fock, density, intersection, fock_mask, density_mask, intersection_mask, product_filter)


def solution(mesh):
    spec = P("row", "col")
    return jax.shard_map(
        per_device, mesh=mesh, in_specs=(spec,) * 7, out_specs=spec, check_vma=False
    )
```

```python
import jax
import jax.numpy as jnp
from jax import lax
from jax.experimental import pallas as pl
from jax.experimental.pallas import tpu as pltpu
from jax.sharding import PartitionSpec as P

MESH = pl.DeviceIdType.MESH
Z, Y, J = 4, 8, 4
X = 4
BF16, F32 = jnp.bfloat16, jnp.float32


def masked(block, mask_ref):
    lane = lax.broadcasted_iota(jnp.int32, block.shape, 1)
    keep = jnp.where(lane < block.shape[1] // 2, mask_ref[0, 0], mask_ref[0, 1])
    return (block.astype(F32) * keep.astype(F32)).astype(BF16)


def kernel(
    f_hbm, p_hbm, s_hbm, fm_hbm, pm_hbm, sm_hbm, filt_hbm, out_ref,
    f_ref, p_ref, s_ref, fm_ref, pm_ref, sm_ref, filt_ref, in_sem,
    f_send, f_all, k_all, p_all, s_all, filt_send, filt_here,
    part, parts_in, part2, part_send, part2_in, own_in, tile_send, tile_in,
    t_send_sem, t_recv_sem,
    p_send_sem, p_recv_sem, p_over_sem, p_core_sem, p_mate_sem,
    s_send_sem, s_recv_sem, s_over_sem, s_core_sem, s_mate_sem,
    f_send_sem, f_recv_sem, k_send_sem, k_recv_sem,
    a_send_sem, a_recv_sem, b_send_sem, b_recv_sem, o_send_sem, o_recv_sem, x_send_sem, x_recv_sem,
):
    r, c = lax.axis_index("row"), lax.axis_index("col")
    zh, y = lax.div(r, Y), lax.rem(r, Y)
    zl, x, core = lax.div(c, 2 * X), lax.rem(lax.div(c, 2), X), lax.rem(c, 2)
    over = (r, c + 1 - 2 * core)
    low = lax.rem(zh, 2)
    pair = zh + 1 - 2 * low
    mate = Z - 1 - zh
    half = lax.rem(lax.div(zh, 2) + low, 2)
    x_high = lax.div(x, 2)
    home = lax.rem(zl + x_high, 2) == half
    away = lax.rem(zl + x_high, 2) != half
    home_row = jnp.where(home, r, pair * Y + y)
    ahead = jnp.where(core == 0, 1, X - 1)

    def holder(l, k):
        return lax.rem(zl + l, 2) * (2 * X) + x * 2 + k

    def slot_of(z_low, at):
        return X * lax.rem(z_low + lax.div(at, 2) + half, 2) + at

    held_z = 2 * lax.div(zh, 2) + core
    held_zl = lax.rem(x_high + half, 2)
    held_l = lax.rem(zl + held_zl, 2)
    held_from = (held_z * Y + y, held_zl * (2 * X) + x * 2 + held_l)
    term_col = held_zl * (2 * X) + x * 2 + core
    move_to = (home_row, holder(core, low))
    stays = jnp.logical_and(home, jnp.logical_and(core == 0, low == 0))
    moved = jnp.logical_not(stays)
    mine = low == core
    not_mine = low != core

    def ring(d):
        return zh * Y + lax.rem(y + d, Y)

    def on_line(dz, dx):
        return lax.rem(zl + dz, 2) * (2 * X) + lax.rem(x + dx, X) * 2 + core

    def tile_to(b):
        return (2 * c + b, lax.div(r, 2))

    def off_diagonal(b):
        return r != 2 * c + b

    def copy(src, dst, send, recv, to):
        return pltpu.make_async_remote_copy(
            src_ref=src, dst_ref=dst, send_sem=send, recv_sem=recv, device_id=to, device_id_type=MESH
        )

    def await_sent(ref, sem):
        copy(ref, ref, sem, sem, over).wait_send()

    def await_recv(ref, sem):
        copy(ref, ref, sem, sem, over).wait_recv()

    fetches = []
    for n, (src, dst) in enumerate((
        (f_hbm, f_ref), (fm_hbm, fm_ref), (p_hbm, p_ref), (pm_hbm, pm_ref),
        (filt_hbm, filt_ref), (s_hbm, s_ref), (sm_hbm, sm_ref),
    )):
        fetches.append(pltpu.make_async_copy(src, dst, in_sem.at[n]))
        fetches[-1].start()

    barrier = pltpu.get_barrier_semaphore()

    def greet(to):
        pl.semaphore_signal(barrier, inc=1, device_id=to, device_id_type=MESH)

    @pl.when(moved)
    def _():
        greet(held_from)

    greet((mate * Y + y, c))
    for d in (2, 6, 1, 7):
        greet((ring(d), c))
    for dz, dx in ((1, 0), (0, 1), (0, X - 1), (1, X - ahead)):
        greet((r, on_line(dz, dx)))
    greet(over)
    greet((pair * Y + y, term_col))

    @pl.when(away)
    def _():
        greet((r, term_col))

    for one in fetches[:5]:
        one.wait()
    f_send[...] = masked(f_ref[...], fm_ref)
    p_all[core, y, low] = masked(p_ref[...], pm_ref)
    lane = lax.broadcasted_iota(jnp.int32, filt_send.shape, 1)
    filt_send[...] = jnp.where(lane < 128, filt_ref[0, 0], filt_ref[0, 1]).astype(F32)

    pl.semaphore_wait(barrier, jnp.where(moved, 1, 0) + 1 + 4 + 4 + 1 + 1 + jnp.where(away, 1, 0))

    my_slot = slot_of(zl, x)
    f_move = copy(f_send, f_all.at[X * core + x], t_send_sem.at[0], t_recv_sem.at[0], move_to)
    filt_move = copy(filt_send, filt_here, t_send_sem.at[1], t_recv_sem.at[1], move_to)

    @pl.when(moved)
    def _():
        f_move.start()
        filt_move.start()

    def mate_copy(buf, sem, t):
        ref = buf.at[core, y, t]
        return copy(ref, ref, sem.at[0], sem.at[1], (mate * Y + y, c))

    def ring_ref(buf, sems, src, t, part_of):
        slot = lax.rem(y + src, Y)
        at = Y + part_of if part_of is not None else slot
        if t is None:
            ref = buf.at[core, slot] if part_of is None else buf.at[core, slot, part_of]
            return ref, sems[1].at[0, at]
        ref = buf.at[core, slot, t] if part_of is None else buf.at[core, slot, t, pl.ds(64 * part_of, 64)]
        return ref, sems[1].at[t, at]

    def ring_send(buf, sems, src, t, d, part_of=None):
        ref, recv = ring_ref(buf, sems, src, t, part_of)
        copy(ref, ref, sems[0], recv, (ring(d), c)).start()

    def ring_wait(buf, sems, src, t, part_of=None):
        await_recv(*ring_ref(buf, sems, src, t, part_of))

    def ring_start(buf, sems, t):
        for d in (2, 6, 1, 7):
            ring_send(buf, sems, 0, t, d)

    def ring_relay(buf, sems, t):
        for src, on, far, part_of in ((6, 1, 2, 0), (2, 7, 6, 1)):
            ring_wait(buf, sems, src, t)
            ring_send(buf, sems, src, t, on)
            ring_send(buf, sems, src, t, far, part_of)

    def cross(buf, sems, src):
        ref = buf.at[core, lax.rem(y + src, Y)]
        copy(ref, ref, sems[2], sems[3], over).start()

    def ring_finish(buf, sems, ts):
        for src in (1, 7, 5, 3):
            for t in ts:
                ring_wait(buf, sems, src, t)
            cross(buf, sems, src)
        for t in ts:
            for part_of in range(2):
                ring_wait(buf, sems, 4, t, part_of)
        cross(buf, sems, 4)

    p_sems = (p_send_sem, p_recv_sem, p_over_sem, p_core_sem)
    s_sems = (s_send_sem, s_recv_sem, s_over_sem, s_core_sem)
    mate_copy(p_all, p_mate_sem, low).start()
    ring_start(p_all, p_sems, low)

    def line_send(buf, sems, dz, dx, to):
        slot = slot_of(lax.rem(zl + dz, 2), lax.rem(x + dx, X))
        ref = buf.at[slot]
        copy(ref, ref, sems[0], sems[1].at[slot], (r, to)).start()

    def line_wait(buf, sems, dz, dx):
        slot = slot_of(lax.rem(zl + dz, 2), lax.rem(x + dx, X))
        await_recv(buf.at[slot], sems[1].at[slot])

    def line_start(buf, sems):
        for to in (on_line(1, 0), on_line(0, ahead), on_line(0, X - ahead)):
            line_send(buf, sems, 0, 0, to)

    def line_relay(buf, sems):
        line_wait(buf, sems, 1, 0)
        line_send(buf, sems, 1, 0, on_line(0, 1))
        line_send(buf, sems, 1, 0, on_line(0, X - 1))
        line_wait(buf, sems, 0, X - ahead)
        line_send(buf, sems, 0, X - ahead, on_line(0, ahead))
        line_send(buf, sems, 0, X - ahead, on_line(1, ahead))

    def line_finish(buf, sems):
        for dz, dx in ((0, ahead), (1, 1), (1, X - 1), (0, 2), (1, 2)):
            line_wait(buf, sems, dz, dx)

    f_sems, k_sems = (f_send_sem, f_recv_sem), (k_send_sem, k_recv_sem)
    mate_copy(p_all, p_mate_sem, 1 - low).wait_recv()
    ring_start(p_all, p_sems, 1 - low)

    @pl.when(moved)
    def _():
        await_recv(f_all.at[my_slot], t_recv_sem.at[0])

    @pl.when(stays)
    def _():
        f_all[my_slot] = f_send[...]

    line_start(f_all, f_sems)
    cross(p_all, p_sems, 0)

    for one in fetches[5:]:
        one.wait()
    s_all[core, y, low] = masked(s_ref[...], sm_ref)
    mate_copy(s_all, s_mate_sem, low).start()

    ring_relay(p_all, p_sems, low)
    line_relay(f_all, f_sems)
    ring_relay(p_all, p_sems, 1 - low)
    cross(p_all, p_sems, 2)
    cross(p_all, p_sems, 6)
    ring_finish(p_all, p_sems, (low, 1 - low))
    mate_copy(s_all, s_mate_sem, 1 - low).wait_recv()
    ring_start(s_all, s_sems, None)
    cross(s_all, s_sems, 0)

    @pl.when(moved)
    def _():
        filt_move.wait_recv()

    @pl.when(stays)
    def _():
        filt_here[...] = filt_send[...]

    line_finish(f_all, f_sems)
    await_recv(p_all.at[0], p_core_sem)

    def product(left, right, b):
        total = None
        for t in range(2):
            for j in range(J):
                rows = left[X * (j % 2) + 2 * t + j // 2]
                depth = jnp.concatenate([right[b, 2 * j, t], right[b, 2 * j + 1, t]], axis=0)
                term = jnp.dot(rows, depth, preferred_element_type=F32)
                total = term if total is None else total + term
        return total

    for b in (1, 0):
        part[b] = product(f_all, p_all, b)
        send = copy(part.at[b], parts_in.at[low], a_send_sem, a_recv_sem, (home_row, holder(b, core)))
        if b == 1:
            send.start()
        else:

            @pl.when(home)
            def _():
                parts_in[low] = part[b]

            @pl.when(away)
            def _():
                send.start()

    @pl.when(away)
    def _():
        await_recv(parts_in, a_recv_sem)

    @pl.when(home)
    def _():
        await_recv(parts_in.at[0], a_recv_sem)

    k_all[my_slot] = ((parts_in[0] + parts_in[1]) * filt_here[0:1, :]).astype(BF16)
    line_start(k_all, k_sems)
    ring_relay(s_all, s_sems, None)
    line_relay(k_all, k_sems)
    cross(s_all, s_sems, 2)
    cross(s_all, s_sems, 6)
    ring_finish(s_all, s_sems, (None,))
    line_finish(k_all, k_sems)
    await_recv(s_all.at[0], s_core_sem)

    def second(b):
        part2[b] = product(k_all, s_all, b)

        @pl.when(not_mine)
        def _():
            part_send[b] = part2[b].astype(BF16)
            copy(part_send.at[b], part2_in, b_send_sem, b_recv_sem, (pair * Y + y, c - core + b)).start()

    for b in range(2):
        second(b)
    own_copy = copy(part2.at[1 - core], own_in, o_send_sem, o_recv_sem, over)

    @pl.when(mine)
    def _():
        own_copy.start()
        own_in[...] = part2[core]

    @pl.when(moved)
    def _():
        f_move.wait_send()
        filt_move.wait_send()

    mate_copy(p_all, p_mate_sem, low).wait_send()
    mate_copy(s_all, s_mate_sem, low).wait_send()
    await_sent(p_all.at[0, pl.ds(0, Y - 1)], p_send_sem)
    await_sent(s_all.at[0, pl.ds(0, Y - 1)], s_send_sem)
    await_sent(p_all.at[0], p_over_sem)
    await_sent(s_all.at[0], s_over_sem)
    await_sent(f_all.at[pl.ds(0, 2 * X - 1)], f_send_sem)
    await_sent(k_all.at[pl.ds(0, 2 * X - 1)], k_send_sem)

    @pl.when(away)
    def _():
        await_sent(part, a_send_sem)

    @pl.when(home)
    def _():
        await_sent(part.at[0], a_send_sem)

    def x_copy(b):
        at = lax.rem(r, 2)
        return copy(tile_send.at[b], tile_in.at[at], x_send_sem.at[b], x_recv_sem.at[at], tile_to(b))

    @pl.when(not_mine)
    def _():
        await_recv(own_in, o_recv_sem)

    await_recv(part2_in, b_recv_sem)
    rounded = (own_in[...] + part2_in[...].astype(F32)).astype(BF16)
    for b in range(2):
        tile_send[b] = rounded[:, 128 * b : 128 * (b + 1)]

        @pl.when(off_diagonal(b))
        def _():
            x_copy(b).start()

        @pl.when(jnp.logical_not(off_diagonal(b)))
        def _():
            tile_in[b] = tile_send[b]

    wide = rounded.astype(F32)

    @pl.when(mine)
    def _():
        own_copy.wait_send()

    @pl.when(not_mine)
    def _():
        await_sent(part_send, b_send_sem)

    for b in range(2):
        here = slice(128 * b, 128 * (b + 1))

        @pl.when(off_diagonal(b))
        def _():
            await_recv(tile_in.at[b], x_recv_sem.at[b])

        out_ref[:, here] = wide[:, here] - tile_in[b].astype(F32).T

    for b in range(2):

        @pl.when(off_diagonal(b))
        def _():
            x_copy(b).wait_send()


def per_device(fock, density, intersection, fock_mask, density_mask, intersection_mask, product_filter):
    hbm = pl.BlockSpec(memory_space=pltpu.HBM)
    vmem = pl.BlockSpec(memory_space=pltpu.VMEM)
    dma = pltpu.SemaphoreType.DMA
    block = (128, 256)
    return pl.pallas_call(
        kernel,
        out_shape=jax.ShapeDtypeStruct(block, F32),
        in_specs=[hbm] * 7,
        out_specs=vmem,
        scratch_shapes=[pltpu.VMEM(block, BF16)] * 3
        + [pltpu.SMEM((1, 2), jnp.int32)] * 4
        + [
            dma((7,)),
            pltpu.VMEM(block, BF16),
            pltpu.VMEM((2 * X,) + block, BF16),
            pltpu.VMEM((2 * X,) + block, BF16),
            pltpu.VMEM((2, Y, 2) + block, BF16),
            pltpu.VMEM((2, Y, 2) + block, BF16),
            pltpu.VMEM((8, 256), F32),
            pltpu.VMEM((8, 256), F32),
            pltpu.VMEM((2,) + block, F32),
            pltpu.VMEM((2,) + block, F32),
            pltpu.VMEM((2,) + block, F32),
            pltpu.VMEM((2,) + block, BF16),
            pltpu.VMEM(block, BF16),
            pltpu.VMEM(block, F32),
            pltpu.VMEM((2, 128, 128), BF16),
            pltpu.VMEM((2, 128, 128), BF16),
            dma((2,)), dma((2,)),
            dma, dma((2, Y + 2)), dma, dma, dma((2,)),
            dma, dma((2, Y + 2)), dma, dma, dma((2,)),
            dma, dma((2 * X,)), dma, dma((2 * X,)),
            dma, dma, dma, dma, dma, dma,
            dma((2,)), dma((2,)),
        ],
        compiler_params=pltpu.CompilerParams(
            collective_id=0, has_side_effects=True, vmem_limit_bytes=60 * 1024 * 1024
        ),
        cost_estimate=pl.CostEstimate(flops=2 * 2 * 512 * 1024 * 256, bytes_accessed=6 * 1024 * 1024, transcendentals=0),
    )(fock, density, intersection, fock_mask, density_mask, intersection_mask, product_filter)


def solution(mesh):
    spec = P("row", "col")
    return jax.shard_map(
        per_device, mesh=mesh, in_specs=(spec,) * 7, out_specs=spec, check_vma=False
    )
```

```python
import jax
import jax.numpy as jnp
from jax import lax
from jax.experimental import pallas as pl
from jax.experimental.pallas import tpu as pltpu
from jax.sharding import PartitionSpec as P

MESH = pl.DeviceIdType.MESH
Z, Y, J = 4, 8, 4
X = 4
BF16, F32 = jnp.bfloat16, jnp.float32


def masked(block, mask_ref):
    lane = lax.broadcasted_iota(jnp.int32, block.shape, 1)
    keep = jnp.where(lane < block.shape[1] // 2, mask_ref[0, 0], mask_ref[0, 1])
    return (block.astype(F32) * keep.astype(F32)).astype(BF16)


def kernel(
    f_hbm, p_hbm, s_hbm, fm_hbm, pm_hbm, sm_hbm, filt_hbm, out_ref,
    f_ref, p_ref, s_ref, fm_ref, pm_ref, sm_ref, filt_ref, in_sem,
    f_send, f_all, k_all, p_all, s_all, filt_send, filt_here,
    part, near_in, far_send, far_in, part2, part_send, part2_in, own_in, tile_send, tile_in,
    t_send_sem, t_recv_sem,
    p_send_sem, p_recv_sem, p_over_sem, p_core_sem, p_mate_sem,
    s_send_sem, s_recv_sem, s_over_sem, s_core_sem, s_mate_sem,
    f_send_sem, f_recv_sem, k_send_sem, k_recv_sem,
    a_send_sem, a_recv_sem, b_send_sem, b_recv_sem, o_send_sem, o_recv_sem, x_send_sem, x_recv_sem,
):
    r, c = lax.axis_index("row"), lax.axis_index("col")
    zh, y = lax.div(r, Y), lax.rem(r, Y)
    zl, x, core = lax.div(c, 2 * X), lax.rem(lax.div(c, 2), X), lax.rem(c, 2)
    over = (r, c + 1 - 2 * core)
    low = lax.rem(zh, 2)
    pair = zh + 1 - 2 * low
    mate = Z - 1 - zh
    half = lax.rem(lax.div(zh, 2) + low, 2)
    x_high = lax.div(x, 2)
    home = lax.rem(zl + x_high, 2) == half
    away = lax.rem(zl + x_high, 2) != half
    home_row = jnp.where(home, r, pair * Y + y)
    ahead = jnp.where(core == 0, 1, X - 1)

    def holder(l, k):
        return lax.rem(zl + l, 2) * (2 * X) + x * 2 + k

    def slot_of(z_low, at):
        return X * lax.rem(z_low + lax.div(at, 2) + half, 2) + at

    held_z = 2 * lax.div(zh, 2) + core
    held_zl = lax.rem(x_high + half, 2)
    held_l = lax.rem(zl + held_zl, 2)
    held_from = (held_z * Y + y, held_zl * (2 * X) + x * 2 + held_l)
    term_col = held_zl * (2 * X) + x * 2 + core
    move_to = (home_row, holder(core, low))
    stays = jnp.logical_and(home, jnp.logical_and(core == 0, low == 0))
    moved = jnp.logical_not(stays)
    mine = low == core
    not_mine = low != core

    def ring(d):
        return zh * Y + lax.rem(y + d, Y)

    def on_line(dz, dx):
        return lax.rem(zl + dz, 2) * (2 * X) + lax.rem(x + dx, X) * 2 + core

    def tile_to(b):
        return (2 * c + b, lax.div(r, 2))

    def off_diagonal(b):
        return r != 2 * c + b

    def copy(src, dst, send, recv, to):
        return pltpu.make_async_remote_copy(
            src_ref=src, dst_ref=dst, send_sem=send, recv_sem=recv, device_id=to, device_id_type=MESH
        )

    def await_sent(ref, sem):
        copy(ref, ref, sem, sem, over).wait_send()

    def await_recv(ref, sem):
        copy(ref, ref, sem, sem, over).wait_recv()

    fetches = []
    for n, (src, dst) in enumerate((
        (f_hbm, f_ref), (fm_hbm, fm_ref), (p_hbm, p_ref), (pm_hbm, pm_ref),
        (filt_hbm, filt_ref), (s_hbm, s_ref), (sm_hbm, sm_ref),
    )):
        fetches.append(pltpu.make_async_copy(src, dst, in_sem.at[n]))
        fetches[-1].start()

    barrier = pltpu.get_barrier_semaphore()

    def greet(to):
        pl.semaphore_signal(barrier, inc=1, device_id=to, device_id_type=MESH)

    @pl.when(moved)
    def _():
        greet(held_from)

    greet((mate * Y + y, c))
    for d in (2, 6, 1, 7):
        greet((ring(d), c))
    for dz, dx in ((1, 0), (0, 1), (0, X - 1), (1, X - ahead)):
        greet((r, on_line(dz, dx)))
    greet(over)
    greet((pair * Y + y, term_col))

    @pl.when(away)
    def _():
        greet((r, term_col))

    for one in fetches[:5]:
        one.wait()
    f_send[...] = masked(f_ref[...], fm_ref)
    p_all[core, y, low] = masked(p_ref[...], pm_ref)
    lane = lax.broadcasted_iota(jnp.int32, filt_send.shape, 1)
    filt_send[...] = jnp.where(lane < 128, filt_ref[0, 0], filt_ref[0, 1]).astype(F32)

    pl.semaphore_wait(barrier, jnp.where(moved, 1, 0) + 1 + 4 + 4 + 1 + 1 + jnp.where(away, 1, 0))

    my_slot = slot_of(zl, x)
    f_move = copy(f_send, f_all.at[X * core + x], t_send_sem.at[0], t_recv_sem.at[0], move_to)
    filt_move = copy(filt_send, filt_here, t_send_sem.at[1], t_recv_sem.at[1], move_to)

    @pl.when(moved)
    def _():
        f_move.start()
        filt_move.start()

    def mate_copy(buf, sem, t):
        ref = buf.at[core, y, t]
        return copy(ref, ref, sem.at[0], sem.at[1], (mate * Y + y, c))

    def ring_ref(buf, sems, src, t, part_of):
        slot = lax.rem(y + src, Y)
        at = Y + part_of if part_of is not None else slot
        if t is None:
            ref = buf.at[core, slot] if part_of is None else buf.at[core, slot, part_of]
            return ref, sems[1].at[0, at]
        ref = buf.at[core, slot, t] if part_of is None else buf.at[core, slot, t, pl.ds(64 * part_of, 64)]
        return ref, sems[1].at[t, at]

    def ring_send(buf, sems, src, t, d, part_of=None):
        ref, recv = ring_ref(buf, sems, src, t, part_of)
        copy(ref, ref, sems[0], recv, (ring(d), c)).start()

    def ring_wait(buf, sems, src, t, part_of=None):
        await_recv(*ring_ref(buf, sems, src, t, part_of))

    def ring_start(buf, sems, t):
        for d in (1, 7):
            ring_send(buf, sems, 0, t, d)

    def ring_pass(buf, sems, t):
        for src, on in ((7, 1), (1, 7)):
            ring_wait(buf, sems, src, t)
            ring_send(buf, sems, src, t, on)

    def ring_relay(buf, sems, t):
        for src, on, far, part_of in ((6, 1, 2, 0), (2, 7, 6, 1)):
            ring_wait(buf, sems, src, t)
            ring_send(buf, sems, src, t, on)
            ring_send(buf, sems, src, t, far, part_of)

    def cross(buf, sems, src):
        ref = buf.at[core, lax.rem(y + src, Y)]
        copy(ref, ref, sems[2], sems[3], over).start()

    def ring_finish(buf, sems, ts):
        for src in (5, 3):
            for t in ts:
                ring_wait(buf, sems, src, t)
            cross(buf, sems, src)
        for t in ts:
            for part_of in range(2):
                ring_wait(buf, sems, 4, t, part_of)
        cross(buf, sems, 4)

    p_sems = (p_send_sem, p_recv_sem, p_over_sem, p_core_sem)
    s_sems = (s_send_sem, s_recv_sem, s_over_sem, s_core_sem)
    mate_copy(p_all, p_mate_sem, low).start()
    ring_start(p_all, p_sems, low)

    def line_send(buf, sems, dz, dx, to):
        slot = slot_of(lax.rem(zl + dz, 2), lax.rem(x + dx, X))
        ref = buf.at[slot]
        copy(ref, ref, sems[0], sems[1].at[slot], (r, to)).start()

    def line_wait(buf, sems, dz, dx):
        slot = slot_of(lax.rem(zl + dz, 2), lax.rem(x + dx, X))
        await_recv(buf.at[slot], sems[1].at[slot])

    def line_start(buf, sems):
        for to in (on_line(1, 0), on_line(0, ahead), on_line(0, X - ahead)):
            line_send(buf, sems, 0, 0, to)

    def line_relay(buf, sems):
        line_wait(buf, sems, 1, 0)
        line_send(buf, sems, 1, 0, on_line(0, 1))
        line_send(buf, sems, 1, 0, on_line(0, X - 1))
        line_wait(buf, sems, 0, X - ahead)
        line_send(buf, sems, 0, X - ahead, on_line(0, ahead))
        line_send(buf, sems, 0, X - ahead, on_line(1, ahead))

    def line_finish(buf, sems):
        for dz, dx in ((0, ahead), (1, 1), (1, X - 1), (0, 2), (1, 2)):
            line_wait(buf, sems, dz, dx)

    f_sems, k_sems = (f_send_sem, f_recv_sem), (k_send_sem, k_recv_sem)
    ring_pass(p_all, p_sems, low)
    mate_copy(p_all, p_mate_sem, 1 - low).wait_recv()
    ring_start(p_all, p_sems, 1 - low)

    @pl.when(moved)
    def _():
        await_recv(f_all.at[my_slot], t_recv_sem.at[0])

    @pl.when(stays)
    def _():
        f_all[my_slot] = f_send[...]

    line_start(f_all, f_sems)
    cross(p_all, p_sems, 0)
    ring_relay(p_all, p_sems, low)

    for one in fetches[5:]:
        one.wait()
    s_all[core, y, low] = masked(s_ref[...], sm_ref)
    mate_copy(s_all, s_mate_sem, low).start()

    line_relay(f_all, f_sems)
    ring_pass(p_all, p_sems, 1 - low)
    cross(p_all, p_sems, 1)
    cross(p_all, p_sems, 7)
    ring_relay(p_all, p_sems, 1 - low)
    cross(p_all, p_sems, 2)
    cross(p_all, p_sems, 6)
    ring_finish(p_all, p_sems, (low, 1 - low))
    mate_copy(s_all, s_mate_sem, 1 - low).wait_recv()
    ring_start(s_all, s_sems, None)
    cross(s_all, s_sems, 0)

    @pl.when(moved)
    def _():
        filt_move.wait_recv()

    @pl.when(stays)
    def _():
        filt_here[...] = filt_send[...]

    line_finish(f_all, f_sems)

    def product(left, right, b):
        total = None
        for t in range(2):
            for j in range(J):
                rows = left[X * (j % 2) + 2 * t + j // 2]
                depth = jnp.concatenate([right[b, 2 * j, t], right[b, 2 * j + 1, t]], axis=0)
                term = jnp.dot(rows, depth, preferred_element_type=F32)
                total = term if total is None else total + term
        return total

    def near_copy():
        return copy(part, near_in, a_send_sem.at[0], a_recv_sem.at[0], (r, holder(1, core)))

    def first_terms(b):
        term = product(f_all, p_all, b)

        @pl.when(away)
        def _():
            far_send[b] = term.astype(BF16)
            copy(
                far_send.at[b], far_in, a_send_sem.at[1], a_recv_sem.at[1], (pair * Y + y, holder(b, core))
            ).start()

        @pl.when(jnp.logical_and(home, b == 0))
        def _():
            near_in[...] = term

        @pl.when(jnp.logical_and(home, b == 1))
        def _():
            part[...] = term
            near_copy().start()

    first_terms(core)
    await_recv(p_all.at[0], p_core_sem)
    first_terms(1 - core)
    ring_pass(s_all, s_sems, None)
    cross(s_all, s_sems, 1)
    cross(s_all, s_sems, 7)

    @pl.when(away)
    def _():
        await_recv(near_in, a_recv_sem.at[0])

    await_recv(far_in, a_recv_sem.at[1])
    k_all[my_slot] = ((near_in[...] + far_in[...].astype(F32)) * filt_here[0:1, :]).astype(BF16)
    line_start(k_all, k_sems)
    ring_relay(s_all, s_sems, None)
    line_relay(k_all, k_sems)
    cross(s_all, s_sems, 2)
    cross(s_all, s_sems, 6)
    ring_finish(s_all, s_sems, (None,))
    line_finish(k_all, k_sems)

    own_copy = copy(part2, own_in, o_send_sem, o_recv_sem, over)

    def second_terms(b, others):
        term = product(k_all, s_all, b)

        @pl.when(not_mine)
        def _():
            part_send[b] = term.astype(BF16)
            copy(part_send.at[b], part2_in, b_send_sem, b_recv_sem, (pair * Y + y, c - core + b)).start()

        @pl.when(mine)
        def _():
            if others:
                part2[...] = term
                own_copy.start()
            else:
                own_in[...] = term

    second_terms(core, False)
    await_recv(s_all.at[0], s_core_sem)
    second_terms(1 - core, True)

    @pl.when(moved)
    def _():
        f_move.wait_send()
        filt_move.wait_send()

    mate_copy(p_all, p_mate_sem, low).wait_send()
    mate_copy(s_all, s_mate_sem, low).wait_send()
    await_sent(p_all.at[0, pl.ds(0, Y - 1)], p_send_sem)
    await_sent(s_all.at[0, pl.ds(0, Y - 1)], s_send_sem)
    await_sent(p_all.at[0], p_over_sem)
    await_sent(s_all.at[0], s_over_sem)
    await_sent(f_all.at[pl.ds(0, 2 * X - 1)], f_send_sem)
    await_sent(k_all.at[pl.ds(0, 2 * X - 1)], k_send_sem)

    @pl.when(away)
    def _():
        await_sent(far_send, a_send_sem.at[1])

    @pl.when(home)
    def _():
        near_copy().wait_send()

    def x_copy(b):
        at = lax.rem(r, 2)
        return copy(tile_send.at[b], tile_in.at[at], x_send_sem.at[b], x_recv_sem.at[at], tile_to(b))

    @pl.when(not_mine)
    def _():
        await_recv(own_in, o_recv_sem)

    await_recv(part2_in, b_recv_sem)
    rounded = (own_in[...] + part2_in[...].astype(F32)).astype(BF16)
    for b in range(2):
        tile_send[b] = rounded[:, 128 * b : 128 * (b + 1)]

        @pl.when(off_diagonal(b))
        def _():
            x_copy(b).start()

        @pl.when(jnp.logical_not(off_diagonal(b)))
        def _():
            tile_in[b] = tile_send[b]

    wide = rounded.astype(F32)

    @pl.when(mine)
    def _():
        own_copy.wait_send()

    @pl.when(not_mine)
    def _():
        await_sent(part_send, b_send_sem)

    for b in range(2):
        here = slice(128 * b, 128 * (b + 1))

        @pl.when(off_diagonal(b))
        def _():
            await_recv(tile_in.at[b], x_recv_sem.at[b])

        out_ref[:, here] = wide[:, here] - tile_in[b].astype(F32).T

    for b in range(2):

        @pl.when(off_diagonal(b))
        def _():
            x_copy(b).wait_send()


def per_device(fock, density, intersection, fock_mask, density_mask, intersection_mask, product_filter):
    hbm = pl.BlockSpec(memory_space=pltpu.HBM)
    vmem = pl.BlockSpec(memory_space=pltpu.VMEM)
    dma = pltpu.SemaphoreType.DMA
    block = (128, 256)
    return pl.pallas_call(
        kernel,
        out_shape=jax.ShapeDtypeStruct(block, F32),
        in_specs=[hbm] * 7,
        out_specs=vmem,
        scratch_shapes=[pltpu.VMEM(block, BF16)] * 3
        + [pltpu.SMEM((1, 2), jnp.int32)] * 4
        + [
            dma((7,)),
            pltpu.VMEM(block, BF16),
            pltpu.VMEM((2 * X,) + block, BF16),
            pltpu.VMEM((2 * X,) + block, BF16),
            pltpu.VMEM((2, Y, 2) + block, BF16),
            pltpu.VMEM((2, Y, 2) + block, BF16),
            pltpu.VMEM((8, 256), F32),
            pltpu.VMEM((8, 256), F32),
            pltpu.VMEM(block, F32),
            pltpu.VMEM(block, F32),
            pltpu.VMEM((2,) + block, BF16),
            pltpu.VMEM(block, BF16),
            pltpu.VMEM(block, F32),
            pltpu.VMEM((2,) + block, BF16),
            pltpu.VMEM(block, BF16),
            pltpu.VMEM(block, F32),
            pltpu.VMEM((2, 128, 128), BF16),
            pltpu.VMEM((2, 128, 128), BF16),
            dma((2,)), dma((2,)),
            dma, dma((2, Y + 2)), dma, dma, dma((2,)),
            dma, dma((2, Y + 2)), dma, dma, dma((2,)),
            dma, dma((2 * X,)), dma, dma((2 * X,)),
            dma((2,)), dma((2,)), dma, dma, dma, dma,
            dma((2,)), dma((2,)),
        ],
        compiler_params=pltpu.CompilerParams(
            collective_id=0, has_side_effects=True, vmem_limit_bytes=60 * 1024 * 1024
        ),
        cost_estimate=pl.CostEstimate(flops=2 * 2 * 512 * 1024 * 256, bytes_accessed=6 * 1024 * 1024, transcendentals=0),
    )(fock, density, intersection, fock_mask, density_mask, intersection_mask, product_filter)


def solution(mesh):
    spec = P("row", "col")
    return jax.shard_map(
        per_device, mesh=mesh, in_specs=(spec,) * 7, out_specs=spec, check_vma=False
    )
```

```python
import jax
import jax.numpy as jnp
from jax import lax
from jax.experimental import pallas as pl
from jax.experimental.pallas import tpu as pltpu
from jax.sharding import PartitionSpec as P

MESH = pl.DeviceIdType.MESH
Z, Y, J = 4, 8, 4
X = 4
BF16, F32 = jnp.bfloat16, jnp.float32
FAR = F32


def masked(block, mask_ref):
    lane = lax.broadcasted_iota(jnp.int32, block.shape, 1)
    keep = jnp.where(lane < block.shape[1] // 2, mask_ref[0, 0], mask_ref[0, 1])
    return (block.astype(F32) * keep.astype(F32)).astype(BF16)


def kernel(
    f_hbm, p_hbm, s_hbm, fm_hbm, pm_hbm, sm_hbm, filt_hbm, out_ref,
    f_ref, p_ref, s_ref, fm_ref, pm_ref, sm_ref, filt_ref, in_sem,
    f_send, f_all, k_all, p_all, s_all, filt_send, filt_here,
    part, near_in, far_send, far_in, total, part_send, part2_in, own_in, tile_send, tile_in,
    t_send_sem, t_recv_sem,
    p_send_sem, p_recv_sem, p_over_sem, p_core_sem, p_mate_sem,
    s_send_sem, s_recv_sem, s_over_sem, s_core_sem, s_mate_sem,
    f_send_sem, f_recv_sem, k_send_sem, k_recv_sem,
    a_send_sem, a_recv_sem, b_send_sem, b_recv_sem, o_send_sem, o_recv_sem, x_send_sem, x_recv_sem,
):
    r, c = lax.axis_index("row"), lax.axis_index("col")
    zh, y = lax.div(r, Y), lax.rem(r, Y)
    zl, x, core = lax.div(c, 2 * X), lax.rem(lax.div(c, 2), X), lax.rem(c, 2)
    over = (r, c + 1 - 2 * core)
    low = lax.rem(zh, 2)
    pair = zh + 1 - 2 * low
    mate = Z - 1 - zh
    half = lax.rem(lax.div(zh, 2) + low, 2)
    x_high = lax.div(x, 2)
    home = lax.rem(zl + x_high, 2) == half
    away = lax.rem(zl + x_high, 2) != half
    home_row = jnp.where(home, r, pair * Y + y)
    ahead = jnp.where(core == 0, 1, X - 1)

    def holder(l, k):
        return lax.rem(zl + l, 2) * (2 * X) + x * 2 + k

    def slot_of(z_low, at):
        return X * lax.rem(z_low + lax.div(at, 2) + half, 2) + at

    held_z = 2 * lax.div(zh, 2) + core
    held_zl = lax.rem(x_high + half, 2)
    held_l = lax.rem(zl + held_zl, 2)
    held_from = (held_z * Y + y, held_zl * (2 * X) + x * 2 + held_l)
    term_col = held_zl * (2 * X) + x * 2 + core
    move_to = (home_row, holder(core, low))
    stays = jnp.logical_and(home, jnp.logical_and(core == 0, low == 0))
    moved = jnp.logical_not(stays)
    mine = low == core
    not_mine = low != core

    def ring(d):
        return zh * Y + lax.rem(y + d, Y)

    def on_line(dz, dx):
        return lax.rem(zl + dz, 2) * (2 * X) + lax.rem(x + dx, X) * 2 + core

    def tile_to(b):
        return (2 * c + b, lax.div(r, 2))

    def off_diagonal(b):
        return r != 2 * c + b

    def copy(src, dst, send, recv, to):
        return pltpu.make_async_remote_copy(
            src_ref=src, dst_ref=dst, send_sem=send, recv_sem=recv, device_id=to, device_id_type=MESH
        )

    def await_sent(ref, sem):
        copy(ref, ref, sem, sem, over).wait_send()

    def await_recv(ref, sem):
        copy(ref, ref, sem, sem, over).wait_recv()

    fetches = []
    for n, (src, dst) in enumerate((
        (f_hbm, f_ref), (fm_hbm, fm_ref), (p_hbm, p_ref), (pm_hbm, pm_ref),
        (filt_hbm, filt_ref), (s_hbm, s_ref), (sm_hbm, sm_ref),
    )):
        fetches.append(pltpu.make_async_copy(src, dst, in_sem.at[n]))
        fetches[-1].start()

    barrier = pltpu.get_barrier_semaphore()

    def greet(to):
        pl.semaphore_signal(barrier, inc=1, device_id=to, device_id_type=MESH)

    @pl.when(moved)
    def _():
        greet(held_from)

    greet((mate * Y + y, c))
    for d in (2, 6, 1, 7):
        greet((ring(d), c))
    for dz, dx in ((1, 0), (0, 1), (0, X - 1)):
        greet((r, on_line(dz, dx)))
    greet(over)
    greet((pair * Y + y, term_col))

    @pl.when(away)
    def _():
        greet((r, term_col))

    for one in fetches[:5]:
        one.wait()
    f_send[...] = masked(f_ref[...], fm_ref)
    p_all[core, y, low] = masked(p_ref[...], pm_ref)
    lane = lax.broadcasted_iota(jnp.int32, filt_send.shape, 1)
    filt_send[...] = jnp.where(lane < 128, filt_ref[0, 0], filt_ref[0, 1]).astype(F32)

    pl.semaphore_wait(barrier, jnp.where(moved, 1, 0) + 1 + 4 + 3 + 1 + 1 + jnp.where(away, 1, 0))

    my_slot = slot_of(zl, x)
    f_move = copy(f_send, f_all.at[X * core + x], t_send_sem.at[0], t_recv_sem.at[0], move_to)
    filt_move = copy(filt_send, filt_here, t_send_sem.at[1], t_recv_sem.at[1], move_to)

    @pl.when(moved)
    def _():
        f_move.start()
        filt_move.start()

    def mate_copy(buf, sem, t):
        ref = buf.at[core, y, t]
        return copy(ref, ref, sem.at[0], sem.at[1], (mate * Y + y, c))

    def ring_ref(buf, sems, src, t, part_of):
        slot = lax.rem(y + src, Y)
        at = Y + part_of if part_of is not None else slot
        if t is None:
            ref = buf.at[core, slot] if part_of is None else buf.at[core, slot, part_of]
            return ref, sems[1].at[0, at]
        ref = buf.at[core, slot, t] if part_of is None else buf.at[core, slot, t, pl.ds(64 * part_of, 64)]
        return ref, sems[1].at[t, at]

    def ring_send(buf, sems, src, t, d, part_of=None):
        ref, recv = ring_ref(buf, sems, src, t, part_of)
        copy(ref, ref, sems[0], recv, (ring(d), c)).start()

    def ring_wait(buf, sems, src, t, part_of=None):
        await_recv(*ring_ref(buf, sems, src, t, part_of))

    def ring_start(buf, sems, t, to=(2, 6, 1, 7)):
        for d in to:
            ring_send(buf, sems, 0, t, d)

    def ring_pass(buf, sems, t):
        for src, on in ((7, 1), (1, 7)):
            ring_wait(buf, sems, src, t)
            ring_send(buf, sems, src, t, on)

    def ring_relay(buf, sems, t):
        for src, on, far, part_of in ((6, 1, 2, 0), (2, 7, 6, 1)):
            ring_wait(buf, sems, src, t)
            ring_send(buf, sems, src, t, on)
            ring_send(buf, sems, src, t, far, part_of)

    def cross(buf, sems, src):
        at = lax.rem(y + src, Y)
        ref = buf.at[core, at]
        copy(ref, ref, sems[2], sems[3].at[at], over).start()

    def cross_wait(buf, sems, src):
        at = lax.rem(y + src, Y)
        await_recv(buf.at[1 - core, at], sems[3].at[at])

    def ring_last(buf, sems, ts, src):
        for t in ts:
            for part_of in range(2) if src == 4 else (None,):
                ring_wait(buf, sems, src, t, part_of)
        cross(buf, sems, src)

    p_sems = (p_send_sem, p_recv_sem, p_over_sem, p_core_sem)
    s_sems = (s_send_sem, s_recv_sem, s_over_sem, s_core_sem)
    mate_copy(p_all, p_mate_sem, low).start()
    ring_start(p_all, p_sems, low)

    def line_send(buf, sems, dz, dx, to):
        slot = slot_of(lax.rem(zl + dz, 2), lax.rem(x + dx, X))
        ref = buf.at[slot]
        copy(ref, ref, sems[0], sems[1].at[slot], (r, to)).start()

    def line_wait(buf, sems, dz, dx):
        slot = slot_of(lax.rem(zl + dz, 2), lax.rem(x + dx, X))
        await_recv(buf.at[slot], sems[1].at[slot])

    def line_start(buf, sems):
        for to in (on_line(1, 0), on_line(0, ahead), on_line(0, X - ahead)):
            line_send(buf, sems, 0, 0, to)

    def line_relay(buf, sems):
        line_wait(buf, sems, 1, 0)
        line_send(buf, sems, 1, 0, on_line(0, 1))
        line_send(buf, sems, 1, 0, on_line(0, X - 1))
        line_wait(buf, sems, 0, X - ahead)
        line_send(buf, sems, 0, X - ahead, on_line(0, ahead))
        line_send(buf, sems, 0, X - ahead, on_line(1, ahead))

    def line_finish(buf, sems):
        for dz, dx in ((0, ahead), (1, 1), (1, X - 1), (0, 2), (1, 2)):
            line_wait(buf, sems, dz, dx)

    f_sems, k_sems = (f_send_sem, f_recv_sem), (k_send_sem, k_recv_sem)
    mate_copy(p_all, p_mate_sem, 1 - low).wait_recv()
    ring_start(p_all, p_sems, 1 - low)

    @pl.when(moved)
    def _():
        await_recv(f_all.at[my_slot], t_recv_sem.at[0])

    @pl.when(stays)
    def _():
        f_all[my_slot] = f_send[...]

    line_start(f_all, f_sems)
    cross(p_all, p_sems, 0)

    for one in fetches[5:]:
        one.wait()
    s_all[core, y, low] = masked(s_ref[...], sm_ref)
    mate_copy(s_all, s_mate_sem, low).start()

    ring_relay(p_all, p_sems, low)
    line_relay(f_all, f_sems)
    ring_relay(p_all, p_sems, 1 - low)
    cross(p_all, p_sems, 2)
    cross(p_all, p_sems, 6)
    line_finish(f_all, f_sems)

    def at_place(b, src):
        place = lax.rem(y + src, Y)
        j = lax.div(place, 2)
        lanes = pl.ds(pl.multiple_of(128 * lax.rem(place, 2), 128), 128)
        total = None
        for t in range(2):
            rows = f_all[X * lax.rem(j, 2) + 2 * t + lax.div(j, 2), :, lanes]
            term = jnp.dot(rows, p_all[b, place, t], preferred_element_type=F32)
            total = term if total is None else total + term
        return total

    def near_copy():
        return copy(part, near_in, a_send_sem.at[0], a_recv_sem.at[0], (r, holder(1, core)))

    def send_first(b, term):
        @pl.when(away)
        def _():
            far_send[b] = term.astype(FAR)
            copy(
                far_send.at[b], far_in, a_send_sem.at[1], a_recv_sem.at[1], (pair * Y + y, holder(b, core))
            ).start()

        @pl.when(jnp.logical_and(home, b == 0))
        def _():
            near_in[...] = term

        @pl.when(jnp.logical_and(home, b == 1))
        def _():
            part[...] = term
            near_copy().start()

    term = at_place(core, 0) + at_place(core, 2) + at_place(core, 6)
    for src in (1, 7, 5, 3, 4):
        ring_last(p_all, p_sems, (low, 1 - low), src)
        term = term + at_place(core, src)
    mate_copy(s_all, s_mate_sem, 1 - low).wait_recv()
    ring_start(s_all, s_sems, None, (1, 7))
    send_first(core, term)
    cross(s_all, s_sems, 0)

    term = None
    for src in (0, 2, 6, 1, 7, 5, 3, 4):
        cross_wait(p_all, p_sems, src)
        one = at_place(1 - core, src)
        term = one if term is None else term + one
    send_first(1 - core, term)

    @pl.when(moved)
    def _():
        filt_move.wait_recv()

    @pl.when(stays)
    def _():
        filt_here[...] = filt_send[...]

    ring_pass(s_all, s_sems, None)
    cross(s_all, s_sems, 1)
    cross(s_all, s_sems, 7)

    @pl.when(away)
    def _():
        await_recv(near_in, a_recv_sem.at[0])

    await_recv(far_in, a_recv_sem.at[1])
    k_all[my_slot] = ((near_in[...] + far_in[...].astype(F32)) * filt_here[0:1, :]).astype(BF16)
    line_start(k_all, k_sems)
    ring_relay(s_all, s_sems, None)
    line_relay(k_all, k_sems)
    cross(s_all, s_sems, 2)
    cross(s_all, s_sems, 6)
    for src in (5, 3, 4):
        ring_last(s_all, s_sems, (None,), src)
    for src in range(Y):
        cross_wait(s_all, s_sems, src)

    def by_block(dz, dx):
        at = lax.rem(x + dx, X)
        slot = slot_of(lax.rem(zl + dz, 2), at)
        t, j = lax.div(at, 2), 2 * lax.rem(at, 2) + lax.div(slot, X)
        rows = k_all[slot]
        for b in range(2):
            depth = jnp.concatenate([s_all[b, 2 * j, t], s_all[b, 2 * j + 1, t]], axis=0)
            total[b] += jnp.dot(rows, depth, preferred_element_type=F32)

    total[...] = jnp.zeros_like(total)
    for dz, dx in ((0, 0), (1, 0), (0, X - ahead)):
        by_block(dz, dx)
    for dz, dx in ((0, ahead), (1, 1), (1, X - 1), (0, 2), (1, 2)):
        line_wait(k_all, k_sems, dz, dx)
        by_block(dz, dx)

    own_copy = copy(total.at[1 - core], own_in, o_send_sem, o_recv_sem, over)

    @pl.when(mine)
    def _():
        own_copy.start()
        own_in[...] = total[core]

    @pl.when(not_mine)
    def _():
        for b in range(2):
            part_send[b] = total[b].astype(BF16)
            copy(part_send.at[b], part2_in, b_send_sem, b_recv_sem, (pair * Y + y, c - core + b)).start()

    @pl.when(moved)
    def _():
        f_move.wait_send()
        filt_move.wait_send()

    mate_copy(p_all, p_mate_sem, low).wait_send()
    mate_copy(s_all, s_mate_sem, low).wait_send()
    await_sent(p_all.at[0, pl.ds(0, Y - 1)], p_send_sem)
    await_sent(s_all.at[0, pl.ds(0, Y - 1)], s_send_sem)
    await_sent(p_all.at[0], p_over_sem)
    await_sent(s_all.at[0], s_over_sem)
    await_sent(f_all.at[pl.ds(0, 2 * X - 1)], f_send_sem)
    await_sent(k_all.at[pl.ds(0, 2 * X - 1)], k_send_sem)

    @pl.when(away)
    def _():
        await_sent(far_send, a_send_sem.at[1])

    @pl.when(home)
    def _():
        near_copy().wait_send()

    def x_copy(b):
        at = lax.rem(r, 2)
        return copy(tile_send.at[b], tile_in.at[at], x_send_sem.at[b], x_recv_sem.at[at], tile_to(b))

    @pl.when(not_mine)
    def _():
        await_recv(own_in, o_recv_sem)

    await_recv(part2_in, b_recv_sem)
    rounded = (own_in[...] + part2_in[...].astype(F32)).astype(BF16)
    for b in range(2):
        tile_send[b] = rounded[:, 128 * b : 128 * (b + 1)]

        @pl.when(off_diagonal(b))
        def _():
            x_copy(b).start()

        @pl.when(jnp.logical_not(off_diagonal(b)))
        def _():
            tile_in[b] = tile_send[b]

    wide = rounded.astype(F32)

    @pl.when(mine)
    def _():
        own_copy.wait_send()

    @pl.when(not_mine)
    def _():
        await_sent(part_send, b_send_sem)

    for b in range(2):
        here = slice(128 * b, 128 * (b + 1))

        @pl.when(off_diagonal(b))
        def _():
            await_recv(tile_in.at[b], x_recv_sem.at[b])

        out_ref[:, here] = wide[:, here] - tile_in[b].astype(F32).T

    for b in range(2):

        @pl.when(off_diagonal(b))
        def _():
            x_copy(b).wait_send()


def per_device(fock, density, intersection, fock_mask, density_mask, intersection_mask, product_filter):
    hbm = pl.BlockSpec(memory_space=pltpu.HBM)
    vmem = pl.BlockSpec(memory_space=pltpu.VMEM)
    dma = pltpu.SemaphoreType.DMA
    block = (128, 256)
    return pl.pallas_call(
        kernel,
        out_shape=jax.ShapeDtypeStruct(block, F32),
        in_specs=[hbm] * 7,
        out_specs=vmem,
        scratch_shapes=[pltpu.VMEM(block, BF16)] * 3
        + [pltpu.SMEM((1, 2), jnp.int32)] * 4
        + [
            dma((7,)),
            pltpu.VMEM(block, BF16),
            pltpu.VMEM((2 * X,) + block, BF16),
            pltpu.VMEM((2 * X,) + block, BF16),
            pltpu.VMEM((2, Y, 2) + block, BF16),
            pltpu.VMEM((2, Y, 2) + block, BF16),
            pltpu.VMEM((8, 256), F32),
            pltpu.VMEM((8, 256), F32),
            pltpu.VMEM(block, F32),
            pltpu.VMEM(block, F32),
            pltpu.VMEM((2,) + block, FAR),
            pltpu.VMEM(block, FAR),
            pltpu.VMEM((2,) + block, F32),
            pltpu.VMEM((2,) + block, BF16),
            pltpu.VMEM(block, BF16),
            pltpu.VMEM(block, F32),
            pltpu.VMEM((2, 128, 128), BF16),
            pltpu.VMEM((2, 128, 128), BF16),
            dma((2,)), dma((2,)),
            dma, dma((2, Y + 2)), dma, dma((Y,)), dma((2,)),
            dma, dma((2, Y + 2)), dma, dma((Y,)), dma((2,)),
            dma, dma((2 * X,)), dma, dma((2 * X,)),
            dma((2,)), dma((2,)), dma, dma, dma, dma,
            dma((2,)), dma((2,)),
        ],
        compiler_params=pltpu.CompilerParams(
            collective_id=0, has_side_effects=True, vmem_limit_bytes=60 * 1024 * 1024
        ),
        cost_estimate=pl.CostEstimate(flops=2 * 2 * 512 * 1024 * 256, bytes_accessed=6 * 1024 * 1024, transcendentals=0),
    )(fock, density, intersection, fock_mask, density_mask, intersection_mask, product_filter)


def solution(mesh):
    spec = P("row", "col")
    return jax.shard_map(
        per_device, mesh=mesh, in_specs=(spec,) * 7, out_specs=spec, check_vma=False
    )
```

```python
import jax
import jax.numpy as jnp
from jax import lax
from jax.experimental import pallas as pl
from jax.experimental.pallas import tpu as pltpu
from jax.sharding import PartitionSpec as P

MESH = pl.DeviceIdType.MESH
Z, Y, J = 4, 8, 4
X = 4
BF16, F32 = jnp.bfloat16, jnp.float32
FAR = F32


def masked(block, mask_ref):
    lane = lax.broadcasted_iota(jnp.int32, block.shape, 1)
    keep = jnp.where(lane < block.shape[1] // 2, mask_ref[0, 0], mask_ref[0, 1])
    return (block.astype(F32) * keep.astype(F32)).astype(BF16)


def kernel(
    f_hbm, p_hbm, s_hbm, fm_hbm, pm_hbm, sm_hbm, filt_hbm, out_ref,
    f_ref, p_ref, s_ref, fm_ref, pm_ref, sm_ref, filt_ref, in_sem,
    f_send, f_all, k_all, p_all, s_all, filt_send, filt_here,
    part, near_in, far_send, far_in, total, part_send, part2_in, own_in, tile_send, tile_in,
    t_send_sem, t_recv_sem,
    p_send_sem, p_recv_sem, p_over_sem, p_core_sem, p_mate_sem,
    s_send_sem, s_recv_sem, s_over_sem, s_core_sem, s_mate_sem,
    f_send_sem, f_recv_sem, k_send_sem, k_recv_sem,
    a_send_sem, a_recv_sem, b_send_sem, b_recv_sem, o_send_sem, o_recv_sem, x_send_sem, x_recv_sem,
):
    r, c = lax.axis_index("row"), lax.axis_index("col")
    zh, y = lax.div(r, Y), lax.rem(r, Y)
    zl, x, core = lax.div(c, 2 * X), lax.rem(lax.div(c, 2), X), lax.rem(c, 2)
    over = (r, c + 1 - 2 * core)
    low = lax.rem(zh, 2)
    pair = zh + 1 - 2 * low
    mate = Z - 1 - zh
    half = lax.rem(lax.div(zh, 2) + low, 2)
    x_high = lax.div(x, 2)
    home = lax.rem(zl + x_high, 2) == half
    away = lax.rem(zl + x_high, 2) != half
    home_row = jnp.where(home, r, pair * Y + y)
    ahead = jnp.where(core == 0, 1, X - 1)

    def holder(l, k):
        return lax.rem(zl + l, 2) * (2 * X) + x * 2 + k

    def slot_of(z_low, at):
        return X * lax.rem(z_low + lax.div(at, 2) + half, 2) + at

    held_z = 2 * lax.div(zh, 2) + core
    held_zl = lax.rem(x_high + half, 2)
    held_l = lax.rem(zl + held_zl, 2)
    held_from = (held_z * Y + y, held_zl * (2 * X) + x * 2 + held_l)
    term_col = held_zl * (2 * X) + x * 2 + core
    move_to = (home_row, holder(core, low))
    stays = jnp.logical_and(home, jnp.logical_and(core == 0, low == 0))
    moved = jnp.logical_not(stays)
    mine = low == core
    not_mine = low != core

    def ring(d):
        return zh * Y + lax.rem(y + d, Y)

    def on_line(dz, dx):
        return lax.rem(zl + dz, 2) * (2 * X) + lax.rem(x + dx, X) * 2 + core

    def tile_to(b):
        return (2 * c + b, lax.div(r, 2))

    def off_diagonal(b):
        return r != 2 * c + b

    def copy(src, dst, send, recv, to):
        return pltpu.make_async_remote_copy(
            src_ref=src, dst_ref=dst, send_sem=send, recv_sem=recv, device_id=to, device_id_type=MESH
        )

    def await_sent(ref, sem):
        copy(ref, ref, sem, sem, over).wait_send()

    def await_recv(ref, sem):
        copy(ref, ref, sem, sem, over).wait_recv()

    fetches = []
    for n, (src, dst) in enumerate((
        (f_hbm, f_ref), (fm_hbm, fm_ref), (p_hbm, p_ref), (pm_hbm, pm_ref),
        (filt_hbm, filt_ref), (s_hbm, s_ref), (sm_hbm, sm_ref),
    )):
        fetches.append(pltpu.make_async_copy(src, dst, in_sem.at[n]))
        fetches[-1].start()

    barrier = pltpu.get_barrier_semaphore()

    def greet(to):
        pl.semaphore_signal(barrier, inc=1, device_id=to, device_id_type=MESH)

    @pl.when(moved)
    def _():
        greet(held_from)

    greet((mate * Y + y, c))
    for d in (2, 6, 1, 7):
        greet((ring(d), c))
    for dz, dx in ((1, 0), (0, 1), (0, X - 1)):
        greet((r, on_line(dz, dx)))
    greet(over)
    greet((pair * Y + y, term_col))

    @pl.when(away)
    def _():
        greet((r, term_col))

    for one in fetches[:5]:
        one.wait()
    f_send[...] = masked(f_ref[...], fm_ref)
    p_all[core, y, low] = masked(p_ref[...], pm_ref)
    lane = lax.broadcasted_iota(jnp.int32, filt_send.shape, 1)
    filt_send[...] = jnp.where(lane < 128, filt_ref[0, 0], filt_ref[0, 1]).astype(F32)

    pl.semaphore_wait(barrier, jnp.where(moved, 1, 0) + 1 + 4 + 3 + 1 + 1 + jnp.where(away, 1, 0))

    my_slot = slot_of(zl, x)
    f_move = copy(f_send, f_all.at[X * core + x], t_send_sem.at[0], t_recv_sem.at[0], move_to)
    filt_move = copy(filt_send, filt_here, t_send_sem.at[1], t_recv_sem.at[1], move_to)

    @pl.when(moved)
    def _():
        f_move.start()
        filt_move.start()

    def mate_copy(buf, sem, t):
        ref = buf.at[core, y, t]
        return copy(ref, ref, sem.at[0], sem.at[1], (mate * Y + y, c))

    def ring_ref(buf, sems, src, t, part_of):
        slot = lax.rem(y + src, Y)
        at = Y + part_of if part_of is not None else slot
        if t is None:
            ref = buf.at[core, slot] if part_of is None else buf.at[core, slot, part_of]
            return ref, sems[1].at[0, at]
        ref = buf.at[core, slot, t] if part_of is None else buf.at[core, slot, t, pl.ds(64 * part_of, 64)]
        return ref, sems[1].at[t, at]

    def ring_send(buf, sems, src, t, d, part_of=None):
        ref, recv = ring_ref(buf, sems, src, t, part_of)
        copy(ref, ref, sems[0], recv, (ring(d), c)).start()

    def ring_wait(buf, sems, src, t, part_of=None):
        await_recv(*ring_ref(buf, sems, src, t, part_of))

    def ring_start(buf, sems, t, to=(2, 6, 1, 7)):
        for d in to:
            ring_send(buf, sems, 0, t, d)

    def ring_pass(buf, sems, t):
        for src, on in ((7, 1), (1, 7)):
            ring_wait(buf, sems, src, t)
            ring_send(buf, sems, src, t, on)

    def ring_relay(buf, sems, t):
        for src, on, far, part_of in ((6, 1, 2, 0), (2, 7, 6, 1)):
            ring_wait(buf, sems, src, t)
            ring_send(buf, sems, src, t, on)
            ring_send(buf, sems, src, t, far, part_of)

    def cross(buf, sems, src):
        at = lax.rem(y + src, Y)
        ref = buf.at[core, at]
        copy(ref, ref, sems[2], sems[3].at[at], over).start()

    def cross_wait(buf, sems, src):
        at = lax.rem(y + src, Y)
        await_recv(buf.at[1 - core, at], sems[3].at[at])

    def ring_last(buf, sems, ts, src):
        for t in ts:
            for part_of in range(2) if src == 4 else (None,):
                ring_wait(buf, sems, src, t, part_of)
        cross(buf, sems, src)

    p_sems = (p_send_sem, p_recv_sem, p_over_sem, p_core_sem)
    s_sems = (s_send_sem, s_recv_sem, s_over_sem, s_core_sem)
    mate_copy(p_all, p_mate_sem, low).start()
    ring_start(p_all, p_sems, low)

    def line_send(buf, sems, dz, dx, to):
        slot = slot_of(lax.rem(zl + dz, 2), lax.rem(x + dx, X))
        ref = buf.at[slot]
        copy(ref, ref, sems[0], sems[1].at[slot], (r, to)).start()

    def line_wait(buf, sems, dz, dx):
        slot = slot_of(lax.rem(zl + dz, 2), lax.rem(x + dx, X))
        await_recv(buf.at[slot], sems[1].at[slot])

    def line_start(buf, sems):
        for to in (on_line(1, 0), on_line(0, ahead), on_line(0, X - ahead)):
            line_send(buf, sems, 0, 0, to)

    def line_relay(buf, sems):
        line_wait(buf, sems, 1, 0)
        line_send(buf, sems, 1, 0, on_line(0, 1))
        line_send(buf, sems, 1, 0, on_line(0, X - 1))
        line_wait(buf, sems, 0, X - ahead)
        line_send(buf, sems, 0, X - ahead, on_line(0, ahead))
        line_send(buf, sems, 0, X - ahead, on_line(1, ahead))

    def line_finish(buf, sems):
        for dz, dx in ((0, ahead), (1, 1), (1, X - 1), (0, 2), (1, 2)):
            line_wait(buf, sems, dz, dx)

    f_sems, k_sems = (f_send_sem, f_recv_sem), (k_send_sem, k_recv_sem)
    mate_copy(p_all, p_mate_sem, 1 - low).wait_recv()
    ring_start(p_all, p_sems, 1 - low)

    @pl.when(moved)
    def _():
        await_recv(f_all.at[my_slot], t_recv_sem.at[0])

    @pl.when(stays)
    def _():
        f_all[my_slot] = f_send[...]

    line_start(f_all, f_sems)
    cross(p_all, p_sems, 0)

    for one in fetches[5:]:
        one.wait()
    s_all[core, y, low] = masked(s_ref[...], sm_ref)
    mate_copy(s_all, s_mate_sem, low).start()

    ring_relay(p_all, p_sems, low)
    line_relay(f_all, f_sems)
    ring_relay(p_all, p_sems, 1 - low)
    cross(p_all, p_sems, 2)
    cross(p_all, p_sems, 6)
    mate_copy(s_all, s_mate_sem, 1 - low).wait_recv()
    ring_start(s_all, s_sems, None, (1, 7))
    line_finish(f_all, f_sems)

    def at_place(b, src):
        place = lax.rem(y + src, Y)
        j = lax.div(place, 2)
        lanes = pl.ds(pl.multiple_of(128 * lax.rem(place, 2), 128), 128)
        total = None
        for t in range(2):
            rows = f_all[X * lax.rem(j, 2) + 2 * t + lax.div(j, 2), :, lanes]
            term = jnp.dot(rows, p_all[b, place, t], preferred_element_type=F32)
            total = term if total is None else total + term
        return total

    def near_copy():
        return copy(part, near_in, a_send_sem.at[0], a_recv_sem.at[0], (r, holder(1, core)))

    def send_first(b, term):
        @pl.when(away)
        def _():
            far_send[b] = term.astype(FAR)
            copy(
                far_send.at[b], far_in, a_send_sem.at[1], a_recv_sem.at[1], (pair * Y + y, holder(b, core))
            ).start()

        @pl.when(jnp.logical_and(home, b == 0))
        def _():
            near_in[...] = term

        @pl.when(jnp.logical_and(home, b == 1))
        def _():
            part[...] = term
            near_copy().start()

    term = at_place(core, 0) + at_place(core, 2) + at_place(core, 6)
    for src in (1, 7, 5, 3, 4):
        ring_last(p_all, p_sems, (low, 1 - low), src)
        term = term + at_place(core, src)
    send_first(core, term)
    ring_pass(s_all, s_sems, None)

    term = None
    for src in (0, 2, 6, 1, 7, 5, 3, 4):
        cross_wait(p_all, p_sems, src)
        one = at_place(1 - core, src)
        term = one if term is None else term + one
    send_first(1 - core, term)

    @pl.when(moved)
    def _():
        filt_move.wait_recv()

    @pl.when(stays)
    def _():
        filt_here[...] = filt_send[...]

    ring_relay(s_all, s_sems, None)
    for src in (0, 1, 7, 2, 6):
        cross(s_all, s_sems, src)

    @pl.when(away)
    def _():
        await_recv(near_in, a_recv_sem.at[0])

    await_recv(far_in, a_recv_sem.at[1])
    k_all[my_slot] = ((near_in[...] + far_in[...].astype(F32)) * filt_here[0:1, :]).astype(BF16)
    line_start(k_all, k_sems)
    line_relay(k_all, k_sems)
    for src in (5, 3, 4):
        ring_last(s_all, s_sems, (None,), src)
    for src in range(Y):
        cross_wait(s_all, s_sems, src)

    def by_block(dz, dx):
        at = lax.rem(x + dx, X)
        slot = slot_of(lax.rem(zl + dz, 2), at)
        t, j = lax.div(at, 2), 2 * lax.rem(at, 2) + lax.div(slot, X)
        rows = k_all[slot]
        for b in range(2):
            depth = jnp.concatenate([s_all[b, 2 * j, t], s_all[b, 2 * j + 1, t]], axis=0)
            total[b] += jnp.dot(rows, depth, preferred_element_type=F32)

    total[...] = jnp.zeros_like(total)
    for dz, dx in ((0, 0), (1, 0), (0, X - ahead)):
        by_block(dz, dx)
    for dz, dx in ((0, ahead), (1, 1), (1, X - 1), (0, 2), (1, 2)):
        line_wait(k_all, k_sems, dz, dx)
        by_block(dz, dx)

    own_copy = copy(total.at[1 - core], own_in, o_send_sem, o_recv_sem, over)

    @pl.when(mine)
    def _():
        own_copy.start()
        own_in[...] = total[core]

    @pl.when(not_mine)
    def _():
        for b in range(2):
            part_send[b] = total[b].astype(BF16)
            copy(part_send.at[b], part2_in, b_send_sem, b_recv_sem, (pair * Y + y, c - core + b)).start()

    @pl.when(moved)
    def _():
        f_move.wait_send()
        filt_move.wait_send()

    mate_copy(p_all, p_mate_sem, low).wait_send()
    mate_copy(s_all, s_mate_sem, low).wait_send()
    await_sent(p_all.at[0, pl.ds(0, Y - 1)], p_send_sem)
    await_sent(s_all.at[0, pl.ds(0, Y - 1)], s_send_sem)
    await_sent(p_all.at[0], p_over_sem)
    await_sent(s_all.at[0], s_over_sem)
    await_sent(f_all.at[pl.ds(0, 2 * X - 1)], f_send_sem)
    await_sent(k_all.at[pl.ds(0, 2 * X - 1)], k_send_sem)

    @pl.when(away)
    def _():
        await_sent(far_send, a_send_sem.at[1])

    @pl.when(home)
    def _():
        near_copy().wait_send()

    def x_copy(b):
        at = lax.rem(r, 2)
        return copy(tile_send.at[b], tile_in.at[at], x_send_sem.at[b], x_recv_sem.at[at], tile_to(b))

    @pl.when(not_mine)
    def _():
        await_recv(own_in, o_recv_sem)

    await_recv(part2_in, b_recv_sem)
    rounded = (own_in[...] + part2_in[...].astype(F32)).astype(BF16)
    for b in range(2):
        tile_send[b] = rounded[:, 128 * b : 128 * (b + 1)]

        @pl.when(off_diagonal(b))
        def _():
            x_copy(b).start()

        @pl.when(jnp.logical_not(off_diagonal(b)))
        def _():
            tile_in[b] = tile_send[b]

    wide = rounded.astype(F32)

    @pl.when(mine)
    def _():
        own_copy.wait_send()

    @pl.when(not_mine)
    def _():
        await_sent(part_send, b_send_sem)

    for b in range(2):
        here = slice(128 * b, 128 * (b + 1))

        @pl.when(off_diagonal(b))
        def _():
            await_recv(tile_in.at[b], x_recv_sem.at[b])

        out_ref[:, here] = wide[:, here] - tile_in[b].astype(F32).T

    for b in range(2):

        @pl.when(off_diagonal(b))
        def _():
            x_copy(b).wait_send()


def per_device(fock, density, intersection, fock_mask, density_mask, intersection_mask, product_filter):
    hbm = pl.BlockSpec(memory_space=pltpu.HBM)
    vmem = pl.BlockSpec(memory_space=pltpu.VMEM)
    dma = pltpu.SemaphoreType.DMA
    block = (128, 256)
    return pl.pallas_call(
        kernel,
        out_shape=jax.ShapeDtypeStruct(block, F32),
        in_specs=[hbm] * 7,
        out_specs=vmem,
        scratch_shapes=[pltpu.VMEM(block, BF16)] * 3
        + [pltpu.SMEM((1, 2), jnp.int32)] * 4
        + [
            dma((7,)),
            pltpu.VMEM(block, BF16),
            pltpu.VMEM((2 * X,) + block, BF16),
            pltpu.VMEM((2 * X,) + block, BF16),
            pltpu.VMEM((2, Y, 2) + block, BF16),
            pltpu.VMEM((2, Y, 2) + block, BF16),
            pltpu.VMEM((8, 256), F32),
            pltpu.VMEM((8, 256), F32),
            pltpu.VMEM(block, F32),
            pltpu.VMEM(block, F32),
            pltpu.VMEM((2,) + block, FAR),
            pltpu.VMEM(block, FAR),
            pltpu.VMEM((2,) + block, F32),
            pltpu.VMEM((2,) + block, BF16),
            pltpu.VMEM(block, BF16),
            pltpu.VMEM(block, F32),
            pltpu.VMEM((2, 128, 128), BF16),
            pltpu.VMEM((2, 128, 128), BF16),
            dma((2,)), dma((2,)),
            dma, dma((2, Y + 2)), dma, dma((Y,)), dma((2,)),
            dma, dma((2, Y + 2)), dma, dma((Y,)), dma((2,)),
            dma, dma((2 * X,)), dma, dma((2 * X,)),
            dma((2,)), dma((2,)), dma, dma, dma, dma,
            dma((2,)), dma((2,)),
        ],
        compiler_params=pltpu.CompilerParams(
            collective_id=0, has_side_effects=True, vmem_limit_bytes=60 * 1024 * 1024
        ),
        cost_estimate=pl.CostEstimate(flops=2 * 2 * 512 * 1024 * 256, bytes_accessed=6 * 1024 * 1024, transcendentals=0),
    )(fock, density, intersection, fock_mask, density_mask, intersection_mask, product_filter)


def solution(mesh):
    spec = P("row", "col")
    return jax.shard_map(
        per_device, mesh=mesh, in_specs=(spec,) * 7, out_specs=spec, check_vma=False
    )
```

```python
import jax
import jax.numpy as jnp
from jax import lax
from jax.experimental import pallas as pl
from jax.experimental.pallas import tpu as pltpu
from jax.sharding import PartitionSpec as P

MESH = pl.DeviceIdType.MESH
Z, Y, J = 4, 8, 4
X = 4
BF16, F32 = jnp.bfloat16, jnp.float32
FAR = BF16


def masked(block, mask_ref):
    lane = lax.broadcasted_iota(jnp.int32, block.shape, 1)
    keep = jnp.where(lane < block.shape[1] // 2, mask_ref[0, 0], mask_ref[0, 1])
    return (block.astype(F32) * keep.astype(F32)).astype(BF16)


def kernel(
    f_hbm, p_hbm, s_hbm, fm_hbm, pm_hbm, sm_hbm, filt_hbm, out_ref,
    f_ref, p_ref, s_ref, fm_ref, pm_ref, sm_ref, filt_ref, in_sem,
    f_send, f_all, k_all, p_all, s_all, filt_send, filt_here,
    part, near_in, far_send, far_in, total, part_send, part2_in, own_in, tile_send, tile_in,
    t_send_sem, t_recv_sem,
    p_send_sem, p_recv_sem, p_over_sem, p_core_sem, p_mate_sem,
    s_send_sem, s_recv_sem, s_over_sem, s_core_sem, s_mate_sem,
    f_send_sem, f_recv_sem, k_send_sem, k_recv_sem,
    a_send_sem, a_recv_sem, b_send_sem, b_recv_sem, o_send_sem, o_recv_sem, x_send_sem, x_recv_sem,
):
    r, c = lax.axis_index("row"), lax.axis_index("col")
    zh, y = lax.div(r, Y), lax.rem(r, Y)
    zl, x, core = lax.div(c, 2 * X), lax.rem(lax.div(c, 2), X), lax.rem(c, 2)
    over = (r, c + 1 - 2 * core)
    low = lax.rem(zh, 2)
    pair = zh + 1 - 2 * low
    mate = Z - 1 - zh
    half = lax.rem(lax.div(zh, 2) + low, 2)
    x_high = lax.div(x, 2)
    home = lax.rem(zl + x_high, 2) == half
    away = lax.rem(zl + x_high, 2) != half
    home_row = jnp.where(home, r, pair * Y + y)
    ahead = jnp.where(core == 0, 1, X - 1)

    def holder(l, k):
        return lax.rem(zl + l, 2) * (2 * X) + x * 2 + k

    def slot_of(z_low, at):
        return X * lax.rem(z_low + lax.div(at, 2) + half, 2) + at

    held_z = 2 * lax.div(zh, 2) + core
    held_zl = lax.rem(x_high + half, 2)
    held_l = lax.rem(zl + held_zl, 2)
    held_from = (held_z * Y + y, held_zl * (2 * X) + x * 2 + held_l)
    term_col = held_zl * (2 * X) + x * 2 + core
    move_to = (home_row, holder(core, low))
    stays = jnp.logical_and(home, jnp.logical_and(core == 0, low == 0))
    moved = jnp.logical_not(stays)
    mine = low == core
    not_mine = low != core

    def ring(d):
        return zh * Y + lax.rem(y + d, Y)

    def on_line(dz, dx):
        return lax.rem(zl + dz, 2) * (2 * X) + lax.rem(x + dx, X) * 2 + core

    def tile_to(b):
        return (2 * c + b, lax.div(r, 2))

    def off_diagonal(b):
        return r != 2 * c + b

    def copy(src, dst, send, recv, to):
        return pltpu.make_async_remote_copy(
            src_ref=src, dst_ref=dst, send_sem=send, recv_sem=recv, device_id=to, device_id_type=MESH
        )

    def await_sent(ref, sem):
        copy(ref, ref, sem, sem, over).wait_send()

    def await_recv(ref, sem):
        copy(ref, ref, sem, sem, over).wait_recv()

    fetches = []
    for n, (src, dst) in enumerate((
        (f_hbm, f_ref), (fm_hbm, fm_ref), (p_hbm, p_ref), (pm_hbm, pm_ref),
        (filt_hbm, filt_ref), (s_hbm, s_ref), (sm_hbm, sm_ref),
    )):
        fetches.append(pltpu.make_async_copy(src, dst, in_sem.at[n]))
        fetches[-1].start()

    barrier = pltpu.get_barrier_semaphore()

    def greet(to):
        pl.semaphore_signal(barrier, inc=1, device_id=to, device_id_type=MESH)

    @pl.when(moved)
    def _():
        greet(held_from)

    greet((mate * Y + y, c))
    for d in (2, 6, 1, 7):
        greet((ring(d), c))
    for dz, dx in ((1, 0), (0, 1), (0, X - 1)):
        greet((r, on_line(dz, dx)))
    greet(over)
    greet((pair * Y + y, term_col))

    @pl.when(away)
    def _():
        greet((r, term_col))

    for one in fetches[:5]:
        one.wait()
    f_send[...] = masked(f_ref[...], fm_ref)
    p_all[core, y, low] = masked(p_ref[...], pm_ref)
    lane = lax.broadcasted_iota(jnp.int32, filt_send.shape, 1)
    filt_send[...] = jnp.where(lane < 128, filt_ref[0, 0], filt_ref[0, 1]).astype(F32)

    pl.semaphore_wait(barrier, jnp.where(moved, 1, 0) + 1 + 4 + 3 + 1 + 1 + jnp.where(away, 1, 0))

    my_slot = slot_of(zl, x)
    f_move = copy(f_send, f_all.at[X * core + x], t_send_sem.at[0], t_recv_sem.at[0], move_to)
    filt_move = copy(filt_send, filt_here, t_send_sem.at[1], t_recv_sem.at[1], move_to)

    @pl.when(moved)
    def _():
        f_move.start()
        filt_move.start()

    def mate_copy(buf, sem, t):
        ref = buf.at[core, y, t]
        return copy(ref, ref, sem.at[0], sem.at[1], (mate * Y + y, c))

    def ring_ref(buf, sems, src, t, part_of):
        slot = lax.rem(y + src, Y)
        at = Y + part_of if part_of is not None else slot
        if t is None:
            ref = buf.at[core, slot] if part_of is None else buf.at[core, slot, part_of]
            return ref, sems[1].at[0, at]
        ref = buf.at[core, slot, t] if part_of is None else buf.at[core, slot, t, pl.ds(64 * part_of, 64)]
        return ref, sems[1].at[t, at]

    def ring_send(buf, sems, src, t, d, part_of=None):
        ref, recv = ring_ref(buf, sems, src, t, part_of)
        copy(ref, ref, sems[0], recv, (ring(d), c)).start()

    def ring_wait(buf, sems, src, t, part_of=None):
        await_recv(*ring_ref(buf, sems, src, t, part_of))

    def ring_start(buf, sems, t, to=(2, 6, 1, 7)):
        for d in to:
            ring_send(buf, sems, 0, t, d)

    def ring_pass(buf, sems, t):
        for src, on in ((7, 1), (1, 7)):
            ring_wait(buf, sems, src, t)
            ring_send(buf, sems, src, t, on)

    def ring_relay(buf, sems, t):
        for src, on, far, part_of in ((6, 1, 2, 0), (2, 7, 6, 1)):
            ring_wait(buf, sems, src, t)
            ring_send(buf, sems, src, t, on)
            ring_send(buf, sems, src, t, far, part_of)

    def cross(buf, sems, src):
        at = lax.rem(y + src, Y)
        ref = buf.at[core, at]
        copy(ref, ref, sems[2], sems[3].at[at], over).start()

    def cross_wait(buf, sems, src):
        at = lax.rem(y + src, Y)
        await_recv(buf.at[1 - core, at], sems[3].at[at])

    def ring_last(buf, sems, ts, src):
        for t in ts:
            for part_of in range(2) if src == 4 else (None,):
                ring_wait(buf, sems, src, t, part_of)
        cross(buf, sems, src)

    p_sems = (p_send_sem, p_recv_sem, p_over_sem, p_core_sem)
    s_sems = (s_send_sem, s_recv_sem, s_over_sem, s_core_sem)
    mate_copy(p_all, p_mate_sem, low).start()
    ring_start(p_all, p_sems, low)

    def line_send(buf, sems, dz, dx, to):
        slot = slot_of(lax.rem(zl + dz, 2), lax.rem(x + dx, X))
        ref = buf.at[slot]
        copy(ref, ref, sems[0], sems[1].at[slot], (r, to)).start()

    def line_wait(buf, sems, dz, dx):
        slot = slot_of(lax.rem(zl + dz, 2), lax.rem(x + dx, X))
        await_recv(buf.at[slot], sems[1].at[slot])

    def line_start(buf, sems):
        for to in (on_line(1, 0), on_line(0, ahead), on_line(0, X - ahead)):
            line_send(buf, sems, 0, 0, to)

    def line_relay(buf, sems):
        line_wait(buf, sems, 1, 0)
        line_send(buf, sems, 1, 0, on_line(0, 1))
        line_send(buf, sems, 1, 0, on_line(0, X - 1))
        line_wait(buf, sems, 0, X - ahead)
        line_send(buf, sems, 0, X - ahead, on_line(0, ahead))
        line_send(buf, sems, 0, X - ahead, on_line(1, ahead))

    def line_finish(buf, sems):
        for dz, dx in ((0, ahead), (1, 1), (1, X - 1), (0, 2), (1, 2)):
            line_wait(buf, sems, dz, dx)

    f_sems, k_sems = (f_send_sem, f_recv_sem), (k_send_sem, k_recv_sem)
    mate_copy(p_all, p_mate_sem, 1 - low).wait_recv()
    ring_start(p_all, p_sems, 1 - low)

    @pl.when(moved)
    def _():
        await_recv(f_all.at[my_slot], t_recv_sem.at[0])

    @pl.when(stays)
    def _():
        f_all[my_slot] = f_send[...]

    line_start(f_all, f_sems)
    cross(p_all, p_sems, 0)

    for one in fetches[5:]:
        one.wait()
    s_all[core, y, low] = masked(s_ref[...], sm_ref)
    mate_copy(s_all, s_mate_sem, low).start()

    ring_relay(p_all, p_sems, low)
    line_relay(f_all, f_sems)
    ring_relay(p_all, p_sems, 1 - low)
    cross(p_all, p_sems, 2)
    cross(p_all, p_sems, 6)
    mate_copy(s_all, s_mate_sem, 1 - low).wait_recv()
    ring_start(s_all, s_sems, None, (1, 7))
    line_finish(f_all, f_sems)

    def at_place(b, src):
        place = lax.rem(y + src, Y)
        j = lax.div(place, 2)
        lanes = pl.ds(pl.multiple_of(128 * lax.rem(place, 2), 128), 128)
        total = None
        for t in range(2):
            rows = f_all[X * lax.rem(j, 2) + 2 * t + lax.div(j, 2), :, lanes]
            term = jnp.dot(rows, p_all[b, place, t], preferred_element_type=F32)
            total = term if total is None else total + term
        return total

    def near_copy():
        return copy(part, near_in, a_send_sem.at[0], a_recv_sem.at[0], (r, holder(1, core)))

    def send_first(b, term):
        @pl.when(away)
        def _():
            far_send[b] = term.astype(FAR)
            copy(
                far_send.at[b], far_in, a_send_sem.at[1], a_recv_sem.at[1], (pair * Y + y, holder(b, core))
            ).start()

        @pl.when(jnp.logical_and(home, b == 0))
        def _():
            near_in[...] = term

        @pl.when(jnp.logical_and(home, b == 1))
        def _():
            part[...] = term
            near_copy().start()

    term = at_place(core, 0) + at_place(core, 2) + at_place(core, 6)
    for src in (1, 7, 5, 3, 4):
        ring_last(p_all, p_sems, (low, 1 - low), src)
        term = term + at_place(core, src)
    send_first(core, term)
    ring_pass(s_all, s_sems, None)

    term = None
    for src in (0, 2, 6, 1, 7, 5, 3, 4):
        cross_wait(p_all, p_sems, src)
        one = at_place(1 - core, src)
        term = one if term is None else term + one
    send_first(1 - core, term)

    @pl.when(moved)
    def _():
        filt_move.wait_recv()

    @pl.when(stays)
    def _():
        filt_here[...] = filt_send[...]

    ring_relay(s_all, s_sems, None)
    for src in (0, 1, 7, 2, 6):
        cross(s_all, s_sems, src)

    @pl.when(away)
    def _():
        await_recv(near_in, a_recv_sem.at[0])

    await_recv(far_in, a_recv_sem.at[1])
    k_all[my_slot] = ((near_in[...] + far_in[...].astype(F32)) * filt_here[0:1, :]).astype(BF16)
    line_start(k_all, k_sems)
    line_relay(k_all, k_sems)
    for src in (5, 3, 4):
        ring_last(s_all, s_sems, (None,), src)
    for src in range(Y):
        cross_wait(s_all, s_sems, src)

    def by_block(dz, dx):
        at = lax.rem(x + dx, X)
        slot = slot_of(lax.rem(zl + dz, 2), at)
        t, j = lax.div(at, 2), 2 * lax.rem(at, 2) + lax.div(slot, X)
        rows = k_all[slot]
        for b in range(2):
            depth = jnp.concatenate([s_all[b, 2 * j, t], s_all[b, 2 * j + 1, t]], axis=0)
            total[b] += jnp.dot(rows, depth, preferred_element_type=F32)

    total[...] = jnp.zeros_like(total)
    for dz, dx in ((0, 0), (1, 0), (0, X - ahead)):
        by_block(dz, dx)
    for dz, dx in ((0, ahead), (1, 1), (1, X - 1), (0, 2), (1, 2)):
        line_wait(k_all, k_sems, dz, dx)
        by_block(dz, dx)

    own_copy = copy(total.at[1 - core], own_in, o_send_sem, o_recv_sem, over)

    @pl.when(mine)
    def _():
        own_copy.start()
        own_in[...] = total[core]

    @pl.when(not_mine)
    def _():
        for b in range(2):
            part_send[b] = total[b].astype(BF16)
            copy(part_send.at[b], part2_in, b_send_sem, b_recv_sem, (pair * Y + y, c - core + b)).start()

    @pl.when(moved)
    def _():
        f_move.wait_send()
        filt_move.wait_send()

    mate_copy(p_all, p_mate_sem, low).wait_send()
    mate_copy(s_all, s_mate_sem, low).wait_send()
    await_sent(p_all.at[0, pl.ds(0, Y - 1)], p_send_sem)
    await_sent(s_all.at[0, pl.ds(0, Y - 1)], s_send_sem)
    await_sent(p_all.at[0], p_over_sem)
    await_sent(s_all.at[0], s_over_sem)
    await_sent(f_all.at[pl.ds(0, 2 * X - 1)], f_send_sem)
    await_sent(k_all.at[pl.ds(0, 2 * X - 1)], k_send_sem)

    @pl.when(away)
    def _():
        await_sent(far_send, a_send_sem.at[1])

    @pl.when(home)
    def _():
        near_copy().wait_send()

    def x_copy(b):
        at = lax.rem(r, 2)
        return copy(tile_send.at[b], tile_in.at[at], x_send_sem.at[b], x_recv_sem.at[at], tile_to(b))

    @pl.when(not_mine)
    def _():
        await_recv(own_in, o_recv_sem)

    await_recv(part2_in, b_recv_sem)
    rounded = (own_in[...] + part2_in[...].astype(F32)).astype(BF16)
    for b in range(2):
        tile_send[b] = rounded[:, 128 * b : 128 * (b + 1)]

        @pl.when(off_diagonal(b))
        def _():
            x_copy(b).start()

        @pl.when(jnp.logical_not(off_diagonal(b)))
        def _():
            tile_in[b] = tile_send[b]

    wide = rounded.astype(F32)

    @pl.when(mine)
    def _():
        own_copy.wait_send()

    @pl.when(not_mine)
    def _():
        await_sent(part_send, b_send_sem)

    for b in range(2):
        here = slice(128 * b, 128 * (b + 1))

        @pl.when(off_diagonal(b))
        def _():
            await_recv(tile_in.at[b], x_recv_sem.at[b])

        out_ref[:, here] = wide[:, here] - tile_in[b].astype(F32).T

    for b in range(2):

        @pl.when(off_diagonal(b))
        def _():
            x_copy(b).wait_send()


def per_device(fock, density, intersection, fock_mask, density_mask, intersection_mask, product_filter):
    operands = fock, density, intersection, fock_mask, density_mask, intersection_mask, product_filter
    operands = [pltpu.with_memory_space_constraint(one, pltpu.HBM) for one in operands]
    hbm = pl.BlockSpec(memory_space=pltpu.HBM)
    vmem = pl.BlockSpec(memory_space=pltpu.VMEM)
    dma = pltpu.SemaphoreType.DMA
    block = (128, 256)
    return pl.pallas_call(
        kernel,
        out_shape=jax.ShapeDtypeStruct(block, F32),
        in_specs=[hbm] * 7,
        out_specs=vmem,
        scratch_shapes=[pltpu.VMEM(block, BF16)] * 3
        + [pltpu.SMEM((1, 2), jnp.int32)] * 4
        + [
            dma((7,)),
            pltpu.VMEM(block, BF16),
            pltpu.VMEM((2 * X,) + block, BF16),
            pltpu.VMEM((2 * X,) + block, BF16),
            pltpu.VMEM((2, Y, 2) + block, BF16),
            pltpu.VMEM((2, Y, 2) + block, BF16),
            pltpu.VMEM((8, 256), F32),
            pltpu.VMEM((8, 256), F32),
            pltpu.VMEM(block, F32),
            pltpu.VMEM(block, F32),
            pltpu.VMEM((2,) + block, FAR),
            pltpu.VMEM(block, FAR),
            pltpu.VMEM((2,) + block, F32),
            pltpu.VMEM((2,) + block, BF16),
            pltpu.VMEM(block, BF16),
            pltpu.VMEM(block, F32),
            pltpu.VMEM((2, 128, 128), BF16),
            pltpu.VMEM((2, 128, 128), BF16),
            dma((2,)), dma((2,)),
            dma, dma((2, Y + 2)), dma, dma((Y,)), dma((2,)),
            dma, dma((2, Y + 2)), dma, dma((Y,)), dma((2,)),
            dma, dma((2 * X,)), dma, dma((2 * X,)),
            dma((2,)), dma((2,)), dma, dma, dma, dma,
            dma((2,)), dma((2,)),
        ],
        compiler_params=pltpu.CompilerParams(
            collective_id=0, has_side_effects=True, vmem_limit_bytes=32 * 1024 * 1024
        ),
        cost_estimate=pl.CostEstimate(flops=2 * 2 * 512 * 1024 * 256, bytes_accessed=6 * 1024 * 1024, transcendentals=0),
    )(*operands)


def solution(mesh):
    spec = P("row", "col")
    return jax.shard_map(
        per_device, mesh=mesh, in_specs=(spec,) * 7, out_specs=spec, check_vma=False
    )
```

```python
import jax
import jax.numpy as jnp
from jax import lax
from jax.experimental import pallas as pl
from jax.experimental.pallas import tpu as pltpu
from jax.sharding import PartitionSpec as P

MESH = pl.DeviceIdType.MESH
Z, Y, J = 4, 8, 4
X = 4
BF16, F32 = jnp.bfloat16, jnp.float32
FAR = F32


def masked(block, mask_ref):
    lane = lax.broadcasted_iota(jnp.int32, block.shape, 1)
    keep = jnp.where(lane < block.shape[1] // 2, mask_ref[0, 0], mask_ref[0, 1])
    return (block.astype(F32) * keep.astype(F32)).astype(BF16)


def kernel(
    f_hbm, p_hbm, s_hbm, fm_hbm, pm_hbm, sm_hbm, filt_hbm, out_ref,
    f_ref, p_ref, s_ref, fm_ref, pm_ref, sm_ref, filt_ref, in_sem,
    f_send, f_all, k_all, p_all, s_all, filt_send, filt_here,
    part, near_in, far_send, far_in, total, part_send, part2_in, own_in, tile_send, tile_in,
    t_send_sem, t_recv_sem,
    p_send_sem, p_recv_sem, p_over_sem, p_core_sem, p_mate_sem,
    s_send_sem, s_recv_sem, s_over_sem, s_core_sem, s_mate_sem,
    f_send_sem, f_recv_sem, k_send_sem, k_recv_sem,
    a_send_sem, a_recv_sem, b_send_sem, b_recv_sem, o_send_sem, o_recv_sem, x_send_sem, x_recv_sem,
):
    r, c = lax.axis_index("row"), lax.axis_index("col")
    zh, y = lax.div(r, Y), lax.rem(r, Y)
    zl, x, core = lax.div(c, 2 * X), lax.rem(lax.div(c, 2), X), lax.rem(c, 2)
    over = (r, c + 1 - 2 * core)
    low = lax.rem(zh, 2)
    pair = zh + 1 - 2 * low
    mate = Z - 1 - zh
    half = lax.rem(lax.div(zh, 2) + low, 2)
    x_high = lax.div(x, 2)
    home = lax.rem(zl + x_high, 2) == half
    away = lax.rem(zl + x_high, 2) != half
    home_row = jnp.where(home, r, pair * Y + y)
    ahead = jnp.where(core == 0, 1, X - 1)

    def holder(l, k):
        return lax.rem(zl + l, 2) * (2 * X) + x * 2 + k

    def slot_of(z_low, at):
        return X * lax.rem(z_low + lax.div(at, 2) + half, 2) + at

    held_z = 2 * lax.div(zh, 2) + core
    held_zl = lax.rem(x_high + half, 2)
    held_l = lax.rem(zl + held_zl, 2)
    held_from = (held_z * Y + y, held_zl * (2 * X) + x * 2 + held_l)
    term_col = held_zl * (2 * X) + x * 2 + core
    move_to = (home_row, holder(core, low))
    stays = jnp.logical_and(home, jnp.logical_and(core == 0, low == 0))
    moved = jnp.logical_not(stays)
    mine = low == core
    not_mine = low != core

    def ring(d):
        return zh * Y + lax.rem(y + d, Y)

    def on_line(dz, dx):
        return lax.rem(zl + dz, 2) * (2 * X) + lax.rem(x + dx, X) * 2 + core

    def tile_to(b):
        return (2 * c + b, lax.div(r, 2))

    def off_diagonal(b):
        return r != 2 * c + b

    def copy(src, dst, send, recv, to):
        return pltpu.make_async_remote_copy(
            src_ref=src, dst_ref=dst, send_sem=send, recv_sem=recv, device_id=to, device_id_type=MESH
        )

    def await_sent(ref, sem):
        copy(ref, ref, sem, sem, over).wait_send()

    def await_recv(ref, sem):
        copy(ref, ref, sem, sem, over).wait_recv()

    fetches = []
    for n, (src, dst) in enumerate((
        (f_hbm, f_ref), (fm_hbm, fm_ref), (p_hbm, p_ref), (pm_hbm, pm_ref),
        (filt_hbm, filt_ref), (s_hbm, s_ref), (sm_hbm, sm_ref),
    )):
        fetches.append(pltpu.make_async_copy(src, dst, in_sem.at[n]))
        fetches[-1].start()

    barrier = pltpu.get_barrier_semaphore()

    def greet(to):
        pl.semaphore_signal(barrier, inc=1, device_id=to, device_id_type=MESH)

    @pl.when(moved)
    def _():
        greet(held_from)

    greet((mate * Y + y, c))
    for d in (1, 7):
        greet((ring(d), c))
    for dz, dx in ((1, 0), (0, 1), (0, X - 1)):
        greet((r, on_line(dz, dx)))
    greet(over)
    greet((pair * Y + y, term_col))

    @pl.when(away)
    def _():
        greet((r, term_col))

    for one in fetches[:5]:
        one.wait()
    f_send[...] = masked(f_ref[...], fm_ref)
    p_all[core, y, low] = masked(p_ref[...], pm_ref)
    lane = lax.broadcasted_iota(jnp.int32, filt_send.shape, 1)
    filt_send[...] = jnp.where(lane < 128, filt_ref[0, 0], filt_ref[0, 1]).astype(F32)

    pl.semaphore_wait(barrier, jnp.where(moved, 1, 0) + 1 + 2 + 3 + 1 + 1 + jnp.where(away, 1, 0))

    my_slot = slot_of(zl, x)
    f_move = copy(f_send, f_all.at[X * core + x], t_send_sem.at[0], t_recv_sem.at[0], move_to)
    filt_move = copy(filt_send, filt_here, t_send_sem.at[1], t_recv_sem.at[1], move_to)

    @pl.when(moved)
    def _():
        f_move.start()
        filt_move.start()

    def mate_copy(buf, sem, t):
        ref = buf.at[core, y, t]
        return copy(ref, ref, sem.at[0], sem.at[1], (mate * Y + y, c))

    def ring_ref(buf, sems, src, t, part_of):
        slot = lax.rem(y + src, Y)
        at = Y + part_of if part_of is not None else slot
        if t is None:
            ref = buf.at[core, slot] if part_of is None else buf.at[core, slot, part_of]
            return ref, sems[1].at[0, at]
        ref = buf.at[core, slot, t] if part_of is None else buf.at[core, slot, t, pl.ds(64 * part_of, 64)]
        return ref, sems[1].at[t, at]

    def ring_send(buf, sems, src, t, d, part_of=None):
        ref, recv = ring_ref(buf, sems, src, t, part_of)
        copy(ref, ref, sems[0], recv, (ring(d), c)).start()

    def ring_wait(buf, sems, src, t, part_of=None):
        await_recv(*ring_ref(buf, sems, src, t, part_of))

    def ring_start(buf, sems, t):
        for d in (1, 7):
            ring_send(buf, sems, 0, t, d)

    def ring_pass(buf, sems, t):
        for src, on in ((7, 1), (1, 7)):
            ring_wait(buf, sems, src, t)
            ring_send(buf, sems, src, t, on)

    def ring_relay(buf, sems, t):
        for src, on, far, part_of in ((6, 1, 2, 0), (2, 7, 6, 1)):
            ring_wait(buf, sems, src, t)
            ring_send(buf, sems, src, t, on)
            ring_send(buf, sems, src, t, far, part_of)

    def cross(buf, sems, src):
        at = lax.rem(y + src, Y)
        ref = buf.at[core, at]
        copy(ref, ref, sems[2], sems[3].at[at], over).start()

    def cross_wait(buf, sems, src):
        at = lax.rem(y + src, Y)
        await_recv(buf.at[1 - core, at], sems[3].at[at])

    def ring_last(buf, sems, ts, src):
        for t in ts:
            for part_of in range(2) if src == 4 else (None,):
                ring_wait(buf, sems, src, t, part_of)
        cross(buf, sems, src)

    p_sems = (p_send_sem, p_recv_sem, p_over_sem, p_core_sem)
    s_sems = (s_send_sem, s_recv_sem, s_over_sem, s_core_sem)
    mate_copy(p_all, p_mate_sem, low).start()
    ring_start(p_all, p_sems, low)

    def line_send(buf, sems, dz, dx, to):
        slot = slot_of(lax.rem(zl + dz, 2), lax.rem(x + dx, X))
        ref = buf.at[slot]
        copy(ref, ref, sems[0], sems[1].at[slot], (r, to)).start()

    def line_wait(buf, sems, dz, dx):
        slot = slot_of(lax.rem(zl + dz, 2), lax.rem(x + dx, X))
        await_recv(buf.at[slot], sems[1].at[slot])

    def line_start(buf, sems):
        for to in (on_line(1, 0), on_line(0, ahead), on_line(0, X - ahead)):
            line_send(buf, sems, 0, 0, to)

    def line_relay(buf, sems):
        line_wait(buf, sems, 1, 0)
        line_send(buf, sems, 1, 0, on_line(0, 1))
        line_send(buf, sems, 1, 0, on_line(0, X - 1))
        line_wait(buf, sems, 0, X - ahead)
        line_send(buf, sems, 0, X - ahead, on_line(0, ahead))
        line_send(buf, sems, 0, X - ahead, on_line(1, ahead))

    def line_finish(buf, sems):
        for dz, dx in ((0, ahead), (1, 1), (1, X - 1), (0, 2), (1, 2)):
            line_wait(buf, sems, dz, dx)

    f_sems, k_sems = (f_send_sem, f_recv_sem), (k_send_sem, k_recv_sem)
    ring_pass(p_all, p_sems, low)
    mate_copy(p_all, p_mate_sem, 1 - low).wait_recv()
    ring_start(p_all, p_sems, 1 - low)

    @pl.when(moved)
    def _():
        await_recv(f_all.at[my_slot], t_recv_sem.at[0])

    @pl.when(stays)
    def _():
        f_all[my_slot] = f_send[...]

    line_start(f_all, f_sems)
    cross(p_all, p_sems, 0)

    for one in fetches[5:]:
        one.wait()
    s_all[core, y, low] = masked(s_ref[...], sm_ref)
    mate_copy(s_all, s_mate_sem, low).start()

    ring_relay(p_all, p_sems, low)
    line_relay(f_all, f_sems)
    ring_pass(p_all, p_sems, 1 - low)
    cross(p_all, p_sems, 1)
    cross(p_all, p_sems, 7)
    ring_relay(p_all, p_sems, 1 - low)
    cross(p_all, p_sems, 2)
    cross(p_all, p_sems, 6)
    mate_copy(s_all, s_mate_sem, 1 - low).wait_recv()
    ring_start(s_all, s_sems, None)
    line_finish(f_all, f_sems)

    def at_place(b, src):
        place = lax.rem(y + src, Y)
        j = lax.div(place, 2)
        lanes = pl.ds(pl.multiple_of(128 * lax.rem(place, 2), 128), 128)
        total = None
        for t in range(2):
            rows = f_all[X * lax.rem(j, 2) + 2 * t + lax.div(j, 2), :, lanes]
            term = jnp.dot(rows, p_all[b, place, t], preferred_element_type=F32)
            total = term if total is None else total + term
        return total

    def near_copy():
        return copy(part, near_in, a_send_sem.at[0], a_recv_sem.at[0], (r, holder(1, core)))

    def send_first(b, term):
        @pl.when(away)
        def _():
            far_send[b] = term.astype(FAR)
            copy(
                far_send.at[b], far_in, a_send_sem.at[1], a_recv_sem.at[1], (pair * Y + y, holder(b, core))
            ).start()

        @pl.when(jnp.logical_and(home, b == 0))
        def _():
            near_in[...] = term

        @pl.when(jnp.logical_and(home, b == 1))
        def _():
            part[...] = term
            near_copy().start()

    term = at_place(core, 0)
    for src in (1, 7, 2, 6):
        term = term + at_place(core, src)
    for src in (5, 3, 4):
        ring_last(p_all, p_sems, (low, 1 - low), src)
        term = term + at_place(core, src)
    send_first(core, term)
    ring_pass(s_all, s_sems, None)

    term = None
    for src in (0, 1, 7, 2, 6, 5, 3, 4):
        cross_wait(p_all, p_sems, src)
        one = at_place(1 - core, src)
        term = one if term is None else term + one
    send_first(1 - core, term)

    @pl.when(moved)
    def _():
        filt_move.wait_recv()

    @pl.when(stays)
    def _():
        filt_here[...] = filt_send[...]

    ring_relay(s_all, s_sems, None)
    for src in (0, 1, 7, 2, 6):
        cross(s_all, s_sems, src)

    @pl.when(away)
    def _():
        await_recv(near_in, a_recv_sem.at[0])

    await_recv(far_in, a_recv_sem.at[1])
    k_all[my_slot] = ((near_in[...] + far_in[...].astype(F32)) * filt_here[0:1, :]).astype(BF16)
    line_start(k_all, k_sems)
    line_relay(k_all, k_sems)
    for src in (5, 3, 4):
        ring_last(s_all, s_sems, (None,), src)
    for src in range(Y):
        cross_wait(s_all, s_sems, src)

    def by_block(dz, dx):
        at = lax.rem(x + dx, X)
        slot = slot_of(lax.rem(zl + dz, 2), at)
        t, j = lax.div(at, 2), 2 * lax.rem(at, 2) + lax.div(slot, X)
        rows = k_all[slot]
        for b in range(2):
            depth = jnp.concatenate([s_all[b, 2 * j, t], s_all[b, 2 * j + 1, t]], axis=0)
            total[b] += jnp.dot(rows, depth, preferred_element_type=F32)

    total[...] = jnp.zeros_like(total)
    for dz, dx in ((0, 0), (1, 0), (0, X - ahead)):
        by_block(dz, dx)
    for dz, dx in ((0, ahead), (1, 1), (1, X - 1), (0, 2), (1, 2)):
        line_wait(k_all, k_sems, dz, dx)
        by_block(dz, dx)

    own_copy = copy(total.at[1 - core], own_in, o_send_sem, o_recv_sem, over)

    @pl.when(mine)
    def _():
        own_copy.start()
        own_in[...] = total[core]

    @pl.when(not_mine)
    def _():
        for b in range(2):
            part_send[b] = total[b].astype(BF16)
            copy(part_send.at[b], part2_in, b_send_sem, b_recv_sem, (pair * Y + y, c - core + b)).start()

    @pl.when(moved)
    def _():
        f_move.wait_send()
        filt_move.wait_send()

    mate_copy(p_all, p_mate_sem, low).wait_send()
    mate_copy(s_all, s_mate_sem, low).wait_send()
    await_sent(p_all.at[0, pl.ds(0, Y - 1)], p_send_sem)
    await_sent(s_all.at[0, pl.ds(0, Y - 1)], s_send_sem)
    await_sent(p_all.at[0], p_over_sem)
    await_sent(s_all.at[0], s_over_sem)
    await_sent(f_all.at[pl.ds(0, 2 * X - 1)], f_send_sem)
    await_sent(k_all.at[pl.ds(0, 2 * X - 1)], k_send_sem)

    @pl.when(away)
    def _():
        await_sent(far_send, a_send_sem.at[1])

    @pl.when(home)
    def _():
        near_copy().wait_send()

    def x_copy(b):
        at = lax.rem(r, 2)
        return copy(tile_send.at[b], tile_in.at[at], x_send_sem.at[b], x_recv_sem.at[at], tile_to(b))

    @pl.when(not_mine)
    def _():
        await_recv(own_in, o_recv_sem)

    await_recv(part2_in, b_recv_sem)
    rounded = (own_in[...] + part2_in[...].astype(F32)).astype(BF16)
    for b in range(2):
        tile_send[b] = rounded[:, 128 * b : 128 * (b + 1)]

        @pl.when(off_diagonal(b))
        def _():
            x_copy(b).start()

        @pl.when(jnp.logical_not(off_diagonal(b)))
        def _():
            tile_in[b] = tile_send[b]

    wide = rounded.astype(F32)

    @pl.when(mine)
    def _():
        own_copy.wait_send()

    @pl.when(not_mine)
    def _():
        await_sent(part_send, b_send_sem)

    for b in range(2):
        here = slice(128 * b, 128 * (b + 1))

        @pl.when(off_diagonal(b))
        def _():
            await_recv(tile_in.at[b], x_recv_sem.at[b])

        out_ref[:, here] = wide[:, here] - tile_in[b].astype(F32).T

    for b in range(2):

        @pl.when(off_diagonal(b))
        def _():
            x_copy(b).wait_send()


def per_device(fock, density, intersection, fock_mask, density_mask, intersection_mask, product_filter):
    operands = fock, density, intersection, fock_mask, density_mask, intersection_mask, product_filter
    operands = [pltpu.with_memory_space_constraint(one, pltpu.HBM) for one in operands]
    hbm = pl.BlockSpec(memory_space=pltpu.HBM)
    vmem = pl.BlockSpec(memory_space=pltpu.VMEM)
    dma = pltpu.SemaphoreType.DMA
    block = (128, 256)
    return pl.pallas_call(
        kernel,
        out_shape=jax.ShapeDtypeStruct(block, F32),
        in_specs=[hbm] * 7,
        out_specs=vmem,
        scratch_shapes=[pltpu.VMEM(block, BF16)] * 3
        + [pltpu.SMEM((1, 2), jnp.int32)] * 4
        + [
            dma((7,)),
            pltpu.VMEM(block, BF16),
            pltpu.VMEM((2 * X,) + block, BF16),
            pltpu.VMEM((2 * X,) + block, BF16),
            pltpu.VMEM((2, Y, 2) + block, BF16),
            pltpu.VMEM((2, Y, 2) + block, BF16),
            pltpu.VMEM((8, 256), F32),
            pltpu.VMEM((8, 256), F32),
            pltpu.VMEM(block, F32),
            pltpu.VMEM(block, F32),
            pltpu.VMEM((2,) + block, FAR),
            pltpu.VMEM(block, FAR),
            pltpu.VMEM((2,) + block, F32),
            pltpu.VMEM((2,) + block, BF16),
            pltpu.VMEM(block, BF16),
            pltpu.VMEM(block, F32),
            pltpu.VMEM((2, 128, 128), BF16),
            pltpu.VMEM((2, 128, 128), BF16),
            dma((2,)), dma((2,)),
            dma, dma((2, Y + 2)), dma, dma((Y,)), dma((2,)),
            dma, dma((2, Y + 2)), dma, dma((Y,)), dma((2,)),
            dma, dma((2 * X,)), dma, dma((2 * X,)),
            dma((2,)), dma((2,)), dma, dma, dma, dma,
            dma((2,)), dma((2,)),
        ],
        compiler_params=pltpu.CompilerParams(
            collective_id=0, has_side_effects=True, vmem_limit_bytes=32 * 1024 * 1024
        ),
        cost_estimate=pl.CostEstimate(flops=2 * 2 * 512 * 1024 * 256, bytes_accessed=6 * 1024 * 1024, transcendentals=0),
    )(*operands)


def solution(mesh):
    spec = P("row", "col")
    return jax.shard_map(
        per_device, mesh=mesh, in_specs=(spec,) * 7, out_specs=spec, check_vma=False
    )
```

```python
import jax
import jax.numpy as jnp
from jax import lax
from jax.experimental import pallas as pl
from jax.experimental.pallas import tpu as pltpu
from jax.sharding import PartitionSpec as P

MESH = pl.DeviceIdType.MESH
Z, Y, J = 4, 8, 4
X = 4
BF16, F32 = jnp.bfloat16, jnp.float32
FAR = BF16


def masked(block, mask_ref):
    lane = lax.broadcasted_iota(jnp.int32, block.shape, 1)
    keep = jnp.where(lane < block.shape[1] // 2, mask_ref[0, 0], mask_ref[0, 1])
    return (block.astype(F32) * keep.astype(F32)).astype(BF16)


def kernel(
    f_hbm, p_hbm, s_hbm, fm_hbm, pm_hbm, sm_hbm, filt_hbm, out_ref,
    f_ref, p_ref, s_ref, fm_ref, pm_ref, sm_ref, filt_ref, in_sem,
    f_send, f_all, k_all, p_all, s_all, filt_send, filt_here,
    part, near_in, far_send, far_in, total, part_send, part2_in, block_send, block_in, tile_send, tile_in,
    t_send_sem, t_recv_sem,
    p_send_sem, p_recv_sem, p_over_sem, p_core_sem, p_mate_sem,
    s_send_sem, s_recv_sem, s_over_sem, s_core_sem, s_mate_sem,
    f_send_sem, f_recv_sem, k_send_sem, k_recv_sem,
    a_send_sem, a_recv_sem, b_send_sem, b_recv_sem, o_send_sem, o_recv_sem, x_send_sem, x_recv_sem,
):
    r, c = lax.axis_index("row"), lax.axis_index("col")
    zh, y = lax.div(r, Y), lax.rem(r, Y)
    zl, x, core = lax.div(c, 2 * X), lax.rem(lax.div(c, 2), X), lax.rem(c, 2)
    over = (r, c + 1 - 2 * core)
    low = lax.rem(zh, 2)
    pair = zh + 1 - 2 * low
    mate = Z - 1 - zh
    half = lax.rem(lax.div(zh, 2) + low, 2)
    x_high = lax.div(x, 2)
    home = lax.rem(zl + x_high, 2) == half
    away = lax.rem(zl + x_high, 2) != half
    home_row = jnp.where(home, r, pair * Y + y)
    ahead = jnp.where(core == 0, 1, X - 1)

    def holder(l, k):
        return lax.rem(zl + l, 2) * (2 * X) + x * 2 + k

    def slot_of(z_low, at):
        return X * lax.rem(z_low + lax.div(at, 2) + half, 2) + at

    held_z = 2 * lax.div(zh, 2) + core
    held_zl = lax.rem(x_high + half, 2)
    held_l = lax.rem(zl + held_zl, 2)
    held_from = (held_z * Y + y, held_zl * (2 * X) + x * 2 + held_l)
    term_col = held_zl * (2 * X) + x * 2 + core
    move_to = (home_row, holder(core, low))
    stays = jnp.logical_and(home, jnp.logical_and(core == 0, low == 0))
    moved = jnp.logical_not(stays)
    mine = low == core

    def ring(d):
        return zh * Y + lax.rem(y + d, Y)

    def on_line(dz, dx):
        return lax.rem(zl + dz, 2) * (2 * X) + lax.rem(x + dx, X) * 2 + core

    def copy(src, dst, send, recv, to):
        return pltpu.make_async_remote_copy(
            src_ref=src, dst_ref=dst, send_sem=send, recv_sem=recv, device_id=to, device_id_type=MESH
        )

    def await_sent(ref, sem):
        copy(ref, ref, sem, sem, over).wait_send()

    def await_recv(ref, sem):
        copy(ref, ref, sem, sem, over).wait_recv()

    fetches = []
    for n, (src, dst) in enumerate((
        (f_hbm, f_ref), (fm_hbm, fm_ref), (p_hbm, p_ref), (pm_hbm, pm_ref),
        (filt_hbm, filt_ref), (s_hbm, s_ref), (sm_hbm, sm_ref),
    )):
        fetches.append(pltpu.make_async_copy(src, dst, in_sem.at[n]))
        fetches[-1].start()

    barrier = pltpu.get_barrier_semaphore()

    def greet(to):
        pl.semaphore_signal(barrier, inc=1, device_id=to, device_id_type=MESH)

    @pl.when(moved)
    def _():
        greet(held_from)

    greet((mate * Y + y, c))
    for d in (2, 6, 1, 7):
        greet((ring(d), c))
    for dz, dx in ((1, 0), (0, 1), (0, X - 1)):
        greet((r, on_line(dz, dx)))
    greet(over)
    greet((pair * Y + y, term_col))

    @pl.when(away)
    def _():
        greet((r, term_col))

    for one in fetches[:5]:
        one.wait()
    f_send[...] = masked(f_ref[...], fm_ref)
    p_all[core, y, low] = masked(p_ref[...], pm_ref)
    lane = lax.broadcasted_iota(jnp.int32, filt_send.shape, 1)
    filt_send[...] = jnp.where(lane < 128, filt_ref[0, 0], filt_ref[0, 1]).astype(F32)

    pl.semaphore_wait(barrier, jnp.where(moved, 1, 0) + 1 + 4 + 3 + 1 + 1 + jnp.where(away, 1, 0))

    my_slot = slot_of(zl, x)
    f_move = copy(f_send, f_all.at[X * core + x], t_send_sem.at[0], t_recv_sem.at[0], move_to)
    filt_move = copy(filt_send, filt_here, t_send_sem.at[1], t_recv_sem.at[1], move_to)

    @pl.when(moved)
    def _():
        f_move.start()
        filt_move.start()

    def mate_copy(buf, sem, t):
        ref = buf.at[core, y, t]
        return copy(ref, ref, sem.at[0], sem.at[1], (mate * Y + y, c))

    def ring_ref(buf, sems, src, t, part_of):
        slot = lax.rem(y + src, Y)
        at = Y + part_of if part_of is not None else slot
        if t is None:
            ref = buf.at[core, slot] if part_of is None else buf.at[core, slot, part_of]
            return ref, sems[1].at[0, at]
        ref = buf.at[core, slot, t] if part_of is None else buf.at[core, slot, t, pl.ds(64 * part_of, 64)]
        return ref, sems[1].at[t, at]

    def ring_send(buf, sems, src, t, d, part_of=None):
        ref, recv = ring_ref(buf, sems, src, t, part_of)
        copy(ref, ref, sems[0], recv, (ring(d), c)).start()

    def ring_wait(buf, sems, src, t, part_of=None):
        await_recv(*ring_ref(buf, sems, src, t, part_of))

    def ring_start(buf, sems, t, to=(2, 6, 1, 7)):
        for d in to:
            ring_send(buf, sems, 0, t, d)

    def ring_pass(buf, sems, t):
        for src, on in ((7, 1), (1, 7)):
            ring_wait(buf, sems, src, t)
            ring_send(buf, sems, src, t, on)

    def ring_relay(buf, sems, t):
        for src, on, far, part_of in ((6, 1, 2, 0), (2, 7, 6, 1)):
            ring_wait(buf, sems, src, t)
            ring_send(buf, sems, src, t, on)
            ring_send(buf, sems, src, t, far, part_of)

    def cross(buf, sems, src):
        at = lax.rem(y + src, Y)
        ref = buf.at[core, at]
        copy(ref, ref, sems[2], sems[3].at[at], over).start()

    def cross_wait(buf, sems, src):
        at = lax.rem(y + src, Y)
        await_recv(buf.at[1 - core, at], sems[3].at[at])

    def ring_last(buf, sems, ts, src):
        for t in ts:
            for part_of in range(2) if src == 4 else (None,):
                ring_wait(buf, sems, src, t, part_of)
        cross(buf, sems, src)

    p_sems = (p_send_sem, p_recv_sem, p_over_sem, p_core_sem)
    s_sems = (s_send_sem, s_recv_sem, s_over_sem, s_core_sem)
    mate_copy(p_all, p_mate_sem, low).start()
    ring_start(p_all, p_sems, low)

    def line_send(buf, sems, dz, dx, to):
        slot = slot_of(lax.rem(zl + dz, 2), lax.rem(x + dx, X))
        ref = buf.at[slot]
        copy(ref, ref, sems[0], sems[1].at[slot], (r, to)).start()

    def line_wait(buf, sems, dz, dx):
        slot = slot_of(lax.rem(zl + dz, 2), lax.rem(x + dx, X))
        await_recv(buf.at[slot], sems[1].at[slot])

    def line_start(buf, sems):
        for to in (on_line(1, 0), on_line(0, ahead), on_line(0, X - ahead)):
            line_send(buf, sems, 0, 0, to)

    def line_relay(buf, sems):
        line_wait(buf, sems, 1, 0)
        line_send(buf, sems, 1, 0, on_line(0, 1))
        line_send(buf, sems, 1, 0, on_line(0, X - 1))
        line_wait(buf, sems, 0, X - ahead)
        line_send(buf, sems, 0, X - ahead, on_line(0, ahead))
        line_send(buf, sems, 0, X - ahead, on_line(1, ahead))

    def line_finish(buf, sems):
        for dz, dx in ((0, ahead), (1, 1), (1, X - 1), (0, 2), (1, 2)):
            line_wait(buf, sems, dz, dx)

    f_sems, k_sems = (f_send_sem, f_recv_sem), (k_send_sem, k_recv_sem)
    mate_copy(p_all, p_mate_sem, 1 - low).wait_recv()
    ring_start(p_all, p_sems, 1 - low)

    @pl.when(moved)
    def _():
        await_recv(f_all.at[my_slot], t_recv_sem.at[0])

    @pl.when(stays)
    def _():
        f_all[my_slot] = f_send[...]

    line_start(f_all, f_sems)
    cross(p_all, p_sems, 0)

    for one in fetches[5:]:
        one.wait()
    s_all[core, y, low] = masked(s_ref[...], sm_ref)
    mate_copy(s_all, s_mate_sem, low).start()

    ring_relay(p_all, p_sems, low)
    line_relay(f_all, f_sems)
    ring_relay(p_all, p_sems, 1 - low)
    cross(p_all, p_sems, 2)
    cross(p_all, p_sems, 6)
    mate_copy(s_all, s_mate_sem, 1 - low).wait_recv()
    ring_start(s_all, s_sems, None, (1, 7))
    line_finish(f_all, f_sems)

    def at_place(b, src):
        place = lax.rem(y + src, Y)
        j = lax.div(place, 2)
        lanes = pl.ds(pl.multiple_of(128 * lax.rem(place, 2), 128), 128)
        total = None
        for t in range(2):
            rows = f_all[X * lax.rem(j, 2) + 2 * t + lax.div(j, 2), :, lanes]
            term = jnp.dot(rows, p_all[b, place, t], preferred_element_type=F32)
            total = term if total is None else total + term
        return total

    def near_copy():
        return copy(part, near_in, a_send_sem.at[0], a_recv_sem.at[0], (r, holder(1, core)))

    def send_first(b, term):
        @pl.when(away)
        def _():
            far_send[b] = term.astype(FAR)
            copy(
                far_send.at[b], far_in, a_send_sem.at[1], a_recv_sem.at[1], (pair * Y + y, holder(b, core))
            ).start()

        @pl.when(jnp.logical_and(home, b == 0))
        def _():
            near_in[...] = term

        @pl.when(jnp.logical_and(home, b == 1))
        def _():
            part[...] = term
            near_copy().start()

    term = at_place(core, 0) + at_place(core, 2) + at_place(core, 6)
    for src in (1, 7, 5, 3, 4):
        ring_last(p_all, p_sems, (low, 1 - low), src)
        term = term + at_place(core, src)
    send_first(core, term)
    ring_pass(s_all, s_sems, None)

    term = None
    for src in (0, 2, 6, 1, 7, 5, 3, 4):
        cross_wait(p_all, p_sems, src)
        one = at_place(1 - core, src)
        term = one if term is None else term + one
    send_first(1 - core, term)

    @pl.when(moved)
    def _():
        filt_move.wait_recv()

    @pl.when(stays)
    def _():
        filt_here[...] = filt_send[...]

    ring_relay(s_all, s_sems, None)
    for src in (0, 1, 7, 2, 6):
        cross(s_all, s_sems, src)

    @pl.when(away)
    def _():
        await_recv(near_in, a_recv_sem.at[0])

    await_recv(far_in, a_recv_sem.at[1])
    k_all[my_slot] = ((near_in[...] + far_in[...].astype(F32)) * filt_here[0:1, :]).astype(BF16)
    line_start(k_all, k_sems)
    line_relay(k_all, k_sems)
    for src in (5, 3, 4):
        ring_last(s_all, s_sems, (None,), src)
    for src in range(Y):
        cross_wait(s_all, s_sems, src)

    def by_block(dz, dx):
        at = lax.rem(x + dx, X)
        slot = slot_of(lax.rem(zl + dz, 2), at)
        t, j = lax.div(at, 2), 2 * lax.rem(at, 2) + lax.div(slot, X)
        rows = k_all[slot]
        for b in range(2):
            depth = jnp.concatenate([s_all[b, 2 * j, t], s_all[b, 2 * j + 1, t]], axis=0)
            total[b] += jnp.dot(rows, depth, preferred_element_type=F32)

    total[...] = jnp.zeros_like(total)
    for dz, dx in ((0, 0), (1, 0), (0, X - ahead)):
        by_block(dz, dx)
    for dz, dx in ((0, ahead), (1, 1), (1, X - 1), (0, 2), (1, 2)):
        line_wait(k_all, k_sems, dz, dx)
        by_block(dz, dx)

    kept_b = jnp.where(mine, 0, 1)
    part_send[...] = total[1 - kept_b].astype(BF16)
    part_copy = copy(part_send, part2_in, b_send_sem, b_recv_sem, (pair * Y + y, c))
    part_copy.start()

    @pl.when(moved)
    def _():
        f_move.wait_send()
        filt_move.wait_send()

    mate_copy(p_all, p_mate_sem, low).wait_send()
    mate_copy(s_all, s_mate_sem, low).wait_send()
    await_sent(p_all.at[0, pl.ds(0, Y - 1)], p_send_sem)
    await_sent(s_all.at[0, pl.ds(0, Y - 1)], s_send_sem)
    await_sent(p_all.at[0], p_over_sem)
    await_sent(s_all.at[0], s_over_sem)
    await_sent(f_all.at[pl.ds(0, 2 * X - 1)], f_send_sem)
    await_sent(k_all.at[pl.ds(0, 2 * X - 1)], k_send_sem)

    @pl.when(away)
    def _():
        await_sent(far_send, a_send_sem.at[1])

    @pl.when(home)
    def _():
        near_copy().wait_send()

    block_row = jnp.where(mine, r, pair * Y + y)
    block_col = c - core + kept_b
    own_here = jnp.logical_and(low == 0, core == 0)
    own_comes = jnp.logical_not(own_here)
    own_sent = jnp.logical_not(jnp.logical_and(mine, core == 0))
    block_copy = copy(block_send, block_in, o_send_sem, o_recv_sem, (block_row, block_col))

    def tile_stays(h):
        return jnp.logical_and(2 * block_col + h == r, lax.div(block_row, 2) == c)

    def tile_copy(h):
        at = lax.rem(block_row, 2)
        return copy(
            tile_send.at[h], tile_in.at[at], x_send_sem.at[h], x_recv_sem.at[at], (2 * block_col + h, lax.div(block_row, 2))
        )

    def tile_is_here(b):
        row, col = 2 * c + b, lax.div(r, 2)
        z = lax.div(row, Y)
        z_low, second = lax.rem(z, 2), lax.rem(col, 2)
        z_at = z + second * (1 - 2 * z_low)
        return jnp.logical_and(z_at * Y + lax.rem(row, Y) == r, col - second + z_low == c)

    part_copy.wait_recv()
    rounded = (total[kept_b] + part2_in[...].astype(F32)).astype(BF16)
    for h in range(2):
        tile_send[h] = rounded[:, 128 * h : 128 * (h + 1)]

        @pl.when(jnp.logical_not(tile_stays(h)))
        def _():
            tile_copy(h).start()

        @pl.when(tile_stays(h))
        def _():
            tile_in[lax.rem(block_row, 2)] = tile_send[h]

    block_send[...] = rounded

    @pl.when(own_sent)
    def _():
        block_copy.start()

    @pl.when(own_here)
    def _():
        block_in[...] = rounded

    part_copy.wait_send()

    @pl.when(own_comes)
    def _():
        await_recv(block_in, o_recv_sem)

    for b in range(2):
        here = slice(128 * b, 128 * (b + 1))

        @pl.when(jnp.logical_not(tile_is_here(b)))
        def _():
            await_recv(tile_in.at[b], x_recv_sem.at[b])

        out_ref[:, here] = block_in[:, here].astype(F32) - tile_in[b].astype(F32).T

    @pl.when(own_sent)
    def _():
        block_copy.wait_send()

    for h in range(2):

        @pl.when(jnp.logical_not(tile_stays(h)))
        def _():
            tile_copy(h).wait_send()


def per_device(fock, density, intersection, fock_mask, density_mask, intersection_mask, product_filter):
    operands = fock, density, intersection, fock_mask, density_mask, intersection_mask, product_filter
    operands = [pltpu.with_memory_space_constraint(one, pltpu.HBM) for one in operands]
    hbm = pl.BlockSpec(memory_space=pltpu.HBM)
    vmem = pl.BlockSpec(memory_space=pltpu.VMEM)
    dma = pltpu.SemaphoreType.DMA
    block = (128, 256)
    return pl.pallas_call(
        kernel,
        out_shape=jax.ShapeDtypeStruct(block, F32),
        in_specs=[hbm] * 7,
        out_specs=vmem,
        scratch_shapes=[pltpu.VMEM(block, BF16)] * 3
        + [pltpu.SMEM((1, 2), jnp.int32)] * 4
        + [
            dma((7,)),
            pltpu.VMEM(block, BF16),
            pltpu.VMEM((2 * X,) + block, BF16),
            pltpu.VMEM((2 * X,) + block, BF16),
            pltpu.VMEM((2, Y, 2) + block, BF16),
            pltpu.VMEM((2, Y, 2) + block, BF16),
            pltpu.VMEM((8, 256), F32),
            pltpu.VMEM((8, 256), F32),
            pltpu.VMEM(block, F32),
            pltpu.VMEM(block, F32),
            pltpu.VMEM((2,) + block, FAR),
            pltpu.VMEM(block, FAR),
            pltpu.VMEM((2,) + block, F32),
            pltpu.VMEM(block, BF16),
            pltpu.VMEM(block, BF16),
            pltpu.VMEM(block, BF16),
            pltpu.VMEM(block, BF16),
            pltpu.VMEM((2, 128, 128), BF16),
            pltpu.VMEM((2, 128, 128), BF16),
            dma((2,)), dma((2,)),
            dma, dma((2, Y + 2)), dma, dma((Y,)), dma((2,)),
            dma, dma((2, Y + 2)), dma, dma((Y,)), dma((2,)),
            dma, dma((2 * X,)), dma, dma((2 * X,)),
            dma((2,)), dma((2,)), dma, dma, dma, dma,
            dma((2,)), dma((2,)),
        ],
        compiler_params=pltpu.CompilerParams(
            collective_id=0, has_side_effects=True, vmem_limit_bytes=32 * 1024 * 1024
        ),
        cost_estimate=pl.CostEstimate(flops=2 * 2 * 512 * 1024 * 256, bytes_accessed=6 * 1024 * 1024, transcendentals=0),
    )(*operands)


def solution(mesh):
    spec = P("row", "col")
    return jax.shard_map(
        per_device, mesh=mesh, in_specs=(spec,) * 7, out_specs=spec, check_vma=False
    )
```

```python
import jax
import jax.numpy as jnp
from jax import lax
from jax.experimental import pallas as pl
from jax.experimental.pallas import tpu as pltpu
from jax.sharding import PartitionSpec as P

MESH = pl.DeviceIdType.MESH
Z, Y, J = 4, 8, 4
X = 4
BF16, F32 = jnp.bfloat16, jnp.float32
FAR = BF16


def masked(block, mask_ref):
    lane = lax.broadcasted_iota(jnp.int32, block.shape, 1)
    keep = jnp.where(lane < block.shape[1] // 2, mask_ref[0, 0], mask_ref[0, 1])
    return (block.astype(F32) * keep.astype(F32)).astype(BF16)


def kernel(
    f_hbm, p_hbm, s_hbm, fm_hbm, pm_hbm, sm_hbm, filt_hbm, out_ref,
    f_ref, p_ref, s_ref, fm_ref, pm_ref, sm_ref, filt_ref, in_sem,
    f_send, f_all, k_all, p_all, s_all, filt_send, filt_here,
    part, near_in, far_send, far_in, total, part_send, part2_in, block_send, block_in, tile_send, tile_in,
    t_send_sem, t_recv_sem,
    p_send_sem, p_recv_sem, p_over_sem, p_core_sem, p_mate_sem,
    s_send_sem, s_recv_sem, s_over_sem, s_core_sem, s_mate_sem,
    f_send_sem, f_recv_sem, k_send_sem, k_recv_sem,
    a_send_sem, a_recv_sem, b_send_sem, b_recv_sem, o_send_sem, o_recv_sem, x_send_sem, x_recv_sem,
):
    r, c = lax.axis_index("row"), lax.axis_index("col")
    zh, y = lax.div(r, Y), lax.rem(r, Y)
    zl, x, core = lax.div(c, 2 * X), lax.rem(lax.div(c, 2), X), lax.rem(c, 2)
    over = (r, c + 1 - 2 * core)
    low = lax.rem(zh, 2)
    pair = zh + 1 - 2 * low
    mate = Z - 1 - zh
    half = lax.rem(lax.div(zh, 2) + low, 2)
    x_high = lax.div(x, 2)
    home = lax.rem(zl + x_high, 2) == half
    away = lax.rem(zl + x_high, 2) != half
    home_row = jnp.where(home, r, pair * Y + y)
    ahead = jnp.where(core == 0, 1, X - 1)

    def holder(l, k):
        return lax.rem(zl + l, 2) * (2 * X) + x * 2 + k

    def slot_of(z_low, at):
        return X * lax.rem(z_low + lax.div(at, 2) + half, 2) + at

    held_z = 2 * lax.div(zh, 2) + core
    held_zl = lax.rem(x_high + half, 2)
    held_l = lax.rem(zl + held_zl, 2)
    held_from = (held_z * Y + y, held_zl * (2 * X) + x * 2 + held_l)
    term_col = held_zl * (2 * X) + x * 2 + core
    move_to = (home_row, holder(core, low))
    stays = jnp.logical_and(home, jnp.logical_and(core == 0, low == 0))
    moved = jnp.logical_not(stays)
    mine = low == core

    def ring(d):
        return zh * Y + lax.rem(y + d, Y)

    def on_line(dz, dx):
        return lax.rem(zl + dz, 2) * (2 * X) + lax.rem(x + dx, X) * 2 + core

    def copy(src, dst, send, recv, to):
        return pltpu.make_async_remote_copy(
            src_ref=src, dst_ref=dst, send_sem=send, recv_sem=recv, device_id=to, device_id_type=MESH
        )

    def await_sent(ref, sem):
        copy(ref, ref, sem, sem, over).wait_send()

    def await_recv(ref, sem):
        copy(ref, ref, sem, sem, over).wait_recv()

    fetches = []
    for n, (src, dst) in enumerate((
        (f_hbm, f_ref), (fm_hbm, fm_ref), (p_hbm, p_ref), (pm_hbm, pm_ref),
        (filt_hbm, filt_ref), (s_hbm, s_ref), (sm_hbm, sm_ref),
    )):
        fetches.append(pltpu.make_async_copy(src, dst, in_sem.at[n]))
        fetches[-1].start()

    barrier = pltpu.get_barrier_semaphore()

    def greet(to):
        pl.semaphore_signal(barrier, inc=1, device_id=to, device_id_type=MESH)

    @pl.when(moved)
    def _():
        greet(held_from)

    greet((mate * Y + y, c))
    for d in (2, 6, 1, 7):
        greet((ring(d), c))
    for dz, dx in ((1, 0), (0, 1), (0, X - 1)):
        greet((r, on_line(dz, dx)))
    greet(over)
    greet((pair * Y + y, term_col))

    @pl.when(away)
    def _():
        greet((r, term_col))

    for one in fetches[:5]:
        one.wait()
    f_send[...] = masked(f_ref[...], fm_ref)
    p_all[core, y, low] = masked(p_ref[...], pm_ref)
    lane = lax.broadcasted_iota(jnp.int32, filt_send.shape, 1)
    filt_send[...] = jnp.where(lane < 128, filt_ref[0, 0], filt_ref[0, 1]).astype(F32)

    pl.semaphore_wait(barrier, jnp.where(moved, 1, 0) + 1 + 4 + 3 + 1 + 1 + jnp.where(away, 1, 0))

    my_slot = slot_of(zl, x)
    f_move = copy(f_send, f_all.at[X * core + x], t_send_sem.at[0], t_recv_sem.at[0], move_to)
    filt_move = copy(filt_send, filt_here, t_send_sem.at[1], t_recv_sem.at[1], move_to)

    @pl.when(moved)
    def _():
        f_move.start()
        filt_move.start()

    def mate_copy(buf, sem, t):
        ref = buf.at[core, y, t]
        return copy(ref, ref, sem.at[0], sem.at[1], (mate * Y + y, c))

    def ring_ref(buf, sems, src, t, part_of):
        slot = lax.rem(y + src, Y)
        at = Y + part_of if part_of is not None else slot
        if t is None:
            ref = buf.at[core, slot] if part_of is None else buf.at[core, slot, part_of]
            return ref, sems[1].at[0, at]
        ref = buf.at[core, slot, t] if part_of is None else buf.at[core, slot, t, pl.ds(64 * part_of, 64)]
        return ref, sems[1].at[t, at]

    def ring_send(buf, sems, src, t, d, part_of=None):
        ref, recv = ring_ref(buf, sems, src, t, part_of)
        copy(ref, ref, sems[0], recv, (ring(d), c)).start()

    def ring_wait(buf, sems, src, t, part_of=None):
        await_recv(*ring_ref(buf, sems, src, t, part_of))

    def ring_start(buf, sems, t):
        for d in (2, 6, 1, 7):
            ring_send(buf, sems, 0, t, d)

    def ring_relay(buf, sems, t):
        for src, on, far, part_of in ((6, 1, 2, 0), (2, 7, 6, 1)):
            ring_wait(buf, sems, src, t)
            ring_send(buf, sems, src, t, on)
            ring_send(buf, sems, src, t, far, part_of)

    def cross(buf, sems, src):
        at = lax.rem(y + src, Y)
        ref = buf.at[core, at]
        copy(ref, ref, sems[2], sems[3].at[at], over).start()

    def cross_wait(buf, sems, src):
        at = lax.rem(y + src, Y)
        await_recv(buf.at[1 - core, at], sems[3].at[at])

    def ring_last(buf, sems, ts, src):
        for t in ts:
            for part_of in range(2) if src == 4 else (None,):
                ring_wait(buf, sems, src, t, part_of)
        cross(buf, sems, src)

    p_sems = (p_send_sem, p_recv_sem, p_over_sem, p_core_sem)
    s_sems = (s_send_sem, s_recv_sem, s_over_sem, s_core_sem)
    mate_copy(p_all, p_mate_sem, low).start()
    ring_start(p_all, p_sems, low)

    def line_send(buf, sems, dz, dx, to):
        slot = slot_of(lax.rem(zl + dz, 2), lax.rem(x + dx, X))
        ref = buf.at[slot]
        copy(ref, ref, sems[0], sems[1].at[slot], (r, to)).start()

    def line_wait(buf, sems, dz, dx):
        slot = slot_of(lax.rem(zl + dz, 2), lax.rem(x + dx, X))
        await_recv(buf.at[slot], sems[1].at[slot])

    def line_start(buf, sems):
        for to in (on_line(1, 0), on_line(0, ahead), on_line(0, X - ahead)):
            line_send(buf, sems, 0, 0, to)

    def line_relay(buf, sems):
        line_wait(buf, sems, 1, 0)
        line_send(buf, sems, 1, 0, on_line(0, 1))
        line_send(buf, sems, 1, 0, on_line(0, X - 1))
        line_wait(buf, sems, 0, X - ahead)
        line_send(buf, sems, 0, X - ahead, on_line(0, ahead))
        line_send(buf, sems, 0, X - ahead, on_line(1, ahead))

    def line_finish(buf, sems):
        for dz, dx in ((0, ahead), (1, 1), (1, X - 1), (0, 2), (1, 2)):
            line_wait(buf, sems, dz, dx)

    f_sems, k_sems = (f_send_sem, f_recv_sem), (k_send_sem, k_recv_sem)
    mate_copy(p_all, p_mate_sem, 1 - low).wait_recv()
    ring_start(p_all, p_sems, 1 - low)

    @pl.when(moved)
    def _():
        await_recv(f_all.at[my_slot], t_recv_sem.at[0])

    @pl.when(stays)
    def _():
        f_all[my_slot] = f_send[...]

    line_start(f_all, f_sems)
    cross(p_all, p_sems, 0)

    for one in fetches[5:]:
        one.wait()
    s_all[core, y, low] = masked(s_ref[...], sm_ref)
    mate_copy(s_all, s_mate_sem, low).start()

    ring_relay(p_all, p_sems, low)
    line_relay(f_all, f_sems)
    ring_relay(p_all, p_sems, 1 - low)
    cross(p_all, p_sems, 2)
    cross(p_all, p_sems, 6)
    mate_copy(s_all, s_mate_sem, 1 - low).wait_recv()
    ring_start(s_all, s_sems, None)
    line_finish(f_all, f_sems)

    def at_place(b, src):
        place = lax.rem(y + src, Y)
        j = lax.div(place, 2)
        lanes = pl.ds(pl.multiple_of(128 * lax.rem(place, 2), 128), 128)
        total = None
        for t in range(2):
            rows = f_all[X * lax.rem(j, 2) + 2 * t + lax.div(j, 2), :, lanes]
            term = jnp.dot(rows, p_all[b, place, t], preferred_element_type=F32)
            total = term if total is None else total + term
        return total

    def near_copy():
        return copy(part, near_in, a_send_sem.at[0], a_recv_sem.at[0], (r, holder(1, core)))

    def send_first(b, term):
        @pl.when(away)
        def _():
            far_send[b] = term.astype(FAR)
            copy(
                far_send.at[b], far_in, a_send_sem.at[1], a_recv_sem.at[1], (pair * Y + y, holder(b, core))
            ).start()

        @pl.when(jnp.logical_and(home, b == 0))
        def _():
            near_in[...] = term

        @pl.when(jnp.logical_and(home, b == 1))
        def _():
            part[...] = term
            near_copy().start()

    term = at_place(core, 0) + at_place(core, 2) + at_place(core, 6)
    for src in (1, 7, 5, 3, 4):
        ring_last(p_all, p_sems, (low, 1 - low), src)
        term = term + at_place(core, src)
    send_first(core, term)

    term = None
    for src in (0, 2, 6, 1, 7, 5, 3, 4):
        cross_wait(p_all, p_sems, src)
        one = at_place(1 - core, src)
        term = one if term is None else term + one
    send_first(1 - core, term)

    @pl.when(moved)
    def _():
        filt_move.wait_recv()

    @pl.when(stays)
    def _():
        filt_here[...] = filt_send[...]

    ring_relay(s_all, s_sems, None)
    for src in (0, 2, 6):
        cross(s_all, s_sems, src)

    @pl.when(away)
    def _():
        await_recv(near_in, a_recv_sem.at[0])

    await_recv(far_in, a_recv_sem.at[1])
    k_all[my_slot] = ((near_in[...] + far_in[...].astype(F32)) * filt_here[0:1, :]).astype(BF16)
    line_start(k_all, k_sems)
    line_relay(k_all, k_sems)
    for src in (1, 7, 5, 3, 4):
        ring_last(s_all, s_sems, (None,), src)
    for src in range(Y):
        cross_wait(s_all, s_sems, src)

    def by_block(dz, dx):
        at = lax.rem(x + dx, X)
        slot = slot_of(lax.rem(zl + dz, 2), at)
        t, j = lax.div(at, 2), 2 * lax.rem(at, 2) + lax.div(slot, X)
        rows = k_all[slot]
        for b in range(2):
            depth = jnp.concatenate([s_all[b, 2 * j, t], s_all[b, 2 * j + 1, t]], axis=0)
            total[b] += jnp.dot(rows, depth, preferred_element_type=F32)

    total[...] = jnp.zeros_like(total)
    for dz, dx in ((0, 0), (1, 0), (0, X - ahead)):
        by_block(dz, dx)
    for dz, dx in ((0, ahead), (1, 1), (1, X - 1), (0, 2), (1, 2)):
        line_wait(k_all, k_sems, dz, dx)
        by_block(dz, dx)

    kept_b = jnp.where(mine, 0, 1)
    part_send[...] = total[1 - kept_b].astype(BF16)
    part_copy = copy(part_send, part2_in, b_send_sem, b_recv_sem, (pair * Y + y, c))
    part_copy.start()

    @pl.when(moved)
    def _():
        f_move.wait_send()
        filt_move.wait_send()

    mate_copy(p_all, p_mate_sem, low).wait_send()
    mate_copy(s_all, s_mate_sem, low).wait_send()
    await_sent(p_all.at[0, pl.ds(0, Y - 1)], p_send_sem)
    await_sent(s_all.at[0, pl.ds(0, Y - 1)], s_send_sem)
    await_sent(p_all.at[0], p_over_sem)
    await_sent(s_all.at[0], s_over_sem)
    await_sent(f_all.at[pl.ds(0, 2 * X - 1)], f_send_sem)
    await_sent(k_all.at[pl.ds(0, 2 * X - 1)], k_send_sem)

    @pl.when(away)
    def _():
        await_sent(far_send, a_send_sem.at[1])

    @pl.when(home)
    def _():
        near_copy().wait_send()

    block_row = jnp.where(mine, r, pair * Y + y)
    block_col = c - core + kept_b
    own_here = jnp.logical_and(low == 0, core == 0)
    own_comes = jnp.logical_not(own_here)
    own_sent = jnp.logical_not(jnp.logical_and(mine, core == 0))
    block_copy = copy(block_send, block_in, o_send_sem, o_recv_sem, (block_row, block_col))

    def tile_stays(h):
        return jnp.logical_and(2 * block_col + h == r, lax.div(block_row, 2) == c)

    def tile_copy(h):
        at = lax.rem(block_row, 2)
        return copy(
            tile_send.at[h], tile_in.at[at], x_send_sem.at[h], x_recv_sem.at[at], (2 * block_col + h, lax.div(block_row, 2))
        )

    def tile_is_here(b):
        row, col = 2 * c + b, lax.div(r, 2)
        z = lax.div(row, Y)
        z_low, second = lax.rem(z, 2), lax.rem(col, 2)
        z_at = z + second * (1 - 2 * z_low)
        return jnp.logical_and(z_at * Y + lax.rem(row, Y) == r, col - second + z_low == c)

    part_copy.wait_recv()
    rounded = (total[kept_b] + part2_in[...].astype(F32)).astype(BF16)
    for h in range(2):
        tile_send[h] = rounded[:, 128 * h : 128 * (h + 1)]

        @pl.when(jnp.logical_not(tile_stays(h)))
        def _():
            tile_copy(h).start()

        @pl.when(tile_stays(h))
        def _():
            tile_in[lax.rem(block_row, 2)] = tile_send[h]

    block_send[...] = rounded

    @pl.when(own_sent)
    def _():
        block_copy.start()

    @pl.when(own_here)
    def _():
        block_in[...] = rounded

    part_copy.wait_send()

    @pl.when(own_comes)
    def _():
        await_recv(block_in, o_recv_sem)

    for b in range(2):
        here = slice(128 * b, 128 * (b + 1))

        @pl.when(jnp.logical_not(tile_is_here(b)))
        def _():
            await_recv(tile_in.at[b], x_recv_sem.at[b])

        out_ref[:, here] = block_in[:, here].astype(F32) - tile_in[b].astype(F32).T

    @pl.when(own_sent)
    def _():
        block_copy.wait_send()

    for h in range(2):

        @pl.when(jnp.logical_not(tile_stays(h)))
        def _():
            tile_copy(h).wait_send()


def per_device(fock, density, intersection, fock_mask, density_mask, intersection_mask, product_filter):
    operands = fock, density, intersection, fock_mask, density_mask, intersection_mask, product_filter
    operands = [pltpu.with_memory_space_constraint(one, pltpu.HBM) for one in operands]
    hbm = pl.BlockSpec(memory_space=pltpu.HBM)
    vmem = pl.BlockSpec(memory_space=pltpu.VMEM)
    dma = pltpu.SemaphoreType.DMA
    block = (128, 256)
    return pl.pallas_call(
        kernel,
        out_shape=jax.ShapeDtypeStruct(block, F32),
        in_specs=[hbm] * 7,
        out_specs=vmem,
        scratch_shapes=[pltpu.VMEM(block, BF16)] * 3
        + [pltpu.SMEM((1, 2), jnp.int32)] * 4
        + [
            dma((7,)),
            pltpu.VMEM(block, BF16),
            pltpu.VMEM((2 * X,) + block, BF16),
            pltpu.VMEM((2 * X,) + block, BF16),
            pltpu.VMEM((2, Y, 2) + block, BF16),
            pltpu.VMEM((2, Y, 2) + block, BF16),
            pltpu.VMEM((8, 256), F32),
            pltpu.VMEM((8, 256), F32),
            pltpu.VMEM(block, F32),
            pltpu.VMEM(block, F32),
            pltpu.VMEM((2,) + block, FAR),
            pltpu.VMEM(block, FAR),
            pltpu.VMEM((2,) + block, F32),
            pltpu.VMEM(block, BF16),
            pltpu.VMEM(block, BF16),
            pltpu.VMEM(block, BF16),
            pltpu.VMEM(block, BF16),
            pltpu.VMEM((2, 128, 128), BF16),
            pltpu.VMEM((2, 128, 128), BF16),
            dma((2,)), dma((2,)),
            dma, dma((2, Y + 2)), dma, dma((Y,)), dma((2,)),
            dma, dma((2, Y + 2)), dma, dma((Y,)), dma((2,)),
            dma, dma((2 * X,)), dma, dma((2 * X,)),
            dma((2,)), dma((2,)), dma, dma, dma, dma,
            dma((2,)), dma((2,)),
        ],
        compiler_params=pltpu.CompilerParams(
            collective_id=0, has_side_effects=True, vmem_limit_bytes=32 * 1024 * 1024
        ),
        cost_estimate=pl.CostEstimate(flops=2 * 2 * 512 * 1024 * 256, bytes_accessed=6 * 1024 * 1024, transcendentals=0),
    )(*operands)


def solution(mesh):
    spec = P("row", "col")
    return jax.shard_map(
        per_device, mesh=mesh, in_specs=(spec,) * 7, out_specs=spec, check_vma=False
    )
```

```python
import jax
import jax.numpy as jnp
from jax import lax
from jax.experimental import pallas as pl
from jax.experimental.pallas import tpu as pltpu
from jax.sharding import PartitionSpec as P

MESH = pl.DeviceIdType.MESH
Z, Y, J = 4, 8, 4
X = 4
BF16, F32 = jnp.bfloat16, jnp.float32
FAR = BF16


def masked(block, mask_ref):
    lane = lax.broadcasted_iota(jnp.int32, block.shape, 1)
    keep = jnp.where(lane < block.shape[1] // 2, mask_ref[0, 0], mask_ref[0, 1])
    return (block.astype(F32) * keep.astype(F32)).astype(BF16)


def kernel(
    f_hbm, p_hbm, s_hbm, fm_hbm, pm_hbm, sm_hbm, filt_hbm, out_ref,
    f_ref, p_ref, s_ref, fm_ref, pm_ref, sm_ref, filt_ref, in_sem,
    f_send, f_all, k_all, p_all, s_all, filt_send, filt_here,
    part, near_in, far_send, far_in, total, part_send, part2_in, block_send, block_in, tile_send, tile_in,
    t_send_sem, t_recv_sem,
    p_send_sem, p_recv_sem, p_over_sem, p_core_sem, p_mate_sem,
    s_send_sem, s_recv_sem, s_over_sem, s_core_sem, s_mate_sem,
    f_send_sem, f_recv_sem, k_send_sem, k_recv_sem,
    a_send_sem, a_recv_sem, b_send_sem, b_recv_sem, o_send_sem, o_recv_sem, x_send_sem, x_recv_sem,
):
    r, c = lax.axis_index("row"), lax.axis_index("col")
    zh, y = lax.div(r, Y), lax.rem(r, Y)
    zl, x, core = lax.div(c, 2 * X), lax.rem(lax.div(c, 2), X), lax.rem(c, 2)
    over = (r, c + 1 - 2 * core)
    low = lax.rem(zh, 2)
    pair = zh + 1 - 2 * low
    mate = Z - 1 - zh
    half = lax.rem(lax.div(zh, 2) + low, 2)
    x_high = lax.div(x, 2)
    home = lax.rem(zl + x_high, 2) == half
    away = lax.rem(zl + x_high, 2) != half
    home_row = jnp.where(home, r, pair * Y + y)
    ahead = jnp.where(core == 0, 1, X - 1)

    def holder(l, k):
        return lax.rem(zl + l, 2) * (2 * X) + x * 2 + k

    def slot_of(z_low, at):
        return X * lax.rem(z_low + lax.div(at, 2) + half, 2) + at

    held_z = 2 * lax.div(zh, 2) + core
    held_zl = lax.rem(x_high + half, 2)
    held_l = lax.rem(zl + held_zl, 2)
    held_from = (held_z * Y + y, held_zl * (2 * X) + x * 2 + held_l)
    term_col = held_zl * (2 * X) + x * 2 + core
    move_to = (home_row, holder(core, low))
    stays = jnp.logical_and(home, jnp.logical_and(core == 0, low == 0))
    moved = jnp.logical_not(stays)
    mine = low == core

    def ring(d):
        return zh * Y + lax.rem(y + d, Y)

    def on_line(dz, dx):
        return lax.rem(zl + dz, 2) * (2 * X) + lax.rem(x + dx, X) * 2 + core

    def copy(src, dst, send, recv, to):
        return pltpu.make_async_remote_copy(
            src_ref=src, dst_ref=dst, send_sem=send, recv_sem=recv, device_id=to, device_id_type=MESH
        )

    def await_sent(ref, sem):
        copy(ref, ref, sem, sem, over).wait_send()

    def await_recv(ref, sem):
        copy(ref, ref, sem, sem, over).wait_recv()

    fetches = []
    for n, (src, dst) in enumerate((
        (f_hbm, f_ref), (fm_hbm, fm_ref), (p_hbm, p_ref), (pm_hbm, pm_ref),
        (filt_hbm, filt_ref), (s_hbm, s_ref), (sm_hbm, sm_ref),
    )):
        fetches.append(pltpu.make_async_copy(src, dst, in_sem.at[n]))
        fetches[-1].start()

    barrier = pltpu.get_barrier_semaphore()

    def greet(to):
        pl.semaphore_signal(barrier, inc=1, device_id=to, device_id_type=MESH)

    @pl.when(moved)
    def _():
        greet(held_from)

    greet((mate * Y + y, c))
    for d in (2, 6, 1, 7):
        greet((ring(d), c))
    for dz, dx in ((1, 0), (0, 1), (0, X - 1)):
        greet((r, on_line(dz, dx)))
    greet(over)
    greet((pair * Y + y, term_col))

    @pl.when(away)
    def _():
        greet((r, term_col))

    for one in fetches[:5]:
        one.wait()
    f_send[...] = masked(f_ref[...], fm_ref)
    p_all[core, y, low] = masked(p_ref[...], pm_ref)
    lane = lax.broadcasted_iota(jnp.int32, filt_send.shape, 1)
    filt_send[...] = jnp.where(lane < 128, filt_ref[0, 0], filt_ref[0, 1]).astype(F32)

    pl.semaphore_wait(barrier, jnp.where(moved, 1, 0) + 1 + 4 + 3 + 1 + 1 + jnp.where(away, 1, 0))

    my_slot = slot_of(zl, x)
    f_move = copy(f_send, f_all.at[X * core + x], t_send_sem.at[0], t_recv_sem.at[0], move_to)
    filt_move = copy(filt_send, filt_here, t_send_sem.at[1], t_recv_sem.at[1], move_to)

    @pl.when(moved)
    def _():
        f_move.start()
        filt_move.start()

    def mate_copy(buf, sem, t):
        ref = buf.at[core, y, t]
        return copy(ref, ref, sem.at[0], sem.at[1], (mate * Y + y, c))

    def ring_ref(buf, sems, src, t, part_of):
        slot = lax.rem(y + src, Y)
        at = Y + part_of if part_of is not None else slot
        if t is None:
            ref = buf.at[core, slot] if part_of is None else buf.at[core, slot, part_of]
            return ref, sems[1].at[0, at]
        ref = buf.at[core, slot, t] if part_of is None else buf.at[core, slot, t, pl.ds(64 * part_of, 64)]
        return ref, sems[1].at[t, at]

    def ring_send(buf, sems, src, t, d, part_of=None):
        ref, recv = ring_ref(buf, sems, src, t, part_of)
        copy(ref, ref, sems[0], recv, (ring(d), c)).start()

    def ring_wait(buf, sems, src, t, part_of=None):
        await_recv(*ring_ref(buf, sems, src, t, part_of))

    def ring_start(buf, sems, t):
        for d in (2, 6, 1, 7):
            ring_send(buf, sems, 0, t, d)

    def ring_relay(buf, sems, t):
        for src, on, far, part_of in ((6, 1, 2, 0), (2, 7, 6, 1)):
            ring_wait(buf, sems, src, t)
            ring_send(buf, sems, src, t, on)
            ring_send(buf, sems, src, t, far, part_of)

    def cross(buf, sems, src):
        at = lax.rem(y + src, Y)
        ref = buf.at[core, at]
        copy(ref, ref, sems[2], sems[3].at[at], over).start()

    def cross_wait(buf, sems, src):
        at = lax.rem(y + src, Y)
        await_recv(buf.at[1 - core, at], sems[3].at[at])

    def ring_last(buf, sems, ts, src):
        for t in ts:
            for part_of in range(2) if src == 4 else (None,):
                ring_wait(buf, sems, src, t, part_of)
        cross(buf, sems, src)

    p_sems = (p_send_sem, p_recv_sem, p_over_sem, p_core_sem)
    s_sems = (s_send_sem, s_recv_sem, s_over_sem, s_core_sem)
    mate_copy(p_all, p_mate_sem, low).start()
    ring_start(p_all, p_sems, low)

    def line_send(buf, sems, dz, dx, to):
        slot = slot_of(lax.rem(zl + dz, 2), lax.rem(x + dx, X))
        ref = buf.at[slot]
        copy(ref, ref, sems[0], sems[1].at[slot], (r, to)).start()

    def line_wait(buf, sems, dz, dx):
        slot = slot_of(lax.rem(zl + dz, 2), lax.rem(x + dx, X))
        await_recv(buf.at[slot], sems[1].at[slot])

    def line_start(buf, sems):
        for to in (on_line(1, 0), on_line(0, ahead), on_line(0, X - ahead)):
            line_send(buf, sems, 0, 0, to)

    def line_relay(buf, sems):
        line_wait(buf, sems, 1, 0)
        line_send(buf, sems, 1, 0, on_line(0, 1))
        line_send(buf, sems, 1, 0, on_line(0, X - 1))
        line_wait(buf, sems, 0, X - ahead)
        line_send(buf, sems, 0, X - ahead, on_line(0, ahead))
        line_send(buf, sems, 0, X - ahead, on_line(1, ahead))

    def line_finish(buf, sems):
        for dz, dx in ((0, ahead), (1, 1), (1, X - 1), (0, 2), (1, 2)):
            line_wait(buf, sems, dz, dx)

    f_sems, k_sems = (f_send_sem, f_recv_sem), (k_send_sem, k_recv_sem)
    mate_copy(p_all, p_mate_sem, 1 - low).wait_recv()
    ring_start(p_all, p_sems, 1 - low)

    @pl.when(moved)
    def _():
        await_recv(f_all.at[my_slot], t_recv_sem.at[0])

    @pl.when(stays)
    def _():
        f_all[my_slot] = f_send[...]

    line_start(f_all, f_sems)
    cross(p_all, p_sems, 0)

    for one in fetches[5:]:
        one.wait()
    s_all[core, y, low] = masked(s_ref[...], sm_ref)
    mate_copy(s_all, s_mate_sem, low).start()

    ring_relay(p_all, p_sems, low)
    line_relay(f_all, f_sems)
    ring_relay(p_all, p_sems, 1 - low)
    cross(p_all, p_sems, 2)
    cross(p_all, p_sems, 6)
    mate_copy(s_all, s_mate_sem, 1 - low).wait_recv()
    ring_start(s_all, s_sems, None)
    line_finish(f_all, f_sems)

    def at_place(b, src):
        place = lax.rem(y + src, Y)
        j = lax.div(place, 2)
        lanes = pl.ds(pl.multiple_of(128 * lax.rem(place, 2), 128), 128)
        total = None
        for t in range(2):
            rows = f_all[X * lax.rem(j, 2) + 2 * t + lax.div(j, 2), :, lanes]
            term = jnp.dot(rows, p_all[b, place, t], preferred_element_type=F32)
            total = term if total is None else total + term
        return total

    def near_copy():
        return copy(part, near_in, a_send_sem.at[0], a_recv_sem.at[0], (r, holder(1, core)))

    def send_first(b, term):
        @pl.when(away)
        def _():
            far_send[b] = term.astype(FAR)
            copy(
                far_send.at[b], far_in, a_send_sem.at[1], a_recv_sem.at[1], (pair * Y + y, holder(b, core))
            ).start()

        @pl.when(jnp.logical_and(home, b == 0))
        def _():
            near_in[...] = term

        @pl.when(jnp.logical_and(home, b == 1))
        def _():
            part[...] = term
            near_copy().start()

    term = at_place(core, 0) + at_place(core, 2) + at_place(core, 6)
    for src in (1, 7, 5, 3, 4):
        ring_last(p_all, p_sems, (low, 1 - low), src)
        term = term + at_place(core, src)
    send_first(core, term)

    term = None
    for src in (0, 2, 6, 1, 7, 5, 3, 4):
        cross_wait(p_all, p_sems, src)
        one = at_place(1 - core, src)
        term = one if term is None else term + one
    send_first(1 - core, term)

    @pl.when(moved)
    def _():
        filt_move.wait_recv()

    @pl.when(stays)
    def _():
        filt_here[...] = filt_send[...]

    ring_relay(s_all, s_sems, None)
    for src in (0, 2, 6):
        cross(s_all, s_sems, src)

    @pl.when(away)
    def _():
        await_recv(near_in, a_recv_sem.at[0])

    await_recv(far_in, a_recv_sem.at[1])
    k_all[my_slot] = ((near_in[...] + far_in[...].astype(F32)) * filt_here[0:1, :]).astype(BF16)
    line_start(k_all, k_sems)
    line_relay(k_all, k_sems)
    for src in (1, 7, 5, 3, 4):
        ring_last(s_all, s_sems, (None,), src)
    for src in range(Y):
        cross_wait(s_all, s_sems, src)

    def by_block(dz, dx):
        at = lax.rem(x + dx, X)
        slot = slot_of(lax.rem(zl + dz, 2), at)
        t, j = lax.div(at, 2), 2 * lax.rem(at, 2) + lax.div(slot, X)
        rows = k_all[slot]
        for b in range(2):
            depth = jnp.concatenate([s_all[b, 2 * j, t], s_all[b, 2 * j + 1, t]], axis=0)
            total[b] += jnp.dot(rows, depth, preferred_element_type=F32)

    total[...] = jnp.zeros_like(total)
    for dz, dx in ((0, 0), (1, 0), (0, X - ahead)):
        by_block(dz, dx)
    for dz, dx in ((0, ahead), (1, 1), (1, X - 1), (0, 2), (1, 2)):
        line_wait(k_all, k_sems, dz, dx)
        by_block(dz, dx)

    odd = lax.rem(y, 2)
    kept_b = jnp.where(mine, odd, 1 - odd)
    part_send[...] = total[1 - kept_b].astype(BF16)
    part_copy = copy(part_send, part2_in, b_send_sem, b_recv_sem, (pair * Y + y, c))
    part_copy.start()

    @pl.when(moved)
    def _():
        f_move.wait_send()
        filt_move.wait_send()

    mate_copy(p_all, p_mate_sem, low).wait_send()
    mate_copy(s_all, s_mate_sem, low).wait_send()
    await_sent(p_all.at[0, pl.ds(0, Y - 1)], p_send_sem)
    await_sent(s_all.at[0, pl.ds(0, Y - 1)], s_send_sem)
    await_sent(p_all.at[0], p_over_sem)
    await_sent(s_all.at[0], s_over_sem)
    await_sent(f_all.at[pl.ds(0, 2 * X - 1)], f_send_sem)
    await_sent(k_all.at[pl.ds(0, 2 * X - 1)], k_send_sem)

    @pl.when(away)
    def _():
        await_sent(far_send, a_send_sem.at[1])

    @pl.when(home)
    def _():
        near_copy().wait_send()

    block_row = jnp.where(mine, r, pair * Y + y)
    block_col = c - core + kept_b
    own_here = jnp.logical_and(low == core, core == odd)
    own_comes = jnp.logical_not(own_here)
    own_sent = own_comes
    block_copy = copy(block_send, block_in, o_send_sem, o_recv_sem, (block_row, block_col))

    def tile_stays(h):
        return jnp.logical_and(2 * block_col + h == r, lax.div(block_row, 2) == c)

    def tile_copy(h):
        at = lax.rem(block_row, 2)
        return copy(
            tile_send.at[h], tile_in.at[at], x_send_sem.at[h], x_recv_sem.at[at], (2 * block_col + h, lax.div(block_row, 2))
        )

    def tile_is_here(b):
        row, col = 2 * c + b, lax.div(r, 2)
        z = lax.div(row, Y)
        z_low, second = lax.rem(z, 2), lax.rem(col, 2)
        away_by = lax.rem(second + lax.rem(row, 2), 2)
        z_at = z + away_by * (1 - 2 * z_low)
        return jnp.logical_and(z_at * Y + lax.rem(row, Y) == r, col - second + z_low == c)

    part_copy.wait_recv()
    rounded = (total[kept_b] + part2_in[...].astype(F32)).astype(BF16)
    for h in range(2):
        tile_send[h] = rounded[:, 128 * h : 128 * (h + 1)]

        @pl.when(jnp.logical_not(tile_stays(h)))
        def _():
            tile_copy(h).start()

        @pl.when(tile_stays(h))
        def _():
            tile_in[lax.rem(block_row, 2)] = tile_send[h]

    block_send[...] = rounded

    @pl.when(own_sent)
    def _():
        block_copy.start()

    @pl.when(own_here)
    def _():
        block_in[...] = rounded

    part_copy.wait_send()

    @pl.when(own_comes)
    def _():
        await_recv(block_in, o_recv_sem)

    for b in range(2):
        here = slice(128 * b, 128 * (b + 1))

        @pl.when(jnp.logical_not(tile_is_here(b)))
        def _():
            await_recv(tile_in.at[b], x_recv_sem.at[b])

        out_ref[:, here] = block_in[:, here].astype(F32) - tile_in[b].astype(F32).T

    @pl.when(own_sent)
    def _():
        block_copy.wait_send()

    for h in range(2):

        @pl.when(jnp.logical_not(tile_stays(h)))
        def _():
            tile_copy(h).wait_send()


def per_device(fock, density, intersection, fock_mask, density_mask, intersection_mask, product_filter):
    operands = fock, density, intersection, fock_mask, density_mask, intersection_mask, product_filter
    operands = [pltpu.with_memory_space_constraint(one, pltpu.HBM) for one in operands]
    hbm = pl.BlockSpec(memory_space=pltpu.HBM)
    vmem = pl.BlockSpec(memory_space=pltpu.VMEM)
    dma = pltpu.SemaphoreType.DMA
    block = (128, 256)
    return pl.pallas_call(
        kernel,
        out_shape=jax.ShapeDtypeStruct(block, F32),
        in_specs=[hbm] * 7,
        out_specs=vmem,
        scratch_shapes=[pltpu.VMEM(block, BF16)] * 3
        + [pltpu.SMEM((1, 2), jnp.int32)] * 4
        + [
            dma((7,)),
            pltpu.VMEM(block, BF16),
            pltpu.VMEM((2 * X,) + block, BF16),
            pltpu.VMEM((2 * X,) + block, BF16),
            pltpu.VMEM((2, Y, 2) + block, BF16),
            pltpu.VMEM((2, Y, 2) + block, BF16),
            pltpu.VMEM((8, 256), F32),
            pltpu.VMEM((8, 256), F32),
            pltpu.VMEM(block, F32),
            pltpu.VMEM(block, F32),
            pltpu.VMEM((2,) + block, FAR),
            pltpu.VMEM(block, FAR),
            pltpu.VMEM((2,) + block, F32),
            pltpu.VMEM(block, BF16),
            pltpu.VMEM(block, BF16),
            pltpu.VMEM(block, BF16),
            pltpu.VMEM(block, BF16),
            pltpu.VMEM((2, 128, 128), BF16),
            pltpu.VMEM((2, 128, 128), BF16),
            dma((2,)), dma((2,)),
            dma, dma((2, Y + 2)), dma, dma((Y,)), dma((2,)),
            dma, dma((2, Y + 2)), dma, dma((Y,)), dma((2,)),
            dma, dma((2 * X,)), dma, dma((2 * X,)),
            dma((2,)), dma((2,)), dma, dma, dma, dma,
            dma((2,)), dma((2,)),
        ],
        compiler_params=pltpu.CompilerParams(
            collective_id=0, has_side_effects=True, vmem_limit_bytes=32 * 1024 * 1024
        ),
        cost_estimate=pl.CostEstimate(flops=2 * 2 * 512 * 1024 * 256, bytes_accessed=6 * 1024 * 1024, transcendentals=0),
    )(*operands)


def solution(mesh):
    spec = P("row", "col")
    return jax.shard_map(
        per_device, mesh=mesh, in_specs=(spec,) * 7, out_specs=spec, check_vma=False
    )
```

```python
import jax
import jax.numpy as jnp
from jax import lax
from jax.experimental import pallas as pl
from jax.experimental.pallas import tpu as pltpu
from jax.sharding import PartitionSpec as P

MESH = pl.DeviceIdType.MESH
Z, Y, J = 4, 8, 4
X = 4
BF16, F32 = jnp.bfloat16, jnp.float32
FAR = BF16


def masked(block, mask_ref):
    lane = lax.broadcasted_iota(jnp.int32, block.shape, 1)
    keep = jnp.where(lane < block.shape[1] // 2, mask_ref[0, 0], mask_ref[0, 1])
    return (block.astype(F32) * keep.astype(F32)).astype(BF16)


def kernel(
    f_hbm, p_hbm, s_hbm, fm_hbm, pm_hbm, sm_hbm, filt_hbm, out_ref,
    f_ref, p_ref, s_ref, fm_ref, pm_ref, sm_ref, filt_ref, in_sem,
    f_send, p_send, s_send, f_all, k_all, p_all, s_all, filt_send, filt_here,
    share, share_in, share2, share2_in, near_send, near_in, far_send, far_in, total, part_send, part2_in, block_send, block_in, tile_send, tile_in,
    t_send_sem, t_recv_sem,
    p_send_sem, p_recv_sem, p_out_sem, p_in_sem, s_send_sem, s_recv_sem, s_out_sem, s_in_sem, share_sem, share2_sem,
    f_send_sem, f_recv_sem, k_send_sem, k_recv_sem,
    a_send_sem, far_sem, a_recv_sem, b_send_sem, b_recv_sem, o_send_sem, o_recv_sem, x_send_sem, x_recv_sem,
):
    r, c = lax.axis_index("row"), lax.axis_index("col")
    zh, y = lax.div(r, Y), lax.rem(r, Y)
    zl, x, core = lax.div(c, 2 * X), lax.rem(lax.div(c, 2), X), lax.rem(c, 2)
    over = (r, c + 1 - 2 * core)
    low = lax.rem(zh, 2)
    pair = zh + 1 - 2 * low
    mate = Z - 1 - zh
    half = lax.rem(lax.div(zh, 2) + low, 2)
    x_high = lax.div(x, 2)
    home = lax.rem(zl + x_high, 2) == half
    away = lax.rem(zl + x_high, 2) != half
    home_row = jnp.where(home, r, pair * Y + y)
    ahead = jnp.where(core == 0, 1, X - 1)

    def holder(l, k):
        at = jnp.where(k == x_high, x, X - 1 - x)
        return lax.rem(zl + l, 2) * (2 * X) + at * 2 + x_high

    def number(k, at, l):
        return J * k + 2 * at + l

    depth_zl = lax.rem(half + core, 2)

    def slot_of(z_low, at):
        k = lax.div(at, 2)
        return number(k, jnp.where(k == core, lax.rem(at, 2), 1 - lax.rem(at, 2)), lax.rem(z_low + depth_zl, 2))

    held_k = x_high
    held_z = 2 * lax.div(zh, 2) + held_k
    held_x = jnp.where(held_k == core, x, X - 1 - x)
    held_l = lax.rem(zl + depth_zl, 2)
    held_from = (held_z * Y + y, depth_zl * (2 * X) + held_x * 2 + held_l)
    term_col = depth_zl * (2 * X) + held_x * 2 + held_k
    near_here = jnp.logical_and(held_l == 0, held_k == core)
    near_comes = jnp.logical_not(near_here)
    move_to = (home_row, holder(core, low))
    stays = jnp.logical_and(jnp.logical_and(home, core == 0), jnp.logical_and(x_high == 0, low == 0))
    moved = jnp.logical_not(stays)
    mine = low == core
    others = low != core

    def ring(d):
        return zh * Y + lax.rem(y + d, Y)

    def on_line(dz, dx):
        return lax.rem(zl + dz, 2) * (2 * X) + lax.rem(x + dx, X) * 2 + core

    def copy(src, dst, send, recv, to):
        return pltpu.make_async_remote_copy(
            src_ref=src, dst_ref=dst, send_sem=send, recv_sem=recv, device_id=to, device_id_type=MESH
        )

    def await_sent(ref, sem):
        copy(ref, ref, sem, sem, over).wait_send()

    def await_recv(ref, sem):
        copy(ref, ref, sem, sem, over).wait_recv()

    fetches = []
    for n, (src, dst) in enumerate((
        (f_hbm, f_ref), (fm_hbm, fm_ref), (p_hbm, p_ref), (pm_hbm, pm_ref),
        (filt_hbm, filt_ref), (s_hbm, s_ref), (sm_hbm, sm_ref),
    )):
        fetches.append(pltpu.make_async_copy(src, dst, in_sem.at[n]))
        fetches[-1].start()

    barrier = pltpu.get_barrier_semaphore()

    def greet(to):
        pl.semaphore_signal(barrier, inc=1, device_id=to, device_id_type=MESH)

    @pl.when(moved)
    def _():
        greet(held_from)

    @pl.when(others)
    def _():
        greet((mate * Y + y, c))
        greet((mate * Y + y, c + 1 - 2 * core))

    for d in (2, 6, 1, 7):
        greet((ring(d), c))
    for dz, dx in ((1, 0), (0, 1), (0, X - 1)):
        greet((r, on_line(dz, dx)))
    greet(over)
    greet((pair * Y + y, term_col))

    @pl.when(near_comes)
    def _():
        greet((r, term_col))

    for one in fetches[:5]:
        one.wait()
    f_send[...] = masked(f_ref[...], fm_ref)
    p_send[...] = masked(p_ref[...], pm_ref)
    lane = lax.broadcasted_iota(jnp.int32, filt_send.shape, 1)
    filt_send[...] = jnp.where(lane < 128, filt_ref[0, 0], filt_ref[0, 1]).astype(F32)

    near_sends = jnp.where(core == x_high, 1, 2)
    pl.semaphore_wait(barrier, jnp.where(moved, 1, 0) + 1 + 1 + 4 + 3 + jnp.where(home, near_sends, 2))

    my_slot = slot_of(zl, x)
    f_move = copy(f_send, f_all.at[number(low, lax.rem(x, 2), core)], t_send_sem.at[0], t_recv_sem.at[0], move_to)
    filt_move = copy(filt_send, filt_here, t_send_sem.at[1], t_recv_sem.at[1], move_to)

    @pl.when(moved)
    def _():
        f_move.start()
        filt_move.start()

    def spread(src, buf, sems):
        to_over = copy(src, buf.at[y, core], sems[2].at[0], sems[3].at[core], over)
        to_mate = copy(src, buf.at[y, core], sems[2].at[1], sems[3].at[core], (mate * Y + y, c - core + low))
        to_mate.start()

        @pl.when(others)
        def _():
            to_over.start()

        @pl.when(mine)
        def _():
            buf[y, core] = src[...]

    def spread_wait(buf, sems):
        await_recv(buf.at[y, 1 - core], sems[3].at[1 - core])

        @pl.when(others)
        def _():
            await_recv(buf.at[y, core], sems[3].at[core])

    def spread_sent(src, sems):
        await_sent(src, sems[2].at[1])

        @pl.when(others)
        def _():
            await_sent(src, sems[2].at[0])

    def ring_ref(buf, sems, src, part_of):
        slot = lax.rem(y + src, Y)
        if part_of is None:
            return buf.at[slot], sems[1].at[slot]
        return buf.at[slot, part_of], sems[1].at[Y + part_of]

    def ring_send(buf, sems, src, d, part_of=None):
        ref, recv = ring_ref(buf, sems, src, part_of)
        copy(ref, ref, sems[0], recv, (ring(d), c)).start()

    def ring_wait(buf, sems, src, part_of=None):
        await_recv(*ring_ref(buf, sems, src, part_of))

    def ring_start(buf, sems):
        for d in (2, 6, 1, 7):
            ring_send(buf, sems, 0, d)

    def ring_relay(buf, sems):
        for src, on, far, part_of in ((6, 1, 2, 0), (2, 7, 6, 1)):
            ring_wait(buf, sems, src)
            ring_send(buf, sems, src, on)
            ring_send(buf, sems, src, far, part_of)

    def ring_last(buf, sems, src):
        for part_of in range(2) if src == 4 else (None,):
            ring_wait(buf, sems, src, part_of)

    p_sems = (p_send_sem, p_recv_sem, p_out_sem, p_in_sem)
    s_sems = (s_send_sem, s_recv_sem, s_out_sem, s_in_sem)
    spread(p_send, p_all, p_sems)

    def line_send(buf, sems, dz, dx, to):
        slot = slot_of(lax.rem(zl + dz, 2), lax.rem(x + dx, X))
        ref = buf.at[slot]
        copy(ref, ref, sems[0], sems[1].at[slot], (r, to)).start()

    def line_wait(buf, sems, dz, dx):
        slot = slot_of(lax.rem(zl + dz, 2), lax.rem(x + dx, X))
        await_recv(buf.at[slot], sems[1].at[slot])

    def line_start(buf, sems):
        for to in (on_line(1, 0), on_line(0, ahead), on_line(0, X - ahead)):
            line_send(buf, sems, 0, 0, to)

    def line_relay(buf, sems):
        line_wait(buf, sems, 1, 0)
        line_send(buf, sems, 1, 0, on_line(0, 1))
        line_send(buf, sems, 1, 0, on_line(0, X - 1))
        line_wait(buf, sems, 0, X - ahead)
        line_send(buf, sems, 0, X - ahead, on_line(0, ahead))
        line_send(buf, sems, 0, X - ahead, on_line(1, ahead))

    def line_finish(buf, sems):
        for dz, dx in ((0, ahead), (1, 1), (1, X - 1), (0, 2), (1, 2)):
            line_wait(buf, sems, dz, dx)

    f_sems, k_sems = (f_send_sem, f_recv_sem), (k_send_sem, k_recv_sem)
    spread_wait(p_all, p_sems)
    ring_start(p_all, p_sems)

    @pl.when(moved)
    def _():
        await_recv(f_all.at[my_slot], t_recv_sem.at[0])

    @pl.when(stays)
    def _():
        f_all[my_slot] = f_send[...]

    line_start(f_all, f_sems)

    for one in fetches[5:]:
        one.wait()
    s_send[...] = masked(s_ref[...], sm_ref)
    spread(s_send, s_all, s_sems)
    line_relay(f_all, f_sems)
    ring_relay(p_all, p_sems)
    spread_wait(s_all, s_sems)
    ring_start(s_all, s_sems)
    line_finish(f_all, f_sems)

    def at_place(src):
        place = lax.rem(y + src, Y)
        j = lax.div(place, 2)
        lanes = pl.ds(pl.multiple_of(128 * lax.rem(place, 2), 128), 128)
        rows = jnp.concatenate([f_all[J * k + j, :, lanes] for k in range(2)], axis=0)
        for b in range(2):
            term = jnp.dot(rows, p_all[place, b], preferred_element_type=F32).reshape(2, 128, 256)
            for k in range(2):
                if src == 0:
                    share[k, b] = term[k]
                else:
                    share[k, b] += term[k]

    def share_copy(buf, into, sem):
        return copy(buf.at[1 - core], into, sem.at[0], sem.at[1], over)

    def near_copy(b):
        return copy(near_send.at[b], near_in, a_send_sem.at[b], a_recv_sem.at[0], (r, holder(b, core)))

    def far_copy(b):
        return copy(far_send.at[b], far_in, far_sem, a_recv_sem.at[1], (pair * Y + y, holder(b, core)))

    def send_first(b, term):
        @pl.when(away)
        def _():
            far_send[b] = term.astype(FAR)
            far_copy(b).start()

        if b == 1:

            @pl.when(home)
            def _():
                near_send[b] = term
                near_copy(b).start()

        else:

            @pl.when(jnp.logical_and(home, core == x_high))
            def _():
                near_in[...] = term

            @pl.when(jnp.logical_and(home, core != x_high))
            def _():
                near_send[b] = term
                near_copy(b).start()

    for src in (0, 2, 6):
        at_place(src)
    for src in (1, 7, 5, 3, 4):
        ring_last(p_all, p_sems, src)
        at_place(src)
    share_copy(share, share_in, share_sem).start()
    await_recv(share_in, share_sem.at[1])
    for b in (1, 0):
        send_first(b, share[core, b] + share_in[b])

    @pl.when(moved)
    def _():
        filt_move.wait_recv()

    @pl.when(stays)
    def _():
        filt_here[...] = filt_send[...]

    ring_relay(s_all, s_sems)

    @pl.when(near_comes)
    def _():
        await_recv(near_in, a_recv_sem.at[0])

    await_recv(far_in, a_recv_sem.at[1])
    k_all[my_slot] = ((near_in[...] + far_in[...].astype(F32)) * filt_here[0:1, :]).astype(BF16)
    line_start(k_all, k_sems)
    line_relay(k_all, k_sems)
    for src in (1, 7, 5, 3, 4):
        ring_last(s_all, s_sems, src)

    def by_block(dz, dx):
        slot = slot_of(lax.rem(zl + dz, 2), lax.rem(x + dx, X))
        k, j = lax.div(slot, J), lax.rem(slot, J)
        rows = k_all[slot]
        for b in range(2):
            depth = jnp.concatenate([s_all[2 * j, b], s_all[2 * j + 1, b]], axis=0)
            share2[k, b] += jnp.dot(rows, depth, preferred_element_type=F32)

    share2[...] = jnp.zeros_like(share2)
    for dz, dx in ((0, 0), (1, 0), (0, X - ahead)):
        by_block(dz, dx)
    for dz, dx in ((0, ahead), (1, 1), (1, X - 1), (0, 2), (1, 2)):
        line_wait(k_all, k_sems, dz, dx)
        by_block(dz, dx)
    share_copy(share2, share2_in, share2_sem).start()
    await_recv(share2_in, share2_sem.at[1])
    total[...] = share2[core] + share2_in[...]

    kept_b = jnp.where(mine, 0, 1)
    part_send[...] = total[1 - kept_b].astype(BF16)
    part_copy = copy(part_send, part2_in, b_send_sem, b_recv_sem, (pair * Y + y, c))
    part_copy.start()

    @pl.when(moved)
    def _():
        f_move.wait_send()
        filt_move.wait_send()

    spread_sent(p_send, p_sems)
    spread_sent(s_send, s_sems)
    await_sent(p_all.at[pl.ds(0, Y - 1)], p_send_sem)
    await_sent(s_all.at[pl.ds(0, Y - 1)], s_send_sem)
    await_sent(share_in, share_sem.at[0])
    await_sent(share2_in, share2_sem.at[0])
    await_sent(f_all.at[pl.ds(0, 2 * X - 1)], f_send_sem)
    await_sent(k_all.at[pl.ds(0, 2 * X - 1)], k_send_sem)

    @pl.when(away)
    def _():
        await_sent(far_send, far_sem)

    @pl.when(home)
    def _():
        near_copy(1).wait_send()

    @pl.when(jnp.logical_and(home, core != x_high))
    def _():
        near_copy(0).wait_send()

    block_row = jnp.where(mine, r, pair * Y + y)
    block_col = c - core + kept_b
    own_here = jnp.logical_and(low == 0, core == 0)
    own_comes = jnp.logical_not(own_here)
    own_sent = jnp.logical_not(jnp.logical_and(mine, core == 0))
    block_copy = copy(block_send, block_in, o_send_sem, o_recv_sem, (block_row, block_col))

    def tile_stays(h):
        return jnp.logical_and(2 * block_col + h == r, lax.div(block_row, 2) == c)

    def tile_copy(h):
        at = lax.rem(block_row, 2)
        return copy(
            tile_send.at[h], tile_in.at[at], x_send_sem.at[h], x_recv_sem.at[at], (2 * block_col + h, lax.div(block_row, 2))
        )

    def tile_is_here(b):
        row, col = 2 * c + b, lax.div(r, 2)
        z = lax.div(row, Y)
        z_low, second = lax.rem(z, 2), lax.rem(col, 2)
        z_at = z + second * (1 - 2 * z_low)
        return jnp.logical_and(z_at * Y + lax.rem(row, Y) == r, col - second + z_low == c)

    part_copy.wait_recv()
    rounded = (total[kept_b] + part2_in[...].astype(F32)).astype(BF16)
    for h in range(2):
        tile_send[h] = rounded[:, 128 * h : 128 * (h + 1)]

        @pl.when(jnp.logical_not(tile_stays(h)))
        def _():
            tile_copy(h).start()

        @pl.when(tile_stays(h))
        def _():
            tile_in[lax.rem(block_row, 2)] = tile_send[h]

    block_send[...] = rounded

    @pl.when(own_sent)
    def _():
        block_copy.start()

    @pl.when(own_here)
    def _():
        block_in[...] = rounded

    part_copy.wait_send()

    @pl.when(own_comes)
    def _():
        await_recv(block_in, o_recv_sem)

    for b in range(2):
        here = slice(128 * b, 128 * (b + 1))

        @pl.when(jnp.logical_not(tile_is_here(b)))
        def _():
            await_recv(tile_in.at[b], x_recv_sem.at[b])

        out_ref[:, here] = block_in[:, here].astype(F32) - tile_in[b].astype(F32).T

    @pl.when(own_sent)
    def _():
        block_copy.wait_send()

    for h in range(2):

        @pl.when(jnp.logical_not(tile_stays(h)))
        def _():
            tile_copy(h).wait_send()


def per_device(fock, density, intersection, fock_mask, density_mask, intersection_mask, product_filter):
    operands = fock, density, intersection, fock_mask, density_mask, intersection_mask, product_filter
    operands = [pltpu.with_memory_space_constraint(one, pltpu.HBM) for one in operands]
    hbm = pl.BlockSpec(memory_space=pltpu.HBM)
    vmem = pl.BlockSpec(memory_space=pltpu.VMEM)
    dma = pltpu.SemaphoreType.DMA
    block = (128, 256)
    return pl.pallas_call(
        kernel,
        out_shape=jax.ShapeDtypeStruct(block, F32),
        in_specs=[hbm] * 7,
        out_specs=vmem,
        scratch_shapes=[pltpu.VMEM(block, BF16)] * 3
        + [pltpu.SMEM((1, 2), jnp.int32)] * 4
        + [
            dma((7,)),
            pltpu.VMEM(block, BF16),
            pltpu.VMEM(block, BF16),
            pltpu.VMEM(block, BF16),
            pltpu.VMEM((2 * X,) + block, BF16),
            pltpu.VMEM((2 * X,) + block, BF16),
            pltpu.VMEM((Y, 2) + block, BF16),
            pltpu.VMEM((Y, 2) + block, BF16),
            pltpu.VMEM((8, 256), F32),
            pltpu.VMEM((8, 256), F32),
            pltpu.VMEM((2, 2) + block, F32),
            pltpu.VMEM((2,) + block, F32),
            pltpu.VMEM((2, 2) + block, F32),
            pltpu.VMEM((2,) + block, F32),
            pltpu.VMEM((2,) + block, F32),
            pltpu.VMEM(block, F32),
            pltpu.VMEM((2,) + block, FAR),
            pltpu.VMEM(block, FAR),
            pltpu.VMEM((2,) + block, F32),
            pltpu.VMEM(block, BF16),
            pltpu.VMEM(block, BF16),
            pltpu.VMEM(block, BF16),
            pltpu.VMEM(block, BF16),
            pltpu.VMEM((2, 128, 128), BF16),
            pltpu.VMEM((2, 128, 128), BF16),
            dma((2,)), dma((2,)),
            dma, dma((Y + 2,)), dma((2,)), dma((2,)),
            dma, dma((Y + 2,)), dma((2,)), dma((2,)),
            dma((2,)), dma((2,)),
            dma, dma((2 * X,)), dma, dma((2 * X,)),
            dma((2,)), dma, dma((2,)), dma, dma, dma, dma,
            dma((2,)), dma((2,)),
        ],
        compiler_params=pltpu.CompilerParams(
            collective_id=0, has_side_effects=True, vmem_limit_bytes=32 * 1024 * 1024
        ),
        cost_estimate=pl.CostEstimate(flops=2 * 2 * 512 * 1024 * 256, bytes_accessed=6 * 1024 * 1024, transcendentals=0),
    )(*operands)


def solution(mesh):
    spec = P("row", "col")
    return jax.shard_map(
        per_device, mesh=mesh, in_specs=(spec,) * 7, out_specs=spec, check_vma=False
    )
```

```python
import jax
import jax.numpy as jnp
from jax import lax
from jax.experimental import pallas as pl
from jax.experimental.pallas import tpu as pltpu
from jax.sharding import PartitionSpec as P

MESH = pl.DeviceIdType.MESH
Z, Y, J = 4, 8, 4
X = 4
BF16, F32 = jnp.bfloat16, jnp.float32
FAR = BF16


def masked(block, mask_ref):
    lane = lax.broadcasted_iota(jnp.int32, block.shape, 1)
    keep = jnp.where(lane < block.shape[1] // 2, mask_ref[0, 0], mask_ref[0, 1])
    return (block.astype(F32) * keep.astype(F32)).astype(BF16)


def kernel(
    f_hbm, p_hbm, s_hbm, fm_hbm, pm_hbm, sm_hbm, filt_hbm, out_ref,
    f_ref, p_ref, s_ref, fm_ref, pm_ref, sm_ref, filt_ref, in_sem,
    f_send, f_all, k_all, p_all, s_all, filt_send, filt_here,
    part, near_in, far_send, far_in, total, part_send, part2_in, block_send, block_in, tile_send, tile_in,
    t_send_sem, t_recv_sem,
    p_send_sem, p_recv_sem, p_over_sem, p_core_sem, p_mate_sem,
    s_send_sem, s_recv_sem, s_over_sem, s_core_sem, s_mate_sem,
    f_send_sem, f_recv_sem, k_send_sem, k_recv_sem,
    a_send_sem, a_recv_sem, b_send_sem, b_recv_sem, o_send_sem, o_recv_sem, x_send_sem, x_recv_sem,
):
    r, c = lax.axis_index("row"), lax.axis_index("col")
    zh, y = lax.div(r, Y), lax.rem(r, Y)
    zl, x, core = lax.div(c, 2 * X), lax.rem(lax.div(c, 2), X), lax.rem(c, 2)
    over = (r, c + 1 - 2 * core)
    low = lax.rem(zh, 2)
    pair = zh + 1 - 2 * low
    mate = Z - 1 - zh
    half = lax.rem(lax.div(zh, 2) + low, 2)
    x_high = lax.div(x, 2)
    home = lax.rem(zl + x_high, 2) == half
    away = lax.rem(zl + x_high, 2) != half
    home_row = jnp.where(home, r, pair * Y + y)
    ahead = jnp.where(core == 0, 1, X - 1)

    def holder(l, k):
        return lax.rem(zl + l, 2) * (2 * X) + x * 2 + k

    def slot_of(z_low, at):
        return X * lax.rem(z_low + lax.div(at, 2) + half, 2) + at

    held_z = 2 * lax.div(zh, 2) + core
    held_zl = lax.rem(x_high + half, 2)
    held_l = lax.rem(zl + held_zl, 2)
    held_from = (held_z * Y + y, held_zl * (2 * X) + x * 2 + held_l)
    term_col = held_zl * (2 * X) + x * 2 + core
    move_to = (home_row, holder(core, low))
    stays = jnp.logical_and(home, jnp.logical_and(core == 0, low == 0))
    moved = jnp.logical_not(stays)
    mine = low == core

    def ring(d):
        return zh * Y + lax.rem(y + d, Y)

    def on_line(dz, dx):
        return lax.rem(zl + dz, 2) * (2 * X) + lax.rem(x + dx, X) * 2 + core

    def copy(src, dst, send, recv, to):
        return pltpu.make_async_remote_copy(
            src_ref=src, dst_ref=dst, send_sem=send, recv_sem=recv, device_id=to, device_id_type=MESH
        )

    def await_sent(ref, sem):
        copy(ref, ref, sem, sem, over).wait_send()

    def await_recv(ref, sem):
        copy(ref, ref, sem, sem, over).wait_recv()

    fetches = []
    for n, (src, dst) in enumerate((
        (f_hbm, f_ref), (fm_hbm, fm_ref), (p_hbm, p_ref), (pm_hbm, pm_ref),
        (filt_hbm, filt_ref), (s_hbm, s_ref), (sm_hbm, sm_ref),
    )):
        fetches.append(pltpu.make_async_copy(src, dst, in_sem.at[n]))
        fetches[-1].start()

    barrier = pltpu.get_barrier_semaphore()

    def greet(to):
        pl.semaphore_signal(barrier, inc=1, device_id=to, device_id_type=MESH)

    @pl.when(moved)
    def _():
        greet(held_from)

    greet((mate * Y + y, c))
    for d in (2, 6):
        greet((mate * Y + lax.rem(y + d, Y), c))
    for d in (2, 6, 1, 7):
        greet((ring(d), c))
    for dz, dx in ((1, 0), (0, 1), (0, X - 1)):
        greet((r, on_line(dz, dx)))
    greet(over)
    greet((pair * Y + y, term_col))

    @pl.when(away)
    def _():
        greet((r, term_col))

    for one in fetches[:5]:
        one.wait()
    f_send[...] = masked(f_ref[...], fm_ref)
    p_all[core, y, low] = masked(p_ref[...], pm_ref)
    lane = lax.broadcasted_iota(jnp.int32, filt_send.shape, 1)
    filt_send[...] = jnp.where(lane < 128, filt_ref[0, 0], filt_ref[0, 1]).astype(F32)

    pl.semaphore_wait(barrier, jnp.where(moved, 1, 0) + 1 + 2 + 4 + 3 + 1 + 1 + jnp.where(away, 1, 0))

    my_slot = slot_of(zl, x)
    f_move = copy(f_send, f_all.at[X * core + x], t_send_sem.at[0], t_recv_sem.at[0], move_to)
    filt_move = copy(filt_send, filt_here, t_send_sem.at[1], t_recv_sem.at[1], move_to)

    @pl.when(moved)
    def _():
        f_move.start()
        filt_move.start()

    def mate_copy(buf, sem, t):
        ref = buf.at[core, y, t]
        return copy(ref, ref, sem.at[0], sem.at[1], (mate * Y + y, c))

    def ring_ref(buf, sems, src, t, part_of):
        slot = lax.rem(y + src, Y)
        at = Y + part_of if part_of is not None else slot
        if t is None:
            ref = buf.at[core, slot] if part_of is None else buf.at[core, slot, part_of]
            return ref, sems[1].at[0, at]
        ref = buf.at[core, slot, t] if part_of is None else buf.at[core, slot, t, pl.ds(64 * part_of, 64)]
        return ref, sems[1].at[t, at]

    def ring_send(buf, sems, src, t, d, part_of=None):
        ref, recv = ring_ref(buf, sems, src, t, part_of)
        copy(ref, ref, sems[0], recv, (ring(d), c)).start()

    def ring_wait(buf, sems, src, t, part_of=None):
        await_recv(*ring_ref(buf, sems, src, t, part_of))

    def ring_start(buf, sems, t, to=(2, 6, 1, 7)):
        for d in to:
            ring_send(buf, sems, 0, t, d)

    def ring_relay(buf, sems, t):
        for src, on, far, part_of in ((6, 1, 2, 0), (2, 7, 6, 1)):
            ring_wait(buf, sems, src, t)
            ring_send(buf, sems, src, t, on)
            ring_send(buf, sems, src, t, far, part_of)

    def cross(buf, sems, src):
        at = lax.rem(y + src, Y)
        ref = buf.at[core, at]
        copy(ref, ref, sems[2], sems[3].at[at], over).start()

    def cross_wait(buf, sems, src):
        at = lax.rem(y + src, Y)
        await_recv(buf.at[1 - core, at], sems[3].at[at])

    def ring_last(buf, sems, ts, src):
        for t in ts:
            for part_of in range(2) if src == 4 else (None,):
                ring_wait(buf, sems, src, t, part_of)
        cross(buf, sems, src)

    p_sems = (p_send_sem, p_recv_sem, p_over_sem, p_core_sem)
    s_sems = (s_send_sem, s_recv_sem, s_over_sem, s_core_sem)
    mate_copy(p_all, p_mate_sem, low).start()
    for d in (2, 6):
        ref, recv = ring_ref(p_all, p_sems, 0, low, None)
        copy(ref, ref, p_send_sem, recv, (mate * Y + lax.rem(y + d, Y), c)).start()
    ring_start(p_all, p_sems, low)

    def line_send(buf, sems, dz, dx, to):
        slot = slot_of(lax.rem(zl + dz, 2), lax.rem(x + dx, X))
        ref = buf.at[slot]
        copy(ref, ref, sems[0], sems[1].at[slot], (r, to)).start()

    def line_wait(buf, sems, dz, dx):
        slot = slot_of(lax.rem(zl + dz, 2), lax.rem(x + dx, X))
        await_recv(buf.at[slot], sems[1].at[slot])

    def line_start(buf, sems):
        for to in (on_line(1, 0), on_line(0, ahead), on_line(0, X - ahead)):
            line_send(buf, sems, 0, 0, to)

    def line_relay(buf, sems):
        line_wait(buf, sems, 1, 0)
        line_send(buf, sems, 1, 0, on_line(0, 1))
        line_send(buf, sems, 1, 0, on_line(0, X - 1))
        line_wait(buf, sems, 0, X - ahead)
        line_send(buf, sems, 0, X - ahead, on_line(0, ahead))
        line_send(buf, sems, 0, X - ahead, on_line(1, ahead))

    def line_finish(buf, sems):
        for dz, dx in ((0, ahead), (1, 1), (1, X - 1), (0, 2), (1, 2)):
            line_wait(buf, sems, dz, dx)

    f_sems, k_sems = (f_send_sem, f_recv_sem), (k_send_sem, k_recv_sem)
    mate_copy(p_all, p_mate_sem, 1 - low).wait_recv()
    ring_start(p_all, p_sems, 1 - low, (1, 7))

    @pl.when(moved)
    def _():
        await_recv(f_all.at[my_slot], t_recv_sem.at[0])

    @pl.when(stays)
    def _():
        f_all[my_slot] = f_send[...]

    line_start(f_all, f_sems)
    cross(p_all, p_sems, 0)

    for one in fetches[5:]:
        one.wait()
    s_all[core, y, low] = masked(s_ref[...], sm_ref)
    mate_copy(s_all, s_mate_sem, low).start()

    ring_relay(p_all, p_sems, low)
    ring_relay(p_all, p_sems, 1 - low)
    line_relay(f_all, f_sems)
    cross(p_all, p_sems, 2)
    cross(p_all, p_sems, 6)
    mate_copy(s_all, s_mate_sem, 1 - low).wait_recv()
    ring_start(s_all, s_sems, None)
    line_finish(f_all, f_sems)

    def at_place(b, src):
        place = lax.rem(y + src, Y)
        j = lax.div(place, 2)
        lanes = pl.ds(pl.multiple_of(128 * lax.rem(place, 2), 128), 128)
        total = None
        for t in range(2):
            rows = f_all[X * lax.rem(j, 2) + 2 * t + lax.div(j, 2), :, lanes]
            term = jnp.dot(rows, p_all[b, place, t], preferred_element_type=F32)
            total = term if total is None else total + term
        return total

    def near_copy():
        return copy(part, near_in, a_send_sem.at[0], a_recv_sem.at[0], (r, holder(1, core)))

    def send_first(b, term):
        @pl.when(away)
        def _():
            far_send[b] = term.astype(FAR)
            copy(
                far_send.at[b], far_in, a_send_sem.at[1], a_recv_sem.at[1], (pair * Y + y, holder(b, core))
            ).start()

        @pl.when(jnp.logical_and(home, b == 0))
        def _():
            near_in[...] = term

        @pl.when(jnp.logical_and(home, b == 1))
        def _():
            part[...] = term
            near_copy().start()

    term = at_place(core, 0) + at_place(core, 2) + at_place(core, 6)
    for src in (1, 7, 5, 3, 4):
        ring_last(p_all, p_sems, (low, 1 - low), src)
        term = term + at_place(core, src)
    send_first(core, term)

    term = None
    for src in (0, 2, 6, 1, 7, 5, 3, 4):
        cross_wait(p_all, p_sems, src)
        one = at_place(1 - core, src)
        term = one if term is None else term + one
    send_first(1 - core, term)

    @pl.when(moved)
    def _():
        filt_move.wait_recv()

    @pl.when(stays)
    def _():
        filt_here[...] = filt_send[...]

    ring_relay(s_all, s_sems, None)
    for src in (0, 2, 6):
        cross(s_all, s_sems, src)

    @pl.when(away)
    def _():
        await_recv(near_in, a_recv_sem.at[0])

    await_recv(far_in, a_recv_sem.at[1])
    k_all[my_slot] = ((near_in[...] + far_in[...].astype(F32)) * filt_here[0:1, :]).astype(BF16)
    line_start(k_all, k_sems)
    line_relay(k_all, k_sems)
    for src in (1, 7, 5, 3, 4):
        ring_last(s_all, s_sems, (None,), src)
    for src in range(Y):
        cross_wait(s_all, s_sems, src)

    def by_block(dz, dx):
        at = lax.rem(x + dx, X)
        slot = slot_of(lax.rem(zl + dz, 2), at)
        t, j = lax.div(at, 2), 2 * lax.rem(at, 2) + lax.div(slot, X)
        rows = k_all[slot]
        for b in range(2):
            depth = jnp.concatenate([s_all[b, 2 * j, t], s_all[b, 2 * j + 1, t]], axis=0)
            total[b] += jnp.dot(rows, depth, preferred_element_type=F32)

    total[...] = jnp.zeros_like(total)
    for dz, dx in ((0, 0), (1, 0), (0, X - ahead)):
        by_block(dz, dx)
    for dz, dx in ((0, ahead), (1, 1), (1, X - 1), (0, 2), (1, 2)):
        line_wait(k_all, k_sems, dz, dx)
        by_block(dz, dx)

    kept_b = jnp.where(mine, 0, 1)
    part_send[...] = total[1 - kept_b].astype(BF16)
    part_copy = copy(part_send, part2_in, b_send_sem, b_recv_sem, (pair * Y + y, c))
    part_copy.start()

    @pl.when(moved)
    def _():
        f_move.wait_send()
        filt_move.wait_send()

    mate_copy(p_all, p_mate_sem, low).wait_send()
    mate_copy(s_all, s_mate_sem, low).wait_send()
    await_sent(p_all.at[0, pl.ds(0, Y - 1)], p_send_sem)
    await_sent(s_all.at[0, pl.ds(0, Y - 1)], s_send_sem)
    await_sent(p_all.at[0], p_over_sem)
    await_sent(s_all.at[0], s_over_sem)
    await_sent(f_all.at[pl.ds(0, 2 * X - 1)], f_send_sem)
    await_sent(k_all.at[pl.ds(0, 2 * X - 1)], k_send_sem)

    @pl.when(away)
    def _():
        await_sent(far_send, a_send_sem.at[1])

    @pl.when(home)
    def _():
        near_copy().wait_send()

    block_row = jnp.where(mine, r, pair * Y + y)
    block_col = c - core + kept_b
    own_here = jnp.logical_and(low == 0, core == 0)
    own_comes = jnp.logical_not(own_here)
    own_sent = jnp.logical_not(jnp.logical_and(mine, core == 0))
    block_copy = copy(block_send, block_in, o_send_sem, o_recv_sem, (block_row, block_col))

    def tile_stays(h):
        return jnp.logical_and(2 * block_col + h == r, lax.div(block_row, 2) == c)

    def tile_copy(h):
        at = lax.rem(block_row, 2)
        return copy(
            tile_send.at[h], tile_in.at[at], x_send_sem.at[h], x_recv_sem.at[at], (2 * block_col + h, lax.div(block_row, 2))
        )

    def tile_is_here(b):
        row, col = 2 * c + b, lax.div(r, 2)
        z = lax.div(row, Y)
        z_low, second = lax.rem(z, 2), lax.rem(col, 2)
        z_at = z + second * (1 - 2 * z_low)
        return jnp.logical_and(z_at * Y + lax.rem(row, Y) == r, col - second + z_low == c)

    part_copy.wait_recv()
    rounded = (total[kept_b] + part2_in[...].astype(F32)).astype(BF16)
    for h in range(2):
        tile_send[h] = rounded[:, 128 * h : 128 * (h + 1)]

        @pl.when(jnp.logical_not(tile_stays(h)))
        def _():
            tile_copy(h).start()

        @pl.when(tile_stays(h))
        def _():
            tile_in[lax.rem(block_row, 2)] = tile_send[h]

    block_send[...] = rounded

    @pl.when(own_sent)
    def _():
        block_copy.start()

    @pl.when(own_here)
    def _():
        block_in[...] = rounded

    part_copy.wait_send()

    @pl.when(own_comes)
    def _():
        await_recv(block_in, o_recv_sem)

    for b in range(2):
        here = slice(128 * b, 128 * (b + 1))

        @pl.when(jnp.logical_not(tile_is_here(b)))
        def _():
            await_recv(tile_in.at[b], x_recv_sem.at[b])

        out_ref[:, here] = block_in[:, here].astype(F32) - tile_in[b].astype(F32).T

    @pl.when(own_sent)
    def _():
        block_copy.wait_send()

    for h in range(2):

        @pl.when(jnp.logical_not(tile_stays(h)))
        def _():
            tile_copy(h).wait_send()


def per_device(fock, density, intersection, fock_mask, density_mask, intersection_mask, product_filter):
    operands = fock, density, intersection, fock_mask, density_mask, intersection_mask, product_filter
    operands = [pltpu.with_memory_space_constraint(one, pltpu.HBM) for one in operands]
    hbm = pl.BlockSpec(memory_space=pltpu.HBM)
    vmem = pl.BlockSpec(memory_space=pltpu.VMEM)
    dma = pltpu.SemaphoreType.DMA
    block = (128, 256)
    return pl.pallas_call(
        kernel,
        out_shape=jax.ShapeDtypeStruct(block, F32),
        in_specs=[hbm] * 7,
        out_specs=vmem,
        scratch_shapes=[pltpu.VMEM(block, BF16)] * 3
        + [pltpu.SMEM((1, 2), jnp.int32)] * 4
        + [
            dma((7,)),
            pltpu.VMEM(block, BF16),
            pltpu.VMEM((2 * X,) + block, BF16),
            pltpu.VMEM((2 * X,) + block, BF16),
            pltpu.VMEM((2, Y, 2) + block, BF16),
            pltpu.VMEM((2, Y, 2) + block, BF16),
            pltpu.VMEM((8, 256), F32),
            pltpu.VMEM((8, 256), F32),
            pltpu.VMEM(block, F32),
            pltpu.VMEM(block, F32),
            pltpu.VMEM((2,) + block, FAR),
            pltpu.VMEM(block, FAR),
            pltpu.VMEM((2,) + block, F32),
            pltpu.VMEM(block, BF16),
            pltpu.VMEM(block, BF16),
            pltpu.VMEM(block, BF16),
            pltpu.VMEM(block, BF16),
            pltpu.VMEM((2, 128, 128), BF16),
            pltpu.VMEM((2, 128, 128), BF16),
            dma((2,)), dma((2,)),
            dma, dma((2, Y + 2)), dma, dma((Y,)), dma((2,)),
            dma, dma((2, Y + 2)), dma, dma((Y,)), dma((2,)),
            dma, dma((2 * X,)), dma, dma((2 * X,)),
            dma((2,)), dma((2,)), dma, dma, dma, dma,
            dma((2,)), dma((2,)),
        ],
        compiler_params=pltpu.CompilerParams(
            collective_id=0, has_side_effects=True, vmem_limit_bytes=32 * 1024 * 1024
        ),
        cost_estimate=pl.CostEstimate(flops=2 * 2 * 512 * 1024 * 256, bytes_accessed=6 * 1024 * 1024, transcendentals=0),
    )(*operands)


def solution(mesh):
    spec = P("row", "col")
    return jax.shard_map(
        per_device, mesh=mesh, in_specs=(spec,) * 7, out_specs=spec, check_vma=False
    )
```

```python
import jax
import jax.numpy as jnp
from jax import lax
from jax.experimental import pallas as pl
from jax.experimental.pallas import tpu as pltpu
from jax.sharding import PartitionSpec as P

MESH = pl.DeviceIdType.MESH
Z, Y, J = 4, 8, 4
X = 4
BF16, F32 = jnp.bfloat16, jnp.float32
FAR = BF16


def masked(block, mask_ref):
    lane = lax.broadcasted_iota(jnp.int32, block.shape, 1)
    keep = jnp.where(lane < block.shape[1] // 2, mask_ref[0, 0], mask_ref[0, 1])
    return (block.astype(F32) * keep.astype(F32)).astype(BF16)


def kernel(
    f_hbm, p_hbm, s_hbm, fm_hbm, pm_hbm, sm_hbm, filt_hbm, out_ref,
    f_ref, p_ref, s_ref, fm_ref, pm_ref, sm_ref, filt_ref, in_sem,
    f_send, f_all, k_all, p_all, s_all, filt_send, filt_here,
    part, near_in, far_send, far_in, total, part_send, part2_in, block_send, block_in, tile_send, tile_in,
    t_send_sem, t_recv_sem,
    p_send_sem, p_recv_sem, p_over_sem, p_core_sem, p_mate_sem,
    s_send_sem, s_recv_sem, s_over_sem, s_core_sem, s_mate_sem,
    f_send_sem, f_recv_sem, k_send_sem, k_recv_sem,
    a_send_sem, a_recv_sem, b_send_sem, b_recv_sem, o_send_sem, o_recv_sem, x_send_sem, x_recv_sem,
):
    r, c = lax.axis_index("row"), lax.axis_index("col")
    zh, y = lax.div(r, Y), lax.rem(r, Y)
    zl, x, core = lax.div(c, 2 * X), lax.rem(lax.div(c, 2), X), lax.rem(c, 2)
    over = (r, c + 1 - 2 * core)
    low = lax.rem(zh, 2)
    pair = zh + 1 - 2 * low
    mate = Z - 1 - zh
    half = lax.rem(lax.div(zh, 2) + low, 2)
    x_high = lax.div(x, 2)
    home = lax.rem(zl + x_high, 2) == half
    away = lax.rem(zl + x_high, 2) != half
    home_row = jnp.where(home, r, pair * Y + y)
    ahead = jnp.where(core == 0, 1, X - 1)

    def holder(l, k):
        return lax.rem(zl + l, 2) * (2 * X) + x * 2 + k

    def slot_of(z_low, at):
        return X * lax.rem(z_low + lax.div(at, 2) + half, 2) + at

    held_z = 2 * lax.div(zh, 2) + core
    held_zl = lax.rem(x_high + half, 2)
    held_l = lax.rem(zl + held_zl, 2)
    held_from = (held_z * Y + y, held_zl * (2 * X) + x * 2 + held_l)
    term_col = held_zl * (2 * X) + x * 2 + core
    move_to = (home_row, holder(core, low))
    stays = jnp.logical_and(home, jnp.logical_and(core == 0, low == 0))
    moved = jnp.logical_not(stays)
    mine = low == core

    def ring(d):
        return zh * Y + lax.rem(y + d, Y)

    def on_line(dz, dx):
        return lax.rem(zl + dz, 2) * (2 * X) + lax.rem(x + dx, X) * 2 + core

    def copy(src, dst, send, recv, to):
        return pltpu.make_async_remote_copy(
            src_ref=src, dst_ref=dst, send_sem=send, recv_sem=recv, device_id=to, device_id_type=MESH
        )

    def await_sent(ref, sem):
        copy(ref, ref, sem, sem, over).wait_send()

    def await_recv(ref, sem):
        copy(ref, ref, sem, sem, over).wait_recv()

    fetches = []
    for n, (src, dst) in enumerate((
        (f_hbm, f_ref), (fm_hbm, fm_ref), (p_hbm, p_ref), (pm_hbm, pm_ref),
        (filt_hbm, filt_ref), (s_hbm, s_ref), (sm_hbm, sm_ref),
    )):
        fetches.append(pltpu.make_async_copy(src, dst, in_sem.at[n]))
        fetches[-1].start()

    barrier = pltpu.get_barrier_semaphore()

    def greet(to):
        pl.semaphore_signal(barrier, inc=1, device_id=to, device_id_type=MESH)

    @pl.when(moved)
    def _():
        greet(held_from)

    greet((mate * Y + y, c))
    for d in (2, 6, 1, 7):
        greet((ring(d), c))
    for dz, dx in ((1, 0), (0, 1), (0, X - 1)):
        greet((r, on_line(dz, dx)))
    greet(over)
    greet((pair * Y + y, term_col))

    @pl.when(away)
    def _():
        greet((r, term_col))

    for one in fetches[:5]:
        one.wait()
    f_send[...] = masked(f_ref[...], fm_ref)
    p_all[core, y, low] = masked(p_ref[...], pm_ref)
    lane = lax.broadcasted_iota(jnp.int32, filt_send.shape, 1)
    filt_send[...] = jnp.where(lane < 128, filt_ref[0, 0], filt_ref[0, 1]).astype(F32)

    pl.semaphore_wait(barrier, jnp.where(moved, 1, 0) + 1 + 4 + 3 + 1 + 1 + jnp.where(away, 1, 0))

    my_slot = slot_of(zl, x)
    f_move = copy(f_send, f_all.at[X * core + x], t_send_sem.at[0], t_recv_sem.at[0], move_to)
    filt_move = copy(filt_send, filt_here, t_send_sem.at[1], t_recv_sem.at[1], move_to)

    @pl.when(moved)
    def _():
        f_move.start()
        filt_move.start()

    def mate_copy(buf, sem, t):
        ref = buf.at[core, y, t]
        return copy(ref, ref, sem.at[0], sem.at[1], (mate * Y + y, c))

    def ring_ref(buf, sems, src, t, part_of):
        slot = lax.rem(y + src, Y)
        at = Y + part_of if part_of is not None else slot
        if t is None:
            ref = buf.at[core, slot] if part_of is None else buf.at[core, slot, part_of]
            return ref, sems[1].at[0, at]
        ref = buf.at[core, slot, t] if part_of is None else buf.at[core, slot, t, pl.ds(64 * part_of, 64)]
        return ref, sems[1].at[t, at]

    def ring_send(buf, sems, src, t, d, part_of=None):
        ref, recv = ring_ref(buf, sems, src, t, part_of)
        copy(ref, ref, sems[0], recv, (ring(d), c)).start()

    def ring_wait(buf, sems, src, t, part_of=None):
        await_recv(*ring_ref(buf, sems, src, t, part_of))

    def ring_start(buf, sems, t):
        for d in (2, 6, 1, 7):
            ring_send(buf, sems, 0, t, d)

    def ring_relay(buf, sems, t):
        for src, on, far, part_of in ((6, 1, 2, 0), (2, 7, 6, 1)):
            ring_wait(buf, sems, src, t)
            ring_send(buf, sems, src, t, on)
            ring_send(buf, sems, src, t, far, part_of)

    def cross(buf, sems, src):
        at = lax.rem(y + src, Y)
        ref = buf.at[core, at]
        copy(ref, ref, sems[2], sems[3].at[at], over).start()

    def cross_wait(buf, sems, src):
        at = lax.rem(y + src, Y)
        await_recv(buf.at[1 - core, at], sems[3].at[at])

    def ring_last(buf, sems, ts, src):
        for t in ts:
            for part_of in range(2) if src == 4 else (None,):
                ring_wait(buf, sems, src, t, part_of)
        cross(buf, sems, src)

    p_sems = (p_send_sem, p_recv_sem, p_over_sem, p_core_sem)
    s_sems = (s_send_sem, s_recv_sem, s_over_sem, s_core_sem)
    mate_copy(p_all, p_mate_sem, low).start()
    ring_start(p_all, p_sems, low)

    def line_send(buf, sems, dz, dx, to):
        slot = slot_of(lax.rem(zl + dz, 2), lax.rem(x + dx, X))
        ref = buf.at[slot]
        copy(ref, ref, sems[0], sems[1].at[slot], (r, to)).start()

    def line_wait(buf, sems, dz, dx):
        slot = slot_of(lax.rem(zl + dz, 2), lax.rem(x + dx, X))
        await_recv(buf.at[slot], sems[1].at[slot])

    def line_start(buf, sems):
        for to in (on_line(1, 0), on_line(0, ahead), on_line(0, X - ahead)):
            line_send(buf, sems, 0, 0, to)

    def line_relay(buf, sems):
        line_wait(buf, sems, 1, 0)
        line_send(buf, sems, 1, 0, on_line(0, 1))
        line_send(buf, sems, 1, 0, on_line(0, X - 1))
        line_wait(buf, sems, 0, X - ahead)
        line_send(buf, sems, 0, X - ahead, on_line(0, ahead))
        line_send(buf, sems, 0, X - ahead, on_line(1, ahead))

    def line_finish(buf, sems):
        for dz, dx in ((0, ahead), (1, 1), (1, X - 1), (0, 2), (1, 2)):
            line_wait(buf, sems, dz, dx)

    f_sems, k_sems = (f_send_sem, f_recv_sem), (k_send_sem, k_recv_sem)
    @pl.when(moved)
    def _():
        await_recv(f_all.at[my_slot], t_recv_sem.at[0])

    @pl.when(stays)
    def _():
        f_all[my_slot] = f_send[...]

    line_start(f_all, f_sems)
    mate_copy(p_all, p_mate_sem, 1 - low).wait_recv()
    ring_start(p_all, p_sems, 1 - low)
    cross(p_all, p_sems, 0)

    for one in fetches[5:]:
        one.wait()
    s_all[core, y, low] = masked(s_ref[...], sm_ref)
    mate_copy(s_all, s_mate_sem, low).start()

    line_relay(f_all, f_sems)
    ring_relay(p_all, p_sems, low)
    ring_relay(p_all, p_sems, 1 - low)
    cross(p_all, p_sems, 2)
    cross(p_all, p_sems, 6)
    mate_copy(s_all, s_mate_sem, 1 - low).wait_recv()
    ring_start(s_all, s_sems, None)
    line_finish(f_all, f_sems)

    def at_place(b, src):
        place = lax.rem(y + src, Y)
        j = lax.div(place, 2)
        lanes = pl.ds(pl.multiple_of(128 * lax.rem(place, 2), 128), 128)
        total = None
        for t in range(2):
            rows = f_all[X * lax.rem(j, 2) + 2 * t + lax.div(j, 2), :, lanes]
            term = jnp.dot(rows, p_all[b, place, t], preferred_element_type=F32)
            total = term if total is None else total + term
        return total

    def near_copy():
        return copy(part, near_in, a_send_sem.at[0], a_recv_sem.at[0], (r, holder(1, core)))

    def send_first(b, term):
        @pl.when(away)
        def _():
            far_send[b] = term.astype(FAR)
            copy(
                far_send.at[b], far_in, a_send_sem.at[1], a_recv_sem.at[1], (pair * Y + y, holder(b, core))
            ).start()

        @pl.when(jnp.logical_and(home, b == 0))
        def _():
            near_in[...] = term

        @pl.when(jnp.logical_and(home, b == 1))
        def _():
            part[...] = term
            near_copy().start()

    term = at_place(core, 0) + at_place(core, 2) + at_place(core, 6)
    for src in (1, 7, 5, 3, 4):
        ring_last(p_all, p_sems, (low, 1 - low), src)
        term = term + at_place(core, src)
    send_first(core, term)

    term = None
    for src in (0, 2, 6, 1, 7, 5, 3, 4):
        cross_wait(p_all, p_sems, src)
        one = at_place(1 - core, src)
        term = one if term is None else term + one
    send_first(1 - core, term)

    @pl.when(moved)
    def _():
        filt_move.wait_recv()

    @pl.when(stays)
    def _():
        filt_here[...] = filt_send[...]

    ring_relay(s_all, s_sems, None)
    for src in (0, 2, 6):
        cross(s_all, s_sems, src)

    @pl.when(away)
    def _():
        await_recv(near_in, a_recv_sem.at[0])

    await_recv(far_in, a_recv_sem.at[1])
    k_all[my_slot] = ((near_in[...] + far_in[...].astype(F32)) * filt_here[0:1, :]).astype(BF16)
    line_start(k_all, k_sems)
    line_relay(k_all, k_sems)
    for src in (1, 7, 5, 3, 4):
        ring_last(s_all, s_sems, (None,), src)
    for src in range(Y):
        cross_wait(s_all, s_sems, src)

    def by_block(dz, dx):
        at = lax.rem(x + dx, X)
        slot = slot_of(lax.rem(zl + dz, 2), at)
        t, j = lax.div(at, 2), 2 * lax.rem(at, 2) + lax.div(slot, X)
        rows = k_all[slot]
        for b in range(2):
            depth = jnp.concatenate([s_all[b, 2 * j, t], s_all[b, 2 * j + 1, t]], axis=0)
            total[b] += jnp.dot(rows, depth, preferred_element_type=F32)

    total[...] = jnp.zeros_like(total)
    for dz, dx in ((0, 0), (1, 0), (0, X - ahead)):
        by_block(dz, dx)
    for dz, dx in ((0, ahead), (1, 1), (1, X - 1), (0, 2), (1, 2)):
        line_wait(k_all, k_sems, dz, dx)
        by_block(dz, dx)

    kept_b = jnp.where(mine, 0, 1)
    part_send[...] = total[1 - kept_b].astype(BF16)
    part_copy = copy(part_send, part2_in, b_send_sem, b_recv_sem, (pair * Y + y, c))
    part_copy.start()

    @pl.when(moved)
    def _():
        f_move.wait_send()
        filt_move.wait_send()

    mate_copy(p_all, p_mate_sem, low).wait_send()
    mate_copy(s_all, s_mate_sem, low).wait_send()
    await_sent(p_all.at[0, pl.ds(0, Y - 1)], p_send_sem)
    await_sent(s_all.at[0, pl.ds(0, Y - 1)], s_send_sem)
    await_sent(p_all.at[0], p_over_sem)
    await_sent(s_all.at[0], s_over_sem)
    await_sent(f_all.at[pl.ds(0, 2 * X - 1)], f_send_sem)
    await_sent(k_all.at[pl.ds(0, 2 * X - 1)], k_send_sem)

    @pl.when(away)
    def _():
        await_sent(far_send, a_send_sem.at[1])

    @pl.when(home)
    def _():
        near_copy().wait_send()

    block_row = jnp.where(mine, r, pair * Y + y)
    block_col = c - core + kept_b
    own_here = jnp.logical_and(low == 0, core == 0)
    own_comes = jnp.logical_not(own_here)
    own_sent = jnp.logical_not(jnp.logical_and(mine, core == 0))
    block_copy = copy(block_send, block_in, o_send_sem, o_recv_sem, (block_row, block_col))

    def tile_stays(h):
        return jnp.logical_and(2 * block_col + h == r, lax.div(block_row, 2) == c)

    def tile_copy(h):
        at = lax.rem(block_row, 2)
        return copy(
            tile_send.at[h], tile_in.at[at], x_send_sem.at[h], x_recv_sem.at[at], (2 * block_col + h, lax.div(block_row, 2))
        )

    def tile_is_here(b):
        row, col = 2 * c + b, lax.div(r, 2)
        z = lax.div(row, Y)
        z_low, second = lax.rem(z, 2), lax.rem(col, 2)
        z_at = z + second * (1 - 2 * z_low)
        return jnp.logical_and(z_at * Y + lax.rem(row, Y) == r, col - second + z_low == c)

    part_copy.wait_recv()
    rounded = (total[kept_b] + part2_in[...].astype(F32)).astype(BF16)
    for h in range(2):
        tile_send[h] = rounded[:, 128 * h : 128 * (h + 1)]

        @pl.when(jnp.logical_not(tile_stays(h)))
        def _():
            tile_copy(h).start()

        @pl.when(tile_stays(h))
        def _():
            tile_in[lax.rem(block_row, 2)] = tile_send[h]

    block_send[...] = rounded

    @pl.when(own_sent)
    def _():
        block_copy.start()

    @pl.when(own_here)
    def _():
        block_in[...] = rounded

    part_copy.wait_send()

    @pl.when(own_comes)
    def _():
        await_recv(block_in, o_recv_sem)

    for b in range(2):
        here = slice(128 * b, 128 * (b + 1))

        @pl.when(jnp.logical_not(tile_is_here(b)))
        def _():
            await_recv(tile_in.at[b], x_recv_sem.at[b])

        out_ref[:, here] = block_in[:, here].astype(F32) - tile_in[b].astype(F32).T

    @pl.when(own_sent)
    def _():
        block_copy.wait_send()

    for h in range(2):

        @pl.when(jnp.logical_not(tile_stays(h)))
        def _():
            tile_copy(h).wait_send()


def per_device(fock, density, intersection, fock_mask, density_mask, intersection_mask, product_filter):
    operands = fock, density, intersection, fock_mask, density_mask, intersection_mask, product_filter
    operands = [pltpu.with_memory_space_constraint(one, pltpu.HBM) for one in operands]
    hbm = pl.BlockSpec(memory_space=pltpu.HBM)
    vmem = pl.BlockSpec(memory_space=pltpu.VMEM)
    dma = pltpu.SemaphoreType.DMA
    block = (128, 256)
    return pl.pallas_call(
        kernel,
        out_shape=jax.ShapeDtypeStruct(block, F32),
        in_specs=[hbm] * 7,
        out_specs=vmem,
        scratch_shapes=[pltpu.VMEM(block, BF16)] * 3
        + [pltpu.SMEM((1, 2), jnp.int32)] * 4
        + [
            dma((7,)),
            pltpu.VMEM(block, BF16),
            pltpu.VMEM((2 * X,) + block, BF16),
            pltpu.VMEM((2 * X,) + block, BF16),
            pltpu.VMEM((2, Y, 2) + block, BF16),
            pltpu.VMEM((2, Y, 2) + block, BF16),
            pltpu.VMEM((8, 256), F32),
            pltpu.VMEM((8, 256), F32),
            pltpu.VMEM(block, F32),
            pltpu.VMEM(block, F32),
            pltpu.VMEM((2,) + block, FAR),
            pltpu.VMEM(block, FAR),
            pltpu.VMEM((2,) + block, F32),
            pltpu.VMEM(block, BF16),
            pltpu.VMEM(block, BF16),
            pltpu.VMEM(block, BF16),
            pltpu.VMEM(block, BF16),
            pltpu.VMEM((2, 128, 128), BF16),
            pltpu.VMEM((2, 128, 128), BF16),
            dma((2,)), dma((2,)),
            dma, dma((2, Y + 2)), dma, dma((Y,)), dma((2,)),
            dma, dma((2, Y + 2)), dma, dma((Y,)), dma((2,)),
            dma, dma((2 * X,)), dma, dma((2 * X,)),
            dma((2,)), dma((2,)), dma, dma, dma, dma,
            dma((2,)), dma((2,)),
        ],
        compiler_params=pltpu.CompilerParams(
            collective_id=0, has_side_effects=True, vmem_limit_bytes=32 * 1024 * 1024
        ),
        cost_estimate=pl.CostEstimate(flops=2 * 2 * 512 * 1024 * 256, bytes_accessed=6 * 1024 * 1024, transcendentals=0),
    )(*operands)


def solution(mesh):
    spec = P("row", "col")
    return jax.shard_map(
        per_device, mesh=mesh, in_specs=(spec,) * 7, out_specs=spec, check_vma=False
    )
```

```python
import jax
import jax.numpy as jnp
from jax import lax
from jax.experimental import pallas as pl
from jax.experimental.pallas import tpu as pltpu
from jax.sharding import PartitionSpec as P

MESH = pl.DeviceIdType.MESH
Z, Y, J = 4, 8, 4
X = 4
BF16, F32 = jnp.bfloat16, jnp.float32
FAR = F32


def masked(block, mask_ref):
    lane = lax.broadcasted_iota(jnp.int32, block.shape, 1)
    keep = jnp.where(lane < block.shape[1] // 2, mask_ref[0, 0], mask_ref[0, 1])
    return (block.astype(F32) * keep.astype(F32)).astype(BF16)


def kernel(
    f_hbm, p_hbm, s_hbm, fm_hbm, pm_hbm, sm_hbm, filt_hbm, out_ref,
    f_ref, p_ref, s_ref, fm_ref, pm_ref, sm_ref, filt_ref, in_sem,
    f_send, f_all, k_all, p_all, s_all, filt_send, filt_here,
    part, near_in, far_send, far_in, total, part_send, part2_in, block_send, block_in, tile_send, tile_in,
    t_send_sem, t_recv_sem,
    p_send_sem, p_recv_sem, p_over_sem, p_core_sem, p_mate_sem,
    s_send_sem, s_recv_sem, s_over_sem, s_core_sem, s_mate_sem,
    f_send_sem, f_recv_sem, k_send_sem, k_recv_sem,
    a_send_sem, a_recv_sem, b_send_sem, b_recv_sem, o_send_sem, o_recv_sem, x_send_sem, x_recv_sem,
):
    r, c = lax.axis_index("row"), lax.axis_index("col")
    zh, y = lax.div(r, Y), lax.rem(r, Y)
    zl, x, core = lax.div(c, 2 * X), lax.rem(lax.div(c, 2), X), lax.rem(c, 2)
    over = (r, c + 1 - 2 * core)
    low = lax.rem(zh, 2)
    pair = zh + 1 - 2 * low
    mate = Z - 1 - zh
    half = lax.rem(lax.div(zh, 2) + low, 2)
    x_high = lax.div(x, 2)
    home = lax.rem(zl + x_high, 2) == half
    away = lax.rem(zl + x_high, 2) != half
    home_row = jnp.where(home, r, pair * Y + y)
    ahead = jnp.where(core == 0, 1, X - 1)

    def holder(l, k):
        return lax.rem(zl + l, 2) * (2 * X) + x * 2 + k

    def slot_of(z_low, at):
        return X * lax.rem(z_low + lax.div(at, 2) + half, 2) + at

    held_z = 2 * lax.div(zh, 2) + core
    held_zl = lax.rem(x_high + half, 2)
    held_l = lax.rem(zl + held_zl, 2)
    held_from = (held_z * Y + y, held_zl * (2 * X) + x * 2 + held_l)
    term_col = held_zl * (2 * X) + x * 2 + core
    move_to = (home_row, holder(core, low))
    stays = jnp.logical_and(home, jnp.logical_and(core == 0, low == 0))
    moved = jnp.logical_not(stays)
    mine = low == core

    def ring(d):
        return zh * Y + lax.rem(y + d, Y)

    def on_line(dz, dx):
        return lax.rem(zl + dz, 2) * (2 * X) + lax.rem(x + dx, X) * 2 + core

    def copy(src, dst, send, recv, to):
        return pltpu.make_async_remote_copy(
            src_ref=src, dst_ref=dst, send_sem=send, recv_sem=recv, device_id=to, device_id_type=MESH
        )

    def await_sent(ref, sem):
        copy(ref, ref, sem, sem, over).wait_send()

    def await_recv(ref, sem):
        copy(ref, ref, sem, sem, over).wait_recv()

    fetches = []
    for n, (src, dst) in enumerate((
        (f_hbm, f_ref), (fm_hbm, fm_ref), (p_hbm, p_ref), (pm_hbm, pm_ref),
        (filt_hbm, filt_ref), (s_hbm, s_ref), (sm_hbm, sm_ref),
    )):
        fetches.append(pltpu.make_async_copy(src, dst, in_sem.at[n]))
        fetches[-1].start()

    barrier = pltpu.get_barrier_semaphore()

    def greet(to):
        pl.semaphore_signal(barrier, inc=1, device_id=to, device_id_type=MESH)

    @pl.when(moved)
    def _():
        greet(held_from)

    greet((mate * Y + y, c))
    for d in (2, 6, 1, 7):
        greet((ring(d), c))
    for dz, dx in ((1, 0), (0, 1), (0, X - 1)):
        greet((r, on_line(dz, dx)))
    greet(over)
    greet((pair * Y + y, term_col))

    @pl.when(away)
    def _():
        greet((r, term_col))

    for one in fetches[:5]:
        one.wait()
    f_send[...] = masked(f_ref[...], fm_ref)
    p_all[core, y, low] = masked(p_ref[...], pm_ref)
    lane = lax.broadcasted_iota(jnp.int32, filt_send.shape, 1)
    filt_send[...] = jnp.where(lane < 128, filt_ref[0, 0], filt_ref[0, 1]).astype(F32)

    pl.semaphore_wait(barrier, jnp.where(moved, 1, 0) + 1 + 4 + 3 + 1 + 1 + jnp.where(away, 1, 0))

    my_slot = slot_of(zl, x)
    f_move = copy(f_send, f_all.at[X * core + x], t_send_sem.at[0], t_recv_sem.at[0], move_to)
    filt_move = copy(filt_send, filt_here, t_send_sem.at[1], t_recv_sem.at[1], move_to)

    @pl.when(moved)
    def _():
        f_move.start()
        filt_move.start()

    def mate_copy(buf, sem, t):
        ref = buf.at[core, y, t]
        return copy(ref, ref, sem.at[0], sem.at[1], (mate * Y + y, c))

    def ring_ref(buf, sems, src, t, part_of):
        slot = lax.rem(y + src, Y)
        at = Y + part_of if part_of is not None else slot
        if t is None:
            ref = buf.at[core, slot] if part_of is None else buf.at[core, slot, part_of]
            return ref, sems[1].at[0, at]
        ref = buf.at[core, slot, t] if part_of is None else buf.at[core, slot, t, pl.ds(64 * part_of, 64)]
        return ref, sems[1].at[t, at]

    def ring_send(buf, sems, src, t, d, part_of=None):
        ref, recv = ring_ref(buf, sems, src, t, part_of)
        copy(ref, ref, sems[0], recv, (ring(d), c)).start()

    def ring_wait(buf, sems, src, t, part_of=None):
        await_recv(*ring_ref(buf, sems, src, t, part_of))

    def ring_start(buf, sems, t):
        for d in (2, 6, 1, 7):
            ring_send(buf, sems, 0, t, d)

    def ring_relay(buf, sems, t):
        for src, on, far, part_of in ((6, 1, 2, 0), (2, 7, 6, 1)):
            ring_wait(buf, sems, src, t)
            ring_send(buf, sems, src, t, on)
            ring_send(buf, sems, src, t, far, part_of)

    def cross(buf, sems, src):
        at = lax.rem(y + src, Y)
        ref = buf.at[core, at]
        copy(ref, ref, sems[2], sems[3].at[at], over).start()

    def cross_wait(buf, sems, src):
        at = lax.rem(y + src, Y)
        await_recv(buf.at[1 - core, at], sems[3].at[at])

    def ring_last(buf, sems, ts, src):
        for t in ts:
            for part_of in range(2) if src == 4 else (None,):
                ring_wait(buf, sems, src, t, part_of)
        cross(buf, sems, src)

    p_sems = (p_send_sem, p_recv_sem, p_over_sem, p_core_sem)
    s_sems = (s_send_sem, s_recv_sem, s_over_sem, s_core_sem)
    mate_copy(p_all, p_mate_sem, low).start()
    ring_start(p_all, p_sems, low)

    def line_send(buf, sems, dz, dx, to):
        slot = slot_of(lax.rem(zl + dz, 2), lax.rem(x + dx, X))
        ref = buf.at[slot]
        copy(ref, ref, sems[0], sems[1].at[slot], (r, to)).start()

    def line_wait(buf, sems, dz, dx):
        slot = slot_of(lax.rem(zl + dz, 2), lax.rem(x + dx, X))
        await_recv(buf.at[slot], sems[1].at[slot])

    def line_start(buf, sems):
        for to in (on_line(1, 0), on_line(0, ahead), on_line(0, X - ahead)):
            line_send(buf, sems, 0, 0, to)

    def line_relay(buf, sems):
        line_wait(buf, sems, 1, 0)
        line_send(buf, sems, 1, 0, on_line(0, 1))
        line_send(buf, sems, 1, 0, on_line(0, X - 1))
        line_wait(buf, sems, 0, X - ahead)
        line_send(buf, sems, 0, X - ahead, on_line(0, ahead))
        line_send(buf, sems, 0, X - ahead, on_line(1, ahead))

    def line_finish(buf, sems):
        for dz, dx in ((0, ahead), (1, 1), (1, X - 1), (0, 2), (1, 2)):
            line_wait(buf, sems, dz, dx)

    f_sems, k_sems = (f_send_sem, f_recv_sem), (k_send_sem, k_recv_sem)
    mate_copy(p_all, p_mate_sem, 1 - low).wait_recv()
    ring_start(p_all, p_sems, 1 - low)

    @pl.when(moved)
    def _():
        await_recv(f_all.at[my_slot], t_recv_sem.at[0])

    @pl.when(stays)
    def _():
        f_all[my_slot] = f_send[...]

    line_start(f_all, f_sems)
    cross(p_all, p_sems, 0)

    for one in fetches[5:]:
        one.wait()
    s_all[core, y, low] = masked(s_ref[...], sm_ref)
    mate_copy(s_all, s_mate_sem, low).start()

    ring_relay(p_all, p_sems, low)
    line_relay(f_all, f_sems)
    ring_relay(p_all, p_sems, 1 - low)
    cross(p_all, p_sems, 2)
    cross(p_all, p_sems, 6)
    mate_copy(s_all, s_mate_sem, 1 - low).wait_recv()
    ring_start(s_all, s_sems, None)
    line_finish(f_all, f_sems)

    def at_place(b, src):
        place = lax.rem(y + src, Y)
        j = lax.div(place, 2)
        lanes = pl.ds(pl.multiple_of(128 * lax.rem(place, 2), 128), 128)
        total = None
        for t in range(2):
            rows = f_all[X * lax.rem(j, 2) + 2 * t + lax.div(j, 2), :, lanes]
            term = jnp.dot(rows, p_all[b, place, t], preferred_element_type=F32)
            total = term if total is None else total + term
        return total

    def near_copy():
        return copy(part, near_in, a_send_sem.at[0], a_recv_sem.at[0], (r, holder(1, core)))

    def send_first(b, term):
        @pl.when(away)
        def _():
            far_send[b] = term.astype(FAR)
            copy(
                far_send.at[b], far_in, a_send_sem.at[1], a_recv_sem.at[1], (pair * Y + y, holder(b, core))
            ).start()

        @pl.when(jnp.logical_and(home, b == 0))
        def _():
            near_in[...] = term

        @pl.when(jnp.logical_and(home, b == 1))
        def _():
            part[...] = term
            near_copy().start()

    term = at_place(core, 0) + at_place(core, 2) + at_place(core, 6)
    for src in (1, 7, 5, 3, 4):
        ring_last(p_all, p_sems, (low, 1 - low), src)
        term = term + at_place(core, src)
    send_first(core, term)

    term = None
    for src in (0, 2, 6, 1, 7, 5, 3, 4):
        cross_wait(p_all, p_sems, src)
        one = at_place(1 - core, src)
        term = one if term is None else term + one
    send_first(1 - core, term)

    @pl.when(moved)
    def _():
        filt_move.wait_recv()

    @pl.when(stays)
    def _():
        filt_here[...] = filt_send[...]

    ring_relay(s_all, s_sems, None)
    for src in (0, 2, 6):
        cross(s_all, s_sems, src)

    @pl.when(away)
    def _():
        await_recv(near_in, a_recv_sem.at[0])

    await_recv(far_in, a_recv_sem.at[1])
    k_all[my_slot] = ((near_in[...] + far_in[...].astype(F32)) * filt_here[0:1, :]).astype(BF16)
    line_start(k_all, k_sems)
    line_relay(k_all, k_sems)
    for src in (1, 7, 5, 3, 4):
        ring_last(s_all, s_sems, (None,), src)

    def by_block(b, dz, dx):
        at = lax.rem(x + dx, X)
        slot = slot_of(lax.rem(zl + dz, 2), at)
        t, j = lax.div(at, 2), 2 * lax.rem(at, 2) + lax.div(slot, X)
        rows = k_all[slot]
        depth = jnp.concatenate([s_all[b, 2 * j, t], s_all[b, 2 * j + 1, t]], axis=0)
        return jnp.dot(rows, depth, preferred_element_type=F32)

    blocks = (0, 0), (1, 0), (0, X - ahead), (0, ahead), (1, 1), (1, X - 1), (0, 2), (1, 2)
    term = None
    for n, at in enumerate(blocks):
        if n >= 3:
            line_wait(k_all, k_sems, *at)
        one = by_block(core, *at)
        term = one if term is None else term + one
    total[core] = term
    for src in range(Y):
        cross_wait(s_all, s_sems, src)
    term = None
    for at in blocks:
        one = by_block(1 - core, *at)
        term = one if term is None else term + one
    total[1 - core] = term

    kept_b = jnp.where(mine, 0, 1)
    part_send[...] = total[1 - kept_b].astype(BF16)
    part_copy = copy(part_send, part2_in, b_send_sem, b_recv_sem, (pair * Y + y, c))
    part_copy.start()

    @pl.when(moved)
    def _():
        f_move.wait_send()
        filt_move.wait_send()

    mate_copy(p_all, p_mate_sem, low).wait_send()
    mate_copy(s_all, s_mate_sem, low).wait_send()
    await_sent(p_all.at[0, pl.ds(0, Y - 1)], p_send_sem)
    await_sent(s_all.at[0, pl.ds(0, Y - 1)], s_send_sem)
    await_sent(p_all.at[0], p_over_sem)
    await_sent(s_all.at[0], s_over_sem)
    await_sent(f_all.at[pl.ds(0, 2 * X - 1)], f_send_sem)
    await_sent(k_all.at[pl.ds(0, 2 * X - 1)], k_send_sem)

    @pl.when(away)
    def _():
        await_sent(far_send, a_send_sem.at[1])

    @pl.when(home)
    def _():
        near_copy().wait_send()

    block_row = jnp.where(mine, r, pair * Y + y)
    block_col = c - core + kept_b
    own_here = jnp.logical_and(low == 0, core == 0)
    own_comes = jnp.logical_not(own_here)
    own_sent = jnp.logical_not(jnp.logical_and(mine, core == 0))
    block_copy = copy(block_send, block_in, o_send_sem, o_recv_sem, (block_row, block_col))

    def tile_stays(h):
        return jnp.logical_and(2 * block_col + h == r, lax.div(block_row, 2) == c)

    def tile_copy(h):
        at = lax.rem(block_row, 2)
        return copy(
            tile_send.at[h], tile_in.at[at], x_send_sem.at[h], x_recv_sem.at[at], (2 * block_col + h, lax.div(block_row, 2))
        )

    def tile_is_here(b):
        row, col = 2 * c + b, lax.div(r, 2)
        z = lax.div(row, Y)
        z_low, second = lax.rem(z, 2), lax.rem(col, 2)
        z_at = z + second * (1 - 2 * z_low)
        return jnp.logical_and(z_at * Y + lax.rem(row, Y) == r, col - second + z_low == c)

    part_copy.wait_recv()
    rounded = (total[kept_b] + part2_in[...].astype(F32)).astype(BF16)
    for h in range(2):
        tile_send[h] = rounded[:, 128 * h : 128 * (h + 1)]

        @pl.when(jnp.logical_not(tile_stays(h)))
        def _():
            tile_copy(h).start()

        @pl.when(tile_stays(h))
        def _():
            tile_in[lax.rem(block_row, 2)] = tile_send[h]

    block_send[...] = rounded

    @pl.when(own_sent)
    def _():
        block_copy.start()

    @pl.when(own_here)
    def _():
        block_in[...] = rounded

    part_copy.wait_send()

    @pl.when(own_comes)
    def _():
        await_recv(block_in, o_recv_sem)

    for b in range(2):
        here = slice(128 * b, 128 * (b + 1))

        @pl.when(jnp.logical_not(tile_is_here(b)))
        def _():
            await_recv(tile_in.at[b], x_recv_sem.at[b])

        out_ref[:, here] = block_in[:, here].astype(F32) - tile_in[b].astype(F32).T

    @pl.when(own_sent)
    def _():
        block_copy.wait_send()

    for h in range(2):

        @pl.when(jnp.logical_not(tile_stays(h)))
        def _():
            tile_copy(h).wait_send()


def per_device(fock, density, intersection, fock_mask, density_mask, intersection_mask, product_filter):
    operands = fock, density, intersection, fock_mask, density_mask, intersection_mask, product_filter
    operands = [pltpu.with_memory_space_constraint(one, pltpu.HBM) for one in operands]
    hbm = pl.BlockSpec(memory_space=pltpu.HBM)
    vmem = pl.BlockSpec(memory_space=pltpu.VMEM)
    dma = pltpu.SemaphoreType.DMA
    block = (128, 256)
    return pl.pallas_call(
        kernel,
        out_shape=jax.ShapeDtypeStruct(block, F32),
        in_specs=[hbm] * 7,
        out_specs=vmem,
        scratch_shapes=[pltpu.VMEM(block, BF16)] * 3
        + [pltpu.SMEM((1, 2), jnp.int32)] * 4
        + [
            dma((7,)),
            pltpu.VMEM(block, BF16),
            pltpu.VMEM((2 * X,) + block, BF16),
            pltpu.VMEM((2 * X,) + block, BF16),
            pltpu.VMEM((2, Y, 2) + block, BF16),
            pltpu.VMEM((2, Y, 2) + block, BF16),
            pltpu.VMEM((8, 256), F32),
            pltpu.VMEM((8, 256), F32),
            pltpu.VMEM(block, F32),
            pltpu.VMEM(block, F32),
            pltpu.VMEM((2,) + block, FAR),
            pltpu.VMEM(block, FAR),
            pltpu.VMEM((2,) + block, F32),
            pltpu.VMEM(block, BF16),
            pltpu.VMEM(block, BF16),
            pltpu.VMEM(block, BF16),
            pltpu.VMEM(block, BF16),
            pltpu.VMEM((2, 128, 128), BF16),
            pltpu.VMEM((2, 128, 128), BF16),
            dma((2,)), dma((2,)),
            dma, dma((2, Y + 2)), dma, dma((Y,)), dma((2,)),
            dma, dma((2, Y + 2)), dma, dma((Y,)), dma((2,)),
            dma, dma((2 * X,)), dma, dma((2 * X,)),
            dma((2,)), dma((2,)), dma, dma, dma, dma,
            dma((2,)), dma((2,)),
        ],
        compiler_params=pltpu.CompilerParams(
            collective_id=0, has_side_effects=True, vmem_limit_bytes=32 * 1024 * 1024
        ),
        cost_estimate=pl.CostEstimate(flops=2 * 2 * 512 * 1024 * 256, bytes_accessed=6 * 1024 * 1024, transcendentals=0),
    )(*operands)


def solution(mesh):
    spec = P("row", "col")
    return jax.shard_map(
        per_device, mesh=mesh, in_specs=(spec,) * 7, out_specs=spec, check_vma=False
    )
```

```python
import jax
import jax.numpy as jnp
from jax import lax
from jax.experimental import pallas as pl
from jax.experimental.pallas import tpu as pltpu
from jax.sharding import PartitionSpec as P

MESH = pl.DeviceIdType.MESH
Z, Y, J = 4, 8, 4
X = 4
BF16, F32 = jnp.bfloat16, jnp.float32
FAR = BF16


def masked(block, mask_ref):
    lane = lax.broadcasted_iota(jnp.int32, block.shape, 1)
    keep = jnp.where(lane < block.shape[1] // 2, mask_ref[0, 0], mask_ref[0, 1])
    return (block.astype(F32) * keep.astype(F32)).astype(BF16)


def kernel(
    f_hbm, p_hbm, s_hbm, fm_hbm, pm_hbm, sm_hbm, filt_hbm, out_ref,
    f_ref, p_ref, s_ref, fm_ref, pm_ref, sm_ref, filt_ref, in_sem,
    f_send, f_all, k_all, p_all, s_all, filt_send, filt_here,
    part, near_in, far_send, far_in, total, part_send, part2_in, block_send, block_in, tile_send, tile_in,
    t_send_sem, t_recv_sem,
    p_send_sem, p_recv_sem, p_over_sem, p_core_sem, p_mate_sem,
    s_send_sem, s_recv_sem, s_over_sem, s_core_sem, s_mate_sem,
    f_send_sem, f_recv_sem, k_send_sem, k_recv_sem,
    a_send_sem, a_recv_sem, b_send_sem, b_recv_sem, o_send_sem, o_recv_sem, x_send_sem, x_recv_sem,
):
    r, c = lax.axis_index("row"), lax.axis_index("col")
    zh, y = lax.div(r, Y), lax.rem(r, Y)
    zl, x, core = lax.div(c, 2 * X), lax.rem(lax.div(c, 2), X), lax.rem(c, 2)
    over = (r, c + 1 - 2 * core)
    low = lax.rem(zh, 2)
    pair = zh + 1 - 2 * low
    mate = Z - 1 - zh
    half = lax.rem(lax.div(zh, 2) + low, 2)
    x_high = lax.div(x, 2)
    home = lax.rem(zl + x_high, 2) == half
    away = lax.rem(zl + x_high, 2) != half
    home_row = jnp.where(home, r, pair * Y + y)
    ahead = jnp.where(core == 0, 1, X - 1)

    def holder(l, k):
        return lax.rem(zl + l, 2) * (2 * X) + x * 2 + k

    def slot_of(z_low, at):
        return X * lax.rem(z_low + lax.div(at, 2) + half, 2) + at

    held_z = 2 * lax.div(zh, 2) + core
    held_zl = lax.rem(x_high + half, 2)
    held_l = lax.rem(zl + held_zl, 2)
    held_from = (held_z * Y + y, held_zl * (2 * X) + x * 2 + held_l)
    term_col = held_zl * (2 * X) + x * 2 + core
    move_to = (home_row, holder(core, low))
    stays = jnp.logical_and(home, jnp.logical_and(core == 0, low == 0))
    moved = jnp.logical_not(stays)
    mine = low == core

    def ring(d):
        return zh * Y + lax.rem(y + d, Y)

    def on_line(dz, dx):
        return lax.rem(zl + dz, 2) * (2 * X) + lax.rem(x + dx, X) * 2 + core

    def copy(src, dst, send, recv, to):
        return pltpu.make_async_remote_copy(
            src_ref=src, dst_ref=dst, send_sem=send, recv_sem=recv, device_id=to, device_id_type=MESH
        )

    def await_sent(ref, sem):
        copy(ref, ref, sem, sem, over).wait_send()

    def await_recv(ref, sem):
        copy(ref, ref, sem, sem, over).wait_recv()

    fetches = []
    for n, (src, dst) in enumerate((
        (f_hbm, f_ref), (fm_hbm, fm_ref), (p_hbm, p_ref), (pm_hbm, pm_ref),
        (filt_hbm, filt_ref), (s_hbm, s_ref), (sm_hbm, sm_ref),
    )):
        fetches.append(pltpu.make_async_copy(src, dst, in_sem.at[n]))
        fetches[-1].start()

    barrier = pltpu.get_barrier_semaphore()

    def greet(to):
        pl.semaphore_signal(barrier, inc=1, device_id=to, device_id_type=MESH)

    @pl.when(moved)
    def _():
        greet(held_from)

    greet((mate * Y + y, c))
    for d in (2, 6, 1, 7):
        greet((ring(d), c))
    for dz, dx in ((1, 0), (0, 1), (0, X - 1)):
        greet((r, on_line(dz, dx)))
    greet(over)
    greet((pair * Y + y, term_col))

    @pl.when(away)
    def _():
        greet((r, term_col))

    for one in fetches[:5]:
        one.wait()
    f_send[...] = masked(f_ref[...], fm_ref)
    p_all[core, y, low] = masked(p_ref[...], pm_ref)
    lane = lax.broadcasted_iota(jnp.int32, filt_send.shape, 1)
    filt_send[...] = jnp.where(lane < 128, filt_ref[0, 0], filt_ref[0, 1]).astype(F32)

    pl.semaphore_wait(barrier, jnp.where(moved, 1, 0) + 1 + 4 + 3 + 1 + 1 + jnp.where(away, 1, 0))

    my_slot = slot_of(zl, x)
    f_move = copy(f_send, f_all.at[X * core + x], t_send_sem.at[0], t_recv_sem.at[0], move_to)
    filt_move = copy(filt_send, filt_here, t_send_sem.at[1], t_recv_sem.at[1], move_to)

    @pl.when(moved)
    def _():
        f_move.start()
        filt_move.start()

    def mate_copy(buf, sem, t):
        ref = buf.at[core, y, t]
        return copy(ref, ref, sem.at[0], sem.at[1], (mate * Y + y, c))

    def ring_ref(buf, sems, src, t, part_of):
        slot = lax.rem(y + src, Y)
        at = Y + part_of if part_of is not None else slot
        if t is None:
            ref = buf.at[core, slot] if part_of is None else buf.at[core, slot, part_of]
            return ref, sems[1].at[0, at]
        ref = buf.at[core, slot, t] if part_of is None else buf.at[core, slot, t, pl.ds(64 * part_of, 64)]
        return ref, sems[1].at[t, at]

    def ring_send(buf, sems, src, t, d, part_of=None):
        ref, recv = ring_ref(buf, sems, src, t, part_of)
        copy(ref, ref, sems[0], recv, (ring(d), c)).start()

    def ring_wait(buf, sems, src, t, part_of=None):
        await_recv(*ring_ref(buf, sems, src, t, part_of))

    def ring_start(buf, sems, t):
        for d in (2, 6, 1, 7):
            ring_send(buf, sems, 0, t, d)

    def ring_relay(buf, sems, t):
        for src, on, far, part_of in ((6, 1, 2, 0), (2, 7, 6, 1)):
            ring_wait(buf, sems, src, t)
            ring_send(buf, sems, src, t, on)
            ring_send(buf, sems, src, t, far, part_of)

    def cross(buf, sems, src):
        at = lax.rem(y + src, Y)
        ref = buf.at[core, at]
        copy(ref, ref, sems[2], sems[3].at[at], over).start()

    def cross_wait(buf, sems, src):
        at = lax.rem(y + src, Y)
        await_recv(buf.at[1 - core, at], sems[3].at[at])

    def ring_last(buf, sems, ts, src):
        for t in ts:
            for part_of in range(2) if src == 4 else (None,):
                ring_wait(buf, sems, src, t, part_of)
        cross(buf, sems, src)

    p_sems = (p_send_sem, p_recv_sem, p_over_sem, p_core_sem)
    s_sems = (s_send_sem, s_recv_sem, s_over_sem, s_core_sem)
    mate_copy(p_all, p_mate_sem, low).start()
    ring_start(p_all, p_sems, low)

    def line_send(buf, sems, dz, dx, to):
        slot = slot_of(lax.rem(zl + dz, 2), lax.rem(x + dx, X))
        ref = buf.at[slot]
        copy(ref, ref, sems[0], sems[1].at[slot], (r, to)).start()

    def line_wait(buf, sems, dz, dx):
        slot = slot_of(lax.rem(zl + dz, 2), lax.rem(x + dx, X))
        await_recv(buf.at[slot], sems[1].at[slot])

    def line_start(buf, sems):
        for to in (on_line(1, 0), on_line(0, ahead), on_line(0, X - ahead)):
            line_send(buf, sems, 0, 0, to)

    def line_relay(buf, sems):
        line_wait(buf, sems, 1, 0)
        line_send(buf, sems, 1, 0, on_line(0, 1))
        line_send(buf, sems, 1, 0, on_line(0, X - 1))
        line_wait(buf, sems, 0, X - ahead)
        line_send(buf, sems, 0, X - ahead, on_line(0, ahead))
        line_send(buf, sems, 0, X - ahead, on_line(1, ahead))

    def line_finish(buf, sems):
        for dz, dx in ((0, ahead), (1, 1), (1, X - 1), (0, 2), (1, 2)):
            line_wait(buf, sems, dz, dx)

    f_sems, k_sems = (f_send_sem, f_recv_sem), (k_send_sem, k_recv_sem)
    mate_copy(p_all, p_mate_sem, 1 - low).wait_recv()
    ring_start(p_all, p_sems, 1 - low)

    @pl.when(moved)
    def _():
        await_recv(f_all.at[my_slot], t_recv_sem.at[0])

    @pl.when(stays)
    def _():
        f_all[my_slot] = f_send[...]

    line_start(f_all, f_sems)
    cross(p_all, p_sems, 0)

    for one in fetches[5:]:
        one.wait()
    s_all[core, y, low] = masked(s_ref[...], sm_ref)
    mate_copy(s_all, s_mate_sem, low).start()

    ring_relay(p_all, p_sems, low)
    line_relay(f_all, f_sems)
    ring_relay(p_all, p_sems, 1 - low)
    cross(p_all, p_sems, 2)
    cross(p_all, p_sems, 6)
    mate_copy(s_all, s_mate_sem, 1 - low).wait_recv()
    ring_start(s_all, s_sems, None)
    line_finish(f_all, f_sems)

    def at_place(b, src):
        place = lax.rem(y + src, Y)
        j = lax.div(place, 2)
        lanes = pl.ds(pl.multiple_of(128 * lax.rem(place, 2), 128), 128)
        total = None
        for t in range(2):
            rows = f_all[X * lax.rem(j, 2) + 2 * t + lax.div(j, 2), :, lanes]
            term = jnp.dot(rows, p_all[b, place, t], preferred_element_type=F32)
            total = term if total is None else total + term
        return total

    def near_copy():
        return copy(part, near_in, a_send_sem.at[0], a_recv_sem.at[0], (r, holder(1, core)))

    def send_first(b, term):
        @pl.when(away)
        def _():
            far_send[b] = term.astype(FAR)
            copy(
                far_send.at[b], far_in, a_send_sem.at[1], a_recv_sem.at[1], (pair * Y + y, holder(b, core))
            ).start()

        @pl.when(jnp.logical_and(home, b == 0))
        def _():
            near_in[...] = term

        @pl.when(jnp.logical_and(home, b == 1))
        def _():
            part[...] = term
            near_copy().start()

    term = at_place(core, 0) + at_place(core, 2) + at_place(core, 6)
    for src in (1, 7, 5, 3, 4):
        ring_last(p_all, p_sems, (low, 1 - low), src)
        term = term + at_place(core, src)
    send_first(core, term)

    term = None
    for src in (0, 2, 6, 1, 7, 5, 3, 4):
        cross_wait(p_all, p_sems, src)
        one = at_place(1 - core, src)
        term = one if term is None else term + one
    send_first(1 - core, term)

    @pl.when(moved)
    def _():
        filt_move.wait_recv()

    @pl.when(stays)
    def _():
        filt_here[...] = filt_send[...]

    ring_relay(s_all, s_sems, None)
    for src in (0, 2, 6):
        cross(s_all, s_sems, src)

    @pl.when(away)
    def _():
        await_recv(near_in, a_recv_sem.at[0])

    await_recv(far_in, a_recv_sem.at[1])
    k_all[my_slot] = ((near_in[...] + far_in[...].astype(F32)) * filt_here[0:1, :]).astype(BF16)
    line_start(k_all, k_sems)
    line_relay(k_all, k_sems)
    for src in (1, 7, 5, 3, 4):
        ring_last(s_all, s_sems, (None,), src)

    def by_block(b, dz, dx):
        at = lax.rem(x + dx, X)
        slot = slot_of(lax.rem(zl + dz, 2), at)
        t, j = lax.div(at, 2), 2 * lax.rem(at, 2) + lax.div(slot, X)
        rows = k_all[slot]
        depth = jnp.concatenate([s_all[b, 2 * j, t], s_all[b, 2 * j + 1, t]], axis=0)
        return jnp.dot(rows, depth, preferred_element_type=F32)

    blocks = (0, 0), (1, 0), (0, X - ahead), (0, ahead), (1, 1), (1, X - 1), (0, 2), (1, 2)
    term = None
    for n, at in enumerate(blocks):
        if n >= 3:
            line_wait(k_all, k_sems, *at)
        one = by_block(core, *at)
        term = one if term is None else term + one
    total[core] = term
    for src in range(Y):
        cross_wait(s_all, s_sems, src)
    term = None
    for at in blocks:
        one = by_block(1 - core, *at)
        term = one if term is None else term + one
    total[1 - core] = term

    kept_b = jnp.where(mine, 0, 1)
    part_send[...] = total[1 - kept_b].astype(BF16)
    part_copy = copy(part_send, part2_in, b_send_sem, b_recv_sem, (pair * Y + y, c))
    part_copy.start()

    @pl.when(moved)
    def _():
        f_move.wait_send()
        filt_move.wait_send()

    mate_copy(p_all, p_mate_sem, low).wait_send()
    mate_copy(s_all, s_mate_sem, low).wait_send()
    await_sent(p_all.at[0, pl.ds(0, Y - 1)], p_send_sem)
    await_sent(s_all.at[0, pl.ds(0, Y - 1)], s_send_sem)
    await_sent(p_all.at[0], p_over_sem)
    await_sent(s_all.at[0], s_over_sem)
    await_sent(f_all.at[pl.ds(0, 2 * X - 1)], f_send_sem)
    await_sent(k_all.at[pl.ds(0, 2 * X - 1)], k_send_sem)

    @pl.when(away)
    def _():
        await_sent(far_send, a_send_sem.at[1])

    @pl.when(home)
    def _():
        near_copy().wait_send()

    block_row = jnp.where(mine, r, pair * Y + y)
    block_col = c - core + kept_b
    own_here = jnp.logical_and(low == 0, core == 0)
    own_comes = jnp.logical_not(own_here)
    own_sent = jnp.logical_not(jnp.logical_and(mine, core == 0))
    block_copy = copy(block_send, block_in, o_send_sem, o_recv_sem, (block_row, block_col))

    def tile_stays(h):
        return jnp.logical_and(2 * block_col + h == r, lax.div(block_row, 2) == c)

    def tile_copy(h):
        at = lax.rem(block_row, 2)
        return copy(
            tile_send.at[h], tile_in.at[at], x_send_sem.at[h], x_recv_sem.at[at], (2 * block_col + h, lax.div(block_row, 2))
        )

    def tile_is_here(b):
        row, col = 2 * c + b, lax.div(r, 2)
        z = lax.div(row, Y)
        z_low, second = lax.rem(z, 2), lax.rem(col, 2)
        z_at = z + second * (1 - 2 * z_low)
        return jnp.logical_and(z_at * Y + lax.rem(row, Y) == r, col - second + z_low == c)

    part_copy.wait_recv()
    rounded = (total[kept_b] + part2_in[...].astype(F32)).astype(BF16)
    for h in range(2):
        tile_send[h] = rounded[:, 128 * h : 128 * (h + 1)]

        @pl.when(jnp.logical_not(tile_stays(h)))
        def _():
            tile_copy(h).start()

        @pl.when(tile_stays(h))
        def _():
            tile_in[lax.rem(block_row, 2)] = tile_send[h]

    block_send[...] = rounded

    @pl.when(own_sent)
    def _():
        block_copy.start()

    @pl.when(own_here)
    def _():
        block_in[...] = rounded

    part_copy.wait_send()

    @pl.when(own_comes)
    def _():
        await_recv(block_in, o_recv_sem)

    for b in range(2):
        here = slice(128 * b, 128 * (b + 1))

        @pl.when(jnp.logical_not(tile_is_here(b)))
        def _():
            await_recv(tile_in.at[b], x_recv_sem.at[b])

        out_ref[:, here] = block_in[:, here].astype(F32) - tile_in[b].astype(F32).T

    @pl.when(own_sent)
    def _():
        block_copy.wait_send()

    for h in range(2):

        @pl.when(jnp.logical_not(tile_stays(h)))
        def _():
            tile_copy(h).wait_send()


def per_device(fock, density, intersection, fock_mask, density_mask, intersection_mask, product_filter):
    operands = fock, density, intersection, fock_mask, density_mask, intersection_mask, product_filter
    operands = [pltpu.with_memory_space_constraint(one, pltpu.HBM) for one in operands]
    hbm = pl.BlockSpec(memory_space=pltpu.HBM)
    vmem = pl.BlockSpec(memory_space=pltpu.VMEM)
    dma = pltpu.SemaphoreType.DMA
    block = (128, 256)
    return pl.pallas_call(
        kernel,
        out_shape=jax.ShapeDtypeStruct(block, F32),
        in_specs=[hbm] * 7,
        out_specs=vmem,
        scratch_shapes=[pltpu.VMEM(block, BF16)] * 3
        + [pltpu.SMEM((1, 2), jnp.int32)] * 4
        + [
            dma((7,)),
            pltpu.VMEM(block, BF16),
            pltpu.VMEM((2 * X,) + block, BF16),
            pltpu.VMEM((2 * X,) + block, BF16),
            pltpu.VMEM((2, Y, 2) + block, BF16),
            pltpu.VMEM((2, Y, 2) + block, BF16),
            pltpu.VMEM((8, 256), F32),
            pltpu.VMEM((8, 256), F32),
            pltpu.VMEM(block, F32),
            pltpu.VMEM(block, F32),
            pltpu.VMEM((2,) + block, FAR),
            pltpu.VMEM(block, FAR),
            pltpu.VMEM((2,) + block, F32),
            pltpu.VMEM(block, BF16),
            pltpu.VMEM(block, BF16),
            pltpu.VMEM(block, BF16),
            pltpu.VMEM(block, BF16),
            pltpu.VMEM((2, 128, 128), BF16),
            pltpu.VMEM((2, 128, 128), BF16),
            dma((2,)), dma((2,)),
            dma, dma((2, Y + 2)), dma, dma((Y,)), dma((2,)),
            dma, dma((2, Y + 2)), dma, dma((Y,)), dma((2,)),
            dma, dma((2 * X,)), dma, dma((2 * X,)),
            dma((2,)), dma((2,)), dma, dma, dma, dma,
            dma((2,)), dma((2,)),
        ],
        compiler_params=pltpu.CompilerParams(
            collective_id=0, has_side_effects=True, vmem_limit_bytes=32 * 1024 * 1024
        ),
        cost_estimate=pl.CostEstimate(flops=2 * 2 * 512 * 1024 * 256, bytes_accessed=6 * 1024 * 1024, transcendentals=0),
    )(*operands)


def solution(mesh):
    spec = P("row", "col")
    return jax.shard_map(
        per_device, mesh=mesh, in_specs=(spec,) * 7, out_specs=spec, check_vma=False
    )
```

```python
import jax
import jax.numpy as jnp
from jax import lax
from jax.experimental import pallas as pl
from jax.experimental.pallas import tpu as pltpu
from jax.sharding import PartitionSpec as P

MESH = pl.DeviceIdType.MESH
Z, Y, J = 4, 8, 4
X = 4
BF16, F32 = jnp.bfloat16, jnp.float32
FAR = BF16


def masked(block, mask_ref):
    lane = lax.broadcasted_iota(jnp.int32, block.shape, 1)
    keep = jnp.where(lane < block.shape[1] // 2, mask_ref[0, 0], mask_ref[0, 1])
    return (block.astype(F32) * keep.astype(F32)).astype(BF16)


def kernel(
    f_hbm, p_hbm, s_hbm, fm_hbm, pm_hbm, sm_hbm, filt_hbm, out_ref,
    f_ref, p_ref, s_ref, fm_ref, pm_ref, sm_ref, filt_ref, in_sem,
    f_send, f_all, k_all, p_all, s_all, filt_send, filt_here,
    part, near_in, far_send, far_in, total, part_send, part2_in, block_send, block_in, tile_send, tile_in,
    t_send_sem, t_recv_sem,
    p_send_sem, p_recv_sem, p_over_sem, p_core_sem, p_mate_sem,
    s_send_sem, s_recv_sem, s_over_sem, s_core_sem, s_mate_sem,
    f_send_sem, f_recv_sem, k_send_sem, k_recv_sem,
    a_send_sem, a_recv_sem, b_send_sem, b_recv_sem, o_send_sem, o_recv_sem, x_send_sem, x_recv_sem,
):
    r, c = lax.axis_index("row"), lax.axis_index("col")
    zh, y = lax.div(r, Y), lax.rem(r, Y)
    zl, x, core = lax.div(c, 2 * X), lax.rem(lax.div(c, 2), X), lax.rem(c, 2)
    over = (r, c + 1 - 2 * core)
    low = lax.rem(zh, 2)
    pair = zh + 1 - 2 * low
    mate = Z - 1 - zh
    half = lax.rem(lax.div(zh, 2) + low, 2)
    x_high = lax.div(x, 2)
    home = lax.rem(zl + x_high, 2) == half
    away = lax.rem(zl + x_high, 2) != half
    home_row = jnp.where(home, r, pair * Y + y)
    ahead = jnp.where(core == 0, 1, X - 1)

    def holder(l, k):
        return lax.rem(zl + l, 2) * (2 * X) + x * 2 + k

    def slot_of(z_low, at):
        return X * lax.rem(z_low + lax.div(at, 2) + half, 2) + at

    held_z = 2 * lax.div(zh, 2) + core
    held_zl = lax.rem(x_high + half, 2)
    held_l = lax.rem(zl + held_zl, 2)
    held_from = (held_z * Y + y, held_zl * (2 * X) + x * 2 + held_l)
    term_col = held_zl * (2 * X) + x * 2 + core
    move_to = (home_row, holder(core, low))
    stays = jnp.logical_and(home, jnp.logical_and(core == 0, low == 0))
    moved = jnp.logical_not(stays)
    mine = low == core

    def ring(d):
        return zh * Y + lax.rem(y + d, Y)

    def on_line(dz, dx):
        return lax.rem(zl + dz, 2) * (2 * X) + lax.rem(x + dx, X) * 2 + core

    def copy(src, dst, send, recv, to):
        return pltpu.make_async_remote_copy(
            src_ref=src, dst_ref=dst, send_sem=send, recv_sem=recv, device_id=to, device_id_type=MESH
        )

    def await_sent(ref, sem):
        copy(ref, ref, sem, sem, over).wait_send()

    def await_recv(ref, sem):
        copy(ref, ref, sem, sem, over).wait_recv()

    fetches = []
    for n, (src, dst) in enumerate((
        (f_hbm, f_ref), (fm_hbm, fm_ref), (p_hbm, p_ref), (pm_hbm, pm_ref),
        (filt_hbm, filt_ref), (s_hbm, s_ref), (sm_hbm, sm_ref),
    )):
        fetches.append(pltpu.make_async_copy(src, dst, in_sem.at[n]))
        fetches[-1].start()

    barrier = pltpu.get_barrier_semaphore()

    def greet(to):
        pl.semaphore_signal(barrier, inc=1, device_id=to, device_id_type=MESH)

    @pl.when(moved)
    def _():
        greet(held_from)

    greet((mate * Y + y, c))
    for d in (1, 7):
        greet((ring(d), c))
    for dz, dx in ((1, 0), (0, 1), (0, X - 1)):
        greet((r, on_line(dz, dx)))
    greet(over)
    greet((pair * Y + y, term_col))

    @pl.when(away)
    def _():
        greet((r, term_col))

    for one in fetches[:5]:
        one.wait()
    f_send[...] = masked(f_ref[...], fm_ref)
    p_all[core, y, low] = masked(p_ref[...], pm_ref)
    lane = lax.broadcasted_iota(jnp.int32, filt_send.shape, 1)
    filt_send[...] = jnp.where(lane < 128, filt_ref[0, 0], filt_ref[0, 1]).astype(F32)

    pl.semaphore_wait(barrier, jnp.where(moved, 1, 0) + 1 + 2 + 3 + 1 + 1 + jnp.where(away, 1, 0))

    my_slot = slot_of(zl, x)
    f_move = copy(f_send, f_all.at[X * core + x], t_send_sem.at[0], t_recv_sem.at[0], move_to)
    filt_move = copy(filt_send, filt_here, t_send_sem.at[1], t_recv_sem.at[1], move_to)

    @pl.when(moved)
    def _():
        f_move.start()
        filt_move.start()

    def mate_copy(buf, sem, t):
        ref = buf.at[core, y, t]
        return copy(ref, ref, sem.at[0], sem.at[1], (mate * Y + y, c))

    def ring_ref(buf, sems, src, t, part_of):
        slot = lax.rem(y + src, Y)
        at = Y + part_of if part_of is not None else slot
        if t is None:
            ref = buf.at[core, slot] if part_of is None else buf.at[core, slot, part_of]
            return ref, sems[1].at[0, at]
        ref = buf.at[core, slot, t] if part_of is None else buf.at[core, slot, t, pl.ds(64 * part_of, 64)]
        return ref, sems[1].at[t, at]

    def ring_send(buf, sems, src, t, d, part_of=None):
        ref, recv = ring_ref(buf, sems, src, t, part_of)
        copy(ref, ref, sems[0], recv, (ring(d), c)).start()

    def ring_wait(buf, sems, src, t, part_of=None):
        await_recv(*ring_ref(buf, sems, src, t, part_of))

    def ring_start(buf, sems, t):
        for d in (1, 7):
            ring_send(buf, sems, 0, t, d)

    def ring_pass(buf, sems, t):
        for src, on in ((7, 1), (1, 7)):
            ring_wait(buf, sems, src, t)
            ring_send(buf, sems, src, t, on)

    def ring_relay(buf, sems, t):
        for src, on, far, part_of in ((6, 1, 2, 0), (2, 7, 6, 1)):
            ring_wait(buf, sems, src, t)
            ring_send(buf, sems, src, t, on)
            ring_send(buf, sems, src, t, far, part_of)

    def cross(buf, sems, src):
        at = lax.rem(y + src, Y)
        ref = buf.at[core, at]
        copy(ref, ref, sems[2], sems[3].at[at], over).start()

    def cross_wait(buf, sems, src):
        at = lax.rem(y + src, Y)
        await_recv(buf.at[1 - core, at], sems[3].at[at])

    def ring_last(buf, sems, ts, src):
        for t in ts:
            for part_of in range(2) if src == 4 else (None,):
                ring_wait(buf, sems, src, t, part_of)
        cross(buf, sems, src)

    p_sems = (p_send_sem, p_recv_sem, p_over_sem, p_core_sem)
    s_sems = (s_send_sem, s_recv_sem, s_over_sem, s_core_sem)
    mate_copy(p_all, p_mate_sem, low).start()
    ring_start(p_all, p_sems, low)

    def line_send(buf, sems, dz, dx, to):
        slot = slot_of(lax.rem(zl + dz, 2), lax.rem(x + dx, X))
        ref = buf.at[slot]
        copy(ref, ref, sems[0], sems[1].at[slot], (r, to)).start()

    def line_wait(buf, sems, dz, dx):
        slot = slot_of(lax.rem(zl + dz, 2), lax.rem(x + dx, X))
        await_recv(buf.at[slot], sems[1].at[slot])

    def line_start(buf, sems):
        for to in (on_line(1, 0), on_line(0, ahead), on_line(0, X - ahead)):
            line_send(buf, sems, 0, 0, to)

    def line_relay(buf, sems):
        line_wait(buf, sems, 1, 0)
        line_send(buf, sems, 1, 0, on_line(0, 1))
        line_send(buf, sems, 1, 0, on_line(0, X - 1))
        line_wait(buf, sems, 0, X - ahead)
        line_send(buf, sems, 0, X - ahead, on_line(0, ahead))
        line_send(buf, sems, 0, X - ahead, on_line(1, ahead))

    def line_finish(buf, sems):
        for dz, dx in ((0, ahead), (1, 1), (1, X - 1), (0, 2), (1, 2)):
            line_wait(buf, sems, dz, dx)

    f_sems, k_sems = (f_send_sem, f_recv_sem), (k_send_sem, k_recv_sem)
    ring_pass(p_all, p_sems, low)
    mate_copy(p_all, p_mate_sem, 1 - low).wait_recv()
    ring_start(p_all, p_sems, 1 - low)

    @pl.when(moved)
    def _():
        await_recv(f_all.at[my_slot], t_recv_sem.at[0])

    @pl.when(stays)
    def _():
        f_all[my_slot] = f_send[...]

    line_start(f_all, f_sems)
    cross(p_all, p_sems, 0)

    for one in fetches[5:]:
        one.wait()
    s_all[core, y, low] = masked(s_ref[...], sm_ref)
    mate_copy(s_all, s_mate_sem, low).start()

    ring_relay(p_all, p_sems, low)
    line_relay(f_all, f_sems)
    ring_pass(p_all, p_sems, 1 - low)
    cross(p_all, p_sems, 1)
    cross(p_all, p_sems, 7)
    ring_relay(p_all, p_sems, 1 - low)
    cross(p_all, p_sems, 2)
    cross(p_all, p_sems, 6)
    mate_copy(s_all, s_mate_sem, 1 - low).wait_recv()
    ring_start(s_all, s_sems, None)
    line_finish(f_all, f_sems)

    def at_place(b, src):
        place = lax.rem(y + src, Y)
        j = lax.div(place, 2)
        lanes = pl.ds(pl.multiple_of(128 * lax.rem(place, 2), 128), 128)
        total = None
        for t in range(2):
            rows = f_all[X * lax.rem(j, 2) + 2 * t + lax.div(j, 2), :, lanes]
            term = jnp.dot(rows, p_all[b, place, t], preferred_element_type=F32)
            total = term if total is None else total + term
        return total

    def near_copy():
        return copy(part, near_in, a_send_sem.at[0], a_recv_sem.at[0], (r, holder(1, core)))

    def send_first(b, term):
        @pl.when(away)
        def _():
            far_send[b] = term.astype(FAR)
            copy(
                far_send.at[b], far_in, a_send_sem.at[1], a_recv_sem.at[1], (pair * Y + y, holder(b, core))
            ).start()

        @pl.when(jnp.logical_and(home, b == 0))
        def _():
            near_in[...] = term

        @pl.when(jnp.logical_and(home, b == 1))
        def _():
            part[...] = term
            near_copy().start()

    term = at_place(core, 0)
    for src in (1, 7, 2, 6):
        term = term + at_place(core, src)
    for src in (5, 3, 4):
        ring_last(p_all, p_sems, (low, 1 - low), src)
        term = term + at_place(core, src)
    send_first(core, term)
    ring_pass(s_all, s_sems, None)

    term = None
    for src in (0, 1, 7, 2, 6, 5, 3, 4):
        cross_wait(p_all, p_sems, src)
        one = at_place(1 - core, src)
        term = one if term is None else term + one
    send_first(1 - core, term)

    @pl.when(moved)
    def _():
        filt_move.wait_recv()

    @pl.when(stays)
    def _():
        filt_here[...] = filt_send[...]

    ring_relay(s_all, s_sems, None)
    for src in (0, 1, 7, 2, 6):
        cross(s_all, s_sems, src)

    @pl.when(away)
    def _():
        await_recv(near_in, a_recv_sem.at[0])

    await_recv(far_in, a_recv_sem.at[1])
    k_all[my_slot] = ((near_in[...] + far_in[...].astype(F32)) * filt_here[0:1, :]).astype(BF16)
    line_start(k_all, k_sems)
    line_relay(k_all, k_sems)
    for src in (5, 3, 4):
        ring_last(s_all, s_sems, (None,), src)
    for src in range(Y):
        cross_wait(s_all, s_sems, src)

    def by_block(dz, dx):
        at = lax.rem(x + dx, X)
        slot = slot_of(lax.rem(zl + dz, 2), at)
        t, j = lax.div(at, 2), 2 * lax.rem(at, 2) + lax.div(slot, X)
        rows = k_all[slot]
        for b in range(2):
            depth = jnp.concatenate([s_all[b, 2 * j, t], s_all[b, 2 * j + 1, t]], axis=0)
            total[b] += jnp.dot(rows, depth, preferred_element_type=F32)

    total[...] = jnp.zeros_like(total)
    for dz, dx in ((0, 0), (1, 0), (0, X - ahead)):
        by_block(dz, dx)
    for dz, dx in ((0, ahead), (1, 1), (1, X - 1), (0, 2), (1, 2)):
        line_wait(k_all, k_sems, dz, dx)
        by_block(dz, dx)

    kept_b = jnp.where(mine, 0, 1)
    part_send[...] = total[1 - kept_b].astype(BF16)
    part_copy = copy(part_send, part2_in, b_send_sem, b_recv_sem, (pair * Y + y, c))
    part_copy.start()

    @pl.when(moved)
    def _():
        f_move.wait_send()
        filt_move.wait_send()

    mate_copy(p_all, p_mate_sem, low).wait_send()
    mate_copy(s_all, s_mate_sem, low).wait_send()
    await_sent(p_all.at[0, pl.ds(0, Y - 1)], p_send_sem)
    await_sent(s_all.at[0, pl.ds(0, Y - 1)], s_send_sem)
    await_sent(p_all.at[0], p_over_sem)
    await_sent(s_all.at[0], s_over_sem)
    await_sent(f_all.at[pl.ds(0, 2 * X - 1)], f_send_sem)
    await_sent(k_all.at[pl.ds(0, 2 * X - 1)], k_send_sem)

    @pl.when(away)
    def _():
        await_sent(far_send, a_send_sem.at[1])

    @pl.when(home)
    def _():
        near_copy().wait_send()

    block_row = jnp.where(mine, r, pair * Y + y)
    block_col = c - core + kept_b
    own_here = jnp.logical_and(low == 0, core == 0)
    own_comes = jnp.logical_not(own_here)
    own_sent = jnp.logical_not(jnp.logical_and(mine, core == 0))
    block_copy = copy(block_send, block_in, o_send_sem, o_recv_sem, (block_row, block_col))

    def tile_stays(h):
        return jnp.logical_and(2 * block_col + h == r, lax.div(block_row, 2) == c)

    def tile_copy(h):
        at = lax.rem(block_row, 2)
        return copy(
            tile_send.at[h], tile_in.at[at], x_send_sem.at[h], x_recv_sem.at[at], (2 * block_col + h, lax.div(block_row, 2))
        )

    def tile_is_here(b):
        row, col = 2 * c + b, lax.div(r, 2)
        z = lax.div(row, Y)
        z_low, second = lax.rem(z, 2), lax.rem(col, 2)
        z_at = z + second * (1 - 2 * z_low)
        return jnp.logical_and(z_at * Y + lax.rem(row, Y) == r, col - second + z_low == c)

    part_copy.wait_recv()
    rounded = (total[kept_b] + part2_in[...].astype(F32)).astype(BF16)
    for h in range(2):
        tile_send[h] = rounded[:, 128 * h : 128 * (h + 1)]

        @pl.when(jnp.logical_not(tile_stays(h)))
        def _():
            tile_copy(h).start()

        @pl.when(tile_stays(h))
        def _():
            tile_in[lax.rem(block_row, 2)] = tile_send[h]

    block_send[...] = rounded

    @pl.when(own_sent)
    def _():
        block_copy.start()

    @pl.when(own_here)
    def _():
        block_in[...] = rounded

    part_copy.wait_send()

    @pl.when(own_comes)
    def _():
        await_recv(block_in, o_recv_sem)

    for b in range(2):
        here = slice(128 * b, 128 * (b + 1))

        @pl.when(jnp.logical_not(tile_is_here(b)))
        def _():
            await_recv(tile_in.at[b], x_recv_sem.at[b])

        out_ref[:, here] = block_in[:, here].astype(F32) - tile_in[b].astype(F32).T

    @pl.when(own_sent)
    def _():
        block_copy.wait_send()

    for h in range(2):

        @pl.when(jnp.logical_not(tile_stays(h)))
        def _():
            tile_copy(h).wait_send()


def per_device(fock, density, intersection, fock_mask, density_mask, intersection_mask, product_filter):
    operands = fock, density, intersection, fock_mask, density_mask, intersection_mask, product_filter
    operands = [pltpu.with_memory_space_constraint(one, pltpu.HBM) for one in operands]
    hbm = pl.BlockSpec(memory_space=pltpu.HBM)
    vmem = pl.BlockSpec(memory_space=pltpu.VMEM)
    dma = pltpu.SemaphoreType.DMA
    block = (128, 256)
    return pl.pallas_call(
        kernel,
        out_shape=jax.ShapeDtypeStruct(block, F32),
        in_specs=[hbm] * 7,
        out_specs=vmem,
        scratch_shapes=[pltpu.VMEM(block, BF16)] * 3
        + [pltpu.SMEM((1, 2), jnp.int32)] * 4
        + [
            dma((7,)),
            pltpu.VMEM(block, BF16),
            pltpu.VMEM((2 * X,) + block, BF16),
            pltpu.VMEM((2 * X,) + block, BF16),
            pltpu.VMEM((2, Y, 2) + block, BF16),
            pltpu.VMEM((2, Y, 2) + block, BF16),
            pltpu.VMEM((8, 256), F32),
            pltpu.VMEM((8, 256), F32),
            pltpu.VMEM(block, F32),
            pltpu.VMEM(block, F32),
            pltpu.VMEM((2,) + block, FAR),
            pltpu.VMEM(block, FAR),
            pltpu.VMEM((2,) + block, F32),
            pltpu.VMEM(block, BF16),
            pltpu.VMEM(block, BF16),
            pltpu.VMEM(block, BF16),
            pltpu.VMEM(block, BF16),
            pltpu.VMEM((2, 128, 128), BF16),
            pltpu.VMEM((2, 128, 128), BF16),
            dma((2,)), dma((2,)),
            dma, dma((2, Y + 2)), dma, dma((Y,)), dma((2,)),
            dma, dma((2, Y + 2)), dma, dma((Y,)), dma((2,)),
            dma, dma((2 * X,)), dma, dma((2 * X,)),
            dma((2,)), dma((2,)), dma, dma, dma, dma,
            dma((2,)), dma((2,)),
        ],
        compiler_params=pltpu.CompilerParams(
            collective_id=0, has_side_effects=True, vmem_limit_bytes=32 * 1024 * 1024
        ),
        cost_estimate=pl.CostEstimate(flops=2 * 2 * 512 * 1024 * 256, bytes_accessed=6 * 1024 * 1024, transcendentals=0),
    )(*operands)


def solution(mesh):
    spec = P("row", "col")
    return jax.shard_map(
        per_device, mesh=mesh, in_specs=(spec,) * 7, out_specs=spec, check_vma=False
    )
```
